256 devices in a mesh: ctx: 32 (over x_hi, z, core), enc: 4 (over y), mp: 2 (over x_lo).
Axes of the slice: x: 4 (x_hi: 2, x_lo: 2; x = x_hi * 2 + x_lo), y: 4, z: 8, core: 2. Of those that a mesh axis runs over, the one named last changes fastest.
Arguments:
- hidden_in: bfloat16 [8192, 4096], P('ctx'), may hold values from -6 to 6
- norm_gains: float32 [2, 4096], replicated, may hold values from 0.5 to 1.5
- w_cross_query: bfloat16 [4096, 2048], P('ctx', ('enc', 'mp')), may hold values from -1 to 1
- w_cross_out: bfloat16 [2048, 4096], P(('enc', 'mp'), 'ctx'), may hold values from -0.125 to 0.125
- w_self_qkv: bfloat16 [4096, 3, 2048], P('ctx', None, ('enc', 'mp')), may hold values from -1 to 1
- w_self_out: bfloat16 [2048, 4096], P(('enc', 'mp'), 'ctx'), may hold values from -0.125 to 0.125
- nbr_kv: bfloat16 [32, 4, 4, 3, 64, 1024], P('ctx', 'enc', None, None, None, 'mp'), may hold values from -6 to 6
- nbr_count: int32 [128], P('ctx'), may hold values from 1 to 2
- nbr_source: int32 [128, 2], P('ctx'), may hold values from 0 to 3, all different within a row; in each aligned block of 4 rows (0 to 3, 4 to 7, ...) at most 3 rows name the same one
- span_order: int32 [128], replicated, may hold values from 0 to 127, each once
Outputs:
- block_out: bfloat16 [8192, 4096], P('ctx', ('enc', 'mp'))
The draws below stay inside these ranges and needn't reach their ends.
Inputs may be any that keep to these rules, and one draw needn't show every extreme that they name: `nbr_source`: within the 4 stored spans of one index of ctx (aligned blocks of rows), no encoder index is named more than 3 times, and one is named exactly 3 times in some block; the 2 entries of a span differ. `span_order`: each of the 128 positions appears once.
All inputs are finite; a program needn't handle non-finite values.
Results may differ from the reference program's by a relative error of at most 0.015.
Values may be sent and summed in bfloat16 or wider, within the bound.
No kernel may reach another device: no remote copies, remote signals or barrier semaphores. Data moves between devices by JAX's collectives and lax.ppermute only.
A program may use at most 128 MiB of HBM per device.

```python
import math
import jax
import jax.numpy as jnp
import numpy as np
from jax import lax

D = 4096
HEADS = 16
HD = 128
SPAN = 64
NBR = 2
NBR_ROWS = 64
CH_DEV = 4
CAP = 3
SPANS = 128
SEQ = 8192
N_CTX = 32
N_ENC = 4
N_MP = 2


def draw_hidden_in(key, part):
    own_key = jax.random.fold_in(key, 11)
    values = jax.random.truncated_normal(own_key, -6.0, 6.0, (SEQ, D), jnp.float32)
    return values.astype(jnp.bfloat16)


def draw_w_cross_query(key, part):
    own_key = jax.random.fold_in(key, 12)
    values = jax.random.truncated_normal(own_key, -6.0, 6.0, (D, HEADS * HD), jnp.float32) / math.sqrt(D)
    return values.astype(jnp.bfloat16)


def draw_w_self_qkv(key, part):
    own_key = jax.random.fold_in(key, 13)
    values = jax.random.truncated_normal(own_key, -6.0, 6.0, (D, 3, HEADS * HD), jnp.float32) / math.sqrt(D)
    return values.astype(jnp.bfloat16)


def draw_nbr_kv(key, part):
    own_key = jax.random.fold_in(key, 14)
    per_group = HEADS // N_ENC
    values = jax.random.truncated_normal(own_key, -6.0, 6.0, (N_CTX, N_ENC, N_ENC, CAP, NBR_ROWS, per_group, 2, HD), jnp.float32)
    values = values.reshape(N_CTX, N_ENC, N_ENC, CAP, NBR_ROWS, per_group * 2 * HD)
    return values.astype(jnp.bfloat16)


def set_ends(entries, rng, least, high):
    shape = entries.shape
    place = [jax.random.randint(jax.random.fold_in(rng, axis), (), 0, shape[axis]) for axis in range(len(shape))]
    entries = entries.at[tuple(place)].set(least)
    longest = shape.index(max(shape))
    place[longest] = (place[longest] + 1) % shape[longest]
    return entries.at[tuple(place)].set(high)


def levels(key, shape, cuts, least, largest):
    def one(position, blocks):
        steps = jax.random.uniform(jax.random.fold_in(jax.random.fold_in(key, 6), position), (blocks,), jnp.float32, least / len(cuts), largest / len(cuts))
        return jnp.repeat(jnp.exp(steps), shape[position] // blocks).reshape((-1,) + (1,) * (len(shape) - position - 1))

    level = one(*cuts[0])
    for cut in cuts[1:]:
        level = level * one(*cut)
    return level


def assign_block(rng, own, number, rows, amount, top, reach, lean):
    sequence = jax.random.permutation(rng, amount)
    heavy_load, usual = portions_of(amount, rows * top, reach, lean, True), portions_of(amount, rows * top, reach, lean, False)
    places = jnp.arange(amount)

    def named(tallies, rotation):
        used = int((tallies > 0).sum())
        fixed = max(1, used // 4)
        shifted = fixed + (places - fixed + rotation * (used - fixed)) % max(1, amount - fixed)
        return jnp.zeros((amount,), jnp.int32).at[sequence[jnp.where(places < fixed, places, shifted)]].set(jnp.asarray(tallies, jnp.int32))

    tallies = jnp.where(number % 4 == 0, named(heavy_load, number // 4), named(usual, number - number // 4 - 1))
    mixed = jax.random.permutation(jax.random.fold_in(own, 3), amount)
    source_of, sink = mixed[0:amount // 2 * 2:2], mixed[1:amount // 2 * 2:2]
    margin = jnp.minimum(tallies[source_of] - 1, reach - tallies[sink]) // 2
    margin = jnp.where((source_of == sequence[0]) | (sink == sequence[0]) | (tallies[sink] == 0), 0, jnp.maximum(margin, 0))
    shifted = jax.random.randint(jax.random.fold_in(own, 4), (amount // 2,), 0, 1 << 20) % (margin + 1)
    tallies = tallies.at[source_of].add(-shifted).at[sink].add(shifted)
    items = jnp.searchsorted(jnp.cumsum(tallies), jnp.arange(rows * top), side="right").astype(jnp.int32)
    table = items.reshape(top, rows).T
    table = table[jax.random.permutation(jax.random.fold_in(own, 1), rows)]
    rotation = jax.random.randint(jax.random.fold_in(own, 2), (rows, 1), 0, top)
    return jnp.take_along_axis(table, (jnp.arange(top)[None, :] + rotation) % top, axis=1)


def portions_of(amount, total, most, skew, full):
    loads = [(1 << 20) // math.isqrt(standing ** skew) + 1 for standing in range(1, amount + 1)]
    largest = most if full else min(most, max(-(-total // amount), total * loads[0] // sum(loads)))
    least = 1 if total - largest >= amount - 1 else 0
    holding, surplus = [largest] + [least] * (amount - 1), total - largest - least * (amount - 1)
    while surplus > 0:
        movable = [i for i in range(1, amount) if holding[i] < largest] or [i for i in range(1, amount) if holding[i] < most]
        pool, budget = sum([loads[i] for i in movable]), surplus
        for i in movable:
            extra = min(most - holding[i], max(1, budget * loads[i] // pool), surplus)
            holding[i] = holding[i] + extra
            surplus = surplus - extra
    return np.array(holding)


def noise(key, shape, spread, reach, pieces=(), kind=jnp.bfloat16):
    drawn = spread * jax.random.normal(key, shape, jnp.float32)
    if pieces:
        drawn = drawn * levels(key, shape, pieces, -0.22, 0.18)
    return jnp.clip(drawn, -reach, reach).astype(kind)


def setup_inputs(seed: int = 0) -> dict:
    streams_of = jax.random.split(jax.random.key(seed), 11)
    hidden_in = draw_hidden_in(jax.random.fold_in(streams_of[10], 71), 0)
    norm_gains = jnp.clip(1.0 + 0.1 * jax.random.normal(streams_of[1], (2, D), jnp.float32), 0.5, 1.5)
    w_cross_query = draw_w_cross_query(jax.random.fold_in(streams_of[10], 71), 0)
    w_cross_out = noise(streams_of[3], (HEADS * HD, D), (HEADS * HD) ** -0.5, 0.125, ((0, 8), (1, 32)))
    w_self_qkv = draw_w_self_qkv(jax.random.fold_in(streams_of[10], 71), 0)
    w_self_out = noise(streams_of[5], (HEADS * HD, D), (HEADS * HD) ** -0.5, 0.125, ((0, 8), (1, 32)))
    nbr_kv = draw_nbr_kv(jax.random.fold_in(streams_of[10], 71), 0)
    nbr_count = set_ends(jax.random.randint(streams_of[7], (SPANS,), 1, NBR + 1), jax.random.fold_in(streams_of[7], 1), 1, NBR).astype(jnp.int32)
    nbr_source_keys = jax.random.split(jax.random.fold_in(streams_of[8], 1), SPANS // CH_DEV)
    nbr_source_turns = jax.random.permutation(jax.random.fold_in(streams_of[8], 3), SPANS // CH_DEV)
    nbr_source = jax.vmap(lambda own, number: assign_block(jax.random.fold_in(streams_of[8], 2), own, number, CH_DEV, N_ENC, NBR, CAP, 2))(nbr_source_keys, nbr_source_turns).reshape((SPANS, NBR))
    span_order = jax.random.permutation(streams_of[9], SPANS).astype(jnp.int32)
    return {"hidden_in": hidden_in, "norm_gains": norm_gains, "w_cross_query": w_cross_query, "w_cross_out": w_cross_out, "w_self_qkv": w_self_qkv, "w_self_out": w_self_out, "nbr_kv": nbr_kv, "nbr_count": nbr_count, "nbr_source": nbr_source, "span_order": span_order}


epsilon = 1e-05
far_below = -1e+30

def rms_rows(row_values, gain_row):
    values = row_values.astype(jnp.float32)
    row_scale = lax.rsqrt(lax.optimization_barrier(jnp.mean(values * values, axis=-1, keepdims=True)) + epsilon)
    return (values * row_scale * gain_row).astype(jnp.bfloat16)

def group_sum(left_side, right_side):
    groups = N_ENC * N_MP
    group_width = left_side.shape[1] // groups
    left_groups = left_side.reshape(left_side.shape[0], groups, group_width).transpose(1, 0, 2)
    right_groups = right_side.reshape(groups, group_width, right_side.shape[1])

    def add_group(running, pair):
        term_value = jnp.dot(pair[0], pair[1], preferred_element_type=jnp.float32).astype(jnp.bfloat16)
        term_value = lax.optimization_barrier(term_value)
        return (running + term_value.astype(jnp.float32), None)
    initial = jnp.zeros((left_side.shape[0], right_side.shape[1]), jnp.float32)
    return lax.scan(add_group, initial, (left_groups, right_groups))[0]

def reference(hidden_in, norm_gains, w_cross_query, w_cross_out, w_self_qkv, w_self_out, nbr_kv, nbr_count, nbr_source, span_order):
    features = HEADS * HD
    per_group = HEADS // N_ENC
    attn_scale = 1.0 / math.sqrt(HD)
    normed = rms_rows(hidden_in, norm_gains[0])
    cross_query = jnp.dot(normed, w_cross_query, preferred_element_type=jnp.float32).astype(jnp.bfloat16)
    chosen = nbr_source.reshape(N_CTX, CH_DEV * NBR)
    matches = (chosen[:, :, None] == jnp.arange(N_ENC, dtype=jnp.int32)[None, None, :]).astype(jnp.int32)
    earlier = jnp.cumsum(matches, axis=1) - matches
    slot_ranks = lax.optimization_barrier(jnp.sum(earlier * matches, axis=2)).astype(jnp.int32)
    columns = jnp.broadcast_to(jnp.arange(N_CTX, dtype=jnp.int32)[:, None], chosen.shape)
    picked = nbr_kv[columns.reshape(-1), chosen.reshape(-1), :, slot_ranks.reshape(-1)]
    picked = picked.reshape(SPANS, NBR, N_ENC, NBR_ROWS, per_group, 2, HD)
    picked = picked.transpose(0, 1, 3, 2, 4, 5, 6).reshape(SPANS, NBR, NBR_ROWS, HEADS, 2, HD)
    nbr_keys = picked[:, :, :, :, 0, :].astype(jnp.float32)
    nbr_values = picked[:, :, :, :, 1, :]
    queries = cross_query.reshape(SPANS, SPAN, HEADS, HD).astype(jnp.float32)
    scores = jnp.einsum('cqhd,cjrhd->chqjr', queries, nbr_keys) * attn_scale
    alive_mask = jnp.arange(NBR, dtype=jnp.int32)[None, :] < nbr_count[:, None]
    scores = jnp.where(alive_mask[:, None, None, :, None], scores, far_below)
    row_top = lax.optimization_barrier(jnp.max(scores, axis=(3, 4), keepdims=True))
    weights_f = jnp.exp(scores - row_top)
    row_total = lax.optimization_barrier(jnp.sum(weights_f, axis=(3, 4)))
    weights_b = weights_f.astype(jnp.bfloat16).astype(jnp.float32)
    mixed_heads = jnp.einsum('chqjr,cjrhd->chqd', weights_b, nbr_values.astype(jnp.float32)) / row_total[..., None]
    cross_att = mixed_heads.transpose(0, 2, 1, 3).reshape(SEQ, features).astype(jnp.bfloat16)
    cross_sum = group_sum(cross_att, w_cross_out)
    mid = (hidden_in.astype(jnp.float32) + cross_sum).astype(jnp.bfloat16)
    mid_normed = rms_rows(mid, norm_gains[1])
    projected = jnp.dot(mid_normed, w_self_qkv.reshape(D, 3 * features), preferred_element_type=jnp.float32)
    projected = projected.astype(jnp.bfloat16).reshape(SEQ, 3, HEADS, HD)
    rows_all = jnp.arange(SEQ, dtype=jnp.int32)
    positions = span_order[rows_all // SPAN].astype(jnp.int32) * SPAN + rows_all % SPAN
    visible = positions[None, :] <= positions[:, None]

    def head_attention(triple):
        head_q, head_k, head_v = triple
        head_scores = jnp.dot(head_q, head_k.T, preferred_element_type=jnp.float32) * attn_scale
        head_scores = jnp.where(visible, head_scores, far_below)
        head_top = lax.optimization_barrier(jnp.max(head_scores, axis=1, keepdims=True))
        head_weights = jnp.where(visible, jnp.exp(head_scores - head_top), 0.0)
        head_total = lax.optimization_barrier(jnp.sum(head_weights, axis=1, keepdims=True))
        head_out = jnp.dot(head_weights.astype(jnp.bfloat16), head_v, preferred_element_type=jnp.float32)
        return head_out / head_total
    per_head = projected.transpose(1, 2, 0, 3)
    self_heads = lax.map(head_attention, (per_head[0], per_head[1], per_head[2]))
    self_att = self_heads.transpose(1, 0, 2).reshape(SEQ, features).astype(jnp.bfloat16)
    self_sum = group_sum(self_att, w_self_out)
    return (mid.astype(jnp.float32) + self_sum).astype(jnp.bfloat16)
```

```python
import functools
import math

import jax
import jax.numpy as jnp
from jax import lax
from jax.experimental import pallas as pl
from jax.experimental.pallas import tpu as pltpu
from jax.sharding import Mesh
from jax.sharding import PartitionSpec as P

HD = 128
SPAN = 64
epsilon = 1e-05
far_below = -1e30
NZ = 8

VMEM = pl.BlockSpec(memory_space=pltpu.VMEM)
SMEM = pl.BlockSpec(memory_space=pltpu.SMEM)
f32 = jnp.float32
bf16 = jnp.bfloat16

CTX = ("xh", "z", "core")
GROUP = ("y", "xl")
ALL = CTX + GROUP


def dot(a, b):
    return jnp.dot(a, b, preferred_element_type=f32)


def dot_t(a, b):
    return lax.dot_general(a, b, (((1,), (1,)), ((), ())), preferred_element_type=f32)


def call(kernel, out_shape, in_specs, scratch, flops, nbytes):
    return pl.pallas_call(
        kernel,
        out_shape=out_shape,
        in_specs=in_specs,
        out_specs=jax.tree.map(lambda _: VMEM, out_shape),
        scratch_shapes=scratch,
        compiler_params=pltpu.CompilerParams(vmem_limit_bytes=48 * 1024 * 1024),
        cost_estimate=pl.CostEstimate(flops=flops, bytes_accessed=nbytes, transcendentals=0),
    )


def ring(x):
    up = [(i, (i + 1) % NZ) for i in range(NZ)]
    down = [(i, (i - 1) % NZ) for i in range(NZ)]
    r1 = lax.ppermute(x, "z", up)
    l1 = lax.ppermute(x, "z", down)
    r2 = lax.ppermute(r1, "z", up)
    l2 = lax.ppermute(l1, "z", down)
    r3 = lax.ppermute(r2, "z", up)
    l3 = lax.ppermute(l2, "z", down)
    r4 = lax.ppermute(r3[:1], "z", up)
    l4 = lax.ppermute(l3[1:], "z", down)
    return [x, l1, l2, l3, r4, l4, r3, r2, r1]


def half(pieces, distance, side):
    if distance < 4:
        return pieces[distance], side
    if distance == 4:
        return pieces[4 + side], 0
    return pieces[distance + 1], side


def swap_cores(x):
    return lax.ppermute(x, "core", [(0, 1), (1, 0)])


def swap_xh(x):
    return lax.ppermute(x, "xh", [(0, 1), (1, 0)])


def cross_kernel(where, source, count, hidden, gain, nbr, *rest):
    pieces = (rest[:9], rest[9:18])
    out, normed = rest[18:]
    xh, z, core = where[0], where[1], where[2]
    values = hidden[...].astype(f32)
    row_scale = lax.rsqrt(jnp.mean(values * values, axis=1, keepdims=True) + epsilon)
    for b in range(32):
        cols = slice(b * 128, (b + 1) * 128)
        block = hidden[:, cols].astype(f32)
        normed[:, cols] = (block * row_scale * gain[b : b + 1, :]).astype(bf16)
    acc = jnp.zeros(out.shape, f32)
    for distance in range(NZ):
        zz = lax.rem(z + distance, NZ)
        for other in range(2):
            left, right = [], []
            for side in range(2):
                owner = (xh ^ side) * 16 + zz * 2 + (core ^ other)
                left.append(normed[:, pl.ds(pl.multiple_of(owner * 128, 128), 128)])
                ref, index = half(pieces[other], distance, side)
                right.append(ref[index])
            acc += dot(jnp.concatenate(left, axis=1), jnp.concatenate(right, axis=0))
    query = acc.astype(bf16)
    scale = 1.0 / math.sqrt(HD)
    lanes = lax.broadcasted_iota(jnp.int32, (SPAN, 128), 1)
    chosen = [source[i] for i in range(8)]
    for s in range(4):
        slots = []
        for j in range(2):
            i = s * 2 + j
            rank = jnp.int32(0)
            for k in range(s * 2):
                rank = rank + (chosen[k] == chosen[i]).astype(jnp.int32)
            slots.append(chosen[i] * 3 + rank)
        alive = lanes < count[s] * 64
        for h in range(2):
            kcols = slice(2 * h * HD, (2 * h + 1) * HD)
            vcols = slice((2 * h + 1) * HD, (2 * h + 2) * HD)
            keys = jnp.concatenate([nbr[slots[0], :, kcols], nbr[slots[1], :, kcols]], axis=0)
            vals = jnp.concatenate([nbr[slots[0], :, vcols], nbr[slots[1], :, vcols]], axis=0)
            part = query[s * SPAN : (s + 1) * SPAN, h * HD : (h + 1) * HD]
            scores = jnp.where(alive, dot_t(part, keys) * scale, far_below)
            top = jnp.max(scores, axis=1, keepdims=True)
            weights = jnp.exp(scores - top)
            total = jnp.sum(weights, axis=1, keepdims=True)
            mixed = dot(weights.astype(bf16), vals) / total
            out[s * SPAN : (s + 1) * SPAN, h * HD : (h + 1) * HD] = mixed.astype(bf16)


def cross_out_kernel(where, att, share, *rest):
    pieces = (rest[:9], rest[9:18])
    out, weights = rest[18:]
    xh, z, core = where[0], where[1], where[2]
    for distance in range(NZ):
        zz = lax.rem(z + distance, NZ)
        for other in range(2):
            for side in range(2):
                first = (core ^ other) * 1024 + (zz * 2 + (xh ^ side)) * 64
                ref, index = half(pieces[other], distance, side)
                weights[pl.ds(pl.multiple_of(first, 64), 64), :] = ref[index]
    acc = share[...].astype(f32)
    for g in range(8):
        acc += dot(att[g], weights[g * 256 : (g + 1) * 256, :])
    out[...] = acc.astype(bf16)


def qkv_kernel(where, mids, gain, own, par, keep, send, normed, proj):
    xh, core = where[0], where[2]
    total = jnp.zeros((mids.shape[1], 1), f32)
    for g in range(8):
        values = mids[g].astype(f32)
        total += jnp.sum(values * values, axis=1, keepdims=True)
    row_scale = lax.rsqrt(total * (1.0 / 4096) + epsilon)
    for b in range(32):
        block = mids[b // 4, :, (b % 4) * 128 : (b % 4 + 1) * 128].astype(f32)
        normed[:, b * 128 : (b + 1) * 128] = (block * row_scale * gain[b : b + 1, :]).astype(bf16)
    for t in range(3):
        acc = jnp.zeros((mids.shape[1], 256), f32)
        for z in range(NZ):
            for other in range(2):
                left, right = [], []
                for side in range(2):
                    owner = (xh ^ side) * 16 + z * 2 + (core ^ other)
                    left.append(normed[:, pl.ds(pl.multiple_of(owner * 128, 128), 128)])
                    right.append((own, par)[other][z, side * 3 + t])
                acc += dot(jnp.concatenate(left, axis=1), jnp.concatenate(right, axis=0))
        if t == 0:
            acc = acc * (math.log2(math.e) / math.sqrt(HD))
        proj[...] = acc.astype(bf16)
        keep[t] = proj[:, pl.ds(pl.multiple_of(xh * 128, 128), 128)]
        send[t] = proj[:, pl.ds(pl.multiple_of((1 - xh) * 128, 128), 128)]


def attention_kernel(where, order, query, *rest):
    pieces = (rest[:9], rest[9:18])
    (out,) = rest[18:]
    xh, z, core = where[0], where[1], where[2]
    rows = lax.broadcasted_iota(jnp.int32, (SPAN, 1), 0)
    lanes = lax.broadcasted_iota(jnp.int32, (1, 256), 1)
    span_of, within = lanes // SPAN, lanes % SPAN
    q_places = []
    for side in range(2):
        c = (xh ^ side) * 16 + z * 2 + core
        for s in range(4):
            q_places.append(order[c * 4 + s] * SPAN + rows)
    q_places = jnp.concatenate(q_places, axis=0)
    top = jnp.full((512, 1), far_below, f32)
    total = jnp.zeros((512, 1), f32)
    mixed = jnp.zeros((512, HD), f32)
    for distance in range(NZ):
        zz = lax.rem(z + distance, NZ)
        for other in range(2):
            places = []
            for side in range(2):
                c = (xh ^ side) * 16 + zz * 2 + (core ^ other)
                place = jnp.zeros((1, 256), jnp.int32)
                for s in range(4):
                    place = jnp.where(span_of == s, order[c * 4 + s], place)
                places.append(place * SPAN + within)
            k_places = jnp.concatenate(places, axis=1)
            key_ref, key_index = half(pieces[other], distance, 0)
            val_ref, val_index = half(pieces[other], distance, 1)
            scores = dot_t(query[...], key_ref[key_index])
            visible = k_places <= q_places
            scores = jnp.where(visible, scores, far_below)
            new_top = jnp.maximum(top, jnp.max(scores, axis=1, keepdims=True))
            weights = jnp.where(visible, jnp.exp2(scores - new_top), 0.0)
            fade = jnp.exp2(top - new_top)
            total = total * fade + jnp.sum(weights, axis=1, keepdims=True)
            mixed = mixed * fade + dot(weights.astype(bf16), val_ref[val_index])
            top = new_top
    result = (mixed / total).astype(bf16)
    out[xh] = result[:256]
    out[1 - xh] = result[256:]


def self_out_kernel(where, att, share, own, par, out, weights):
    xh, core = where[0], where[2]
    for z in range(NZ):
        for other in range(2):
            for side in range(2):
                first = (core ^ other) * 1024 + (z * 2 + (xh ^ side)) * 64
                block = (own, par)[other][z, 6 + side]
                rows = pl.ds(pl.multiple_of(first, 64), 64)
                weights[rows, :256] = block[:64]
                weights[rows, 256:] = block[64:]
    acc = share[...].astype(f32)
    for g in range(8):
        both = jnp.concatenate([att[0, g], att[1, g]], axis=1)
        acc += dot(both, weights[g * 256 : (g + 1) * 256, :])
    out[...] = acc.astype(bf16)


def deal_out_weights(blocks, c):
    n = blocks.shape[0]
    quarters = blocks.reshape(n, 4, 64, 128)
    turn = c % 4
    arrived = []
    for i in range(4):
        pairs = []
        for source_c in range(32):
            for source_g in range(8):
                r = source_g * 4 + (i + source_c) % 4
                target_c = (r % 2) * 16 + ((r % 16) // 2) * 2 + r // 16
                pairs.append((source_c * 8 + source_g, target_c * 8 + source_c // 4))
        piece = lax.dynamic_index_in_dim(quarters, (i + turn) % 4, 1, keepdims=False)
        arrived.append(lax.ppermute(piece, ALL, pairs))
    r = (c % 2) * 16 + ((c // 2) % 8) * 2 + c // 16
    stacked = jnp.stack(arrived)
    columns = [lax.dynamic_index_in_dim(stacked, (r - q) % 4, 0, keepdims=False) for q in range(4)]
    return jnp.concatenate(columns, axis=2)


def per_device(
    hidden_in,
    norm_gains,
    w_cross_query,
    w_cross_out,
    w_self_qkv,
    w_self_out,
    nbr_kv,
    nbr_count,
    nbr_source,
    span_order,
):
    rows, width = hidden_in.shape
    xh, z, core = (lax.axis_index(a) for a in CTX)
    c = lax.axis_index(CTX)
    g = lax.axis_index(GROUP)
    where = jnp.stack([xh, z, core]).astype(jnp.int32)
    gains = norm_gains.reshape(2, 32, 128)

    wq = jnp.stack([w_cross_query, swap_xh(w_cross_query)])
    wq_ring = ring(wq)
    wq_other = [swap_cores(p) for p in wq_ring]
    arrived = lax.all_to_all(nbr_kv[0, 0], "y", split_axis=0, concat_axis=0, tiled=True)

    dealt = deal_out_weights(jnp.stack([w_cross_out, w_self_out]), c)
    dealt_other = swap_xh(dealt)
    wo_ring = ring(jnp.stack([dealt[0], dealt_other[0]]))
    wo_other = [swap_cores(p) for p in wo_ring]

    qkv_own = w_self_qkv.transpose(1, 0, 2)
    qkv_other = swap_xh(qkv_own)

    def halves(x):
        return x.reshape(64, 2, 256).transpose(1, 0, 2).reshape(1, 128, 256)

    late = jnp.concatenate([qkv_own, qkv_other, halves(dealt[1]), halves(dealt_other[1])], axis=0)
    late_own = lax.all_gather(late, "z", axis=0, tiled=False)
    late_par = swap_cores(late_own)

    cross_att = call(
        cross_kernel,
        jax.ShapeDtypeStruct((rows, 256), bf16),
        [SMEM] * 3 + [VMEM] * 21,
        [pltpu.VMEM((rows, width), bf16)],
        600_000_000,
        5_000_000,
    )(where, nbr_source.reshape(-1), nbr_count, hidden_in, gains[0], arrived.reshape(12, 64, 512), *wq_ring, *wq_other)

    att_all = lax.all_to_all(
        jnp.broadcast_to(cross_att[None], (8, rows, 256)), GROUP, 0, 0, tiled=True
    )
    hidden_share = lax.dynamic_slice_in_dim(hidden_in, g * 512, 512, 1)
    mid_share = call(
        cross_out_kernel,
        jax.ShapeDtypeStruct((rows, 512), bf16),
        [SMEM] + [VMEM] * 20,
        [pltpu.VMEM((2048, 512), bf16)],
        600_000_000,
        4_000_000,
    )(where, att_all, hidden_share, *wo_ring, *wo_other)

    mids = lax.all_to_all(
        jnp.broadcast_to(mid_share[None], (8, rows, 512)), GROUP, 0, 0, tiled=True
    )
    keep, send = call(
        qkv_kernel,
        [jax.ShapeDtypeStruct((3, rows, HD), bf16)] * 2,
        [SMEM] + [VMEM] * 4,
        [pltpu.VMEM((rows, width), bf16), pltpu.VMEM((rows, 256), bf16)],
        1_600_000_000,
        11_000_000,
    )(where, mids, gains[1], late_own, late_par)

    got = swap_xh(send)
    both = jnp.concatenate([keep, got], axis=1)
    kv_ring = ring(both[1:])
    kv_other = [swap_cores(p) for p in kv_ring]
    heads = call(
        attention_kernel,
        jax.ShapeDtypeStruct((2, rows, HD), bf16),
        [SMEM] * 2 + [VMEM] * 19,
        [],
        2_200_000_000,
        5_000_000,
    )(where, span_order, both[0], *kv_ring, *kv_other)

    self_all = lax.all_to_all(
        jnp.broadcast_to(heads[:, None], (2, 8, rows, HD)).reshape(16, rows, HD),
        ("xh",) + GROUP,
        0,
        0,
        tiled=True,
    ).reshape(2, 8, rows, HD)
    return call(
        self_out_kernel,
        jax.ShapeDtypeStruct((rows, 512), bf16),
        [SMEM] + [VMEM] * 4,
        [pltpu.VMEM((2048, 512), bf16)],
        600_000_000,
        10_000_000,
    )(where, self_all, mid_share, late_own, late_par)


def solution(mesh):
    fine = Mesh(mesh.devices.reshape(2, 8, 2, 4, 2), ALL)
    in_specs = (
        P(CTX, None),
        P(),
        P(CTX, GROUP),
        P(GROUP, CTX),
        P(CTX, None, GROUP),
        P(GROUP, CTX),
        P(CTX, "y", None, None, None, "xl"),
        P(CTX),
        P(CTX, None),
        P(),
    )
    return jax.shard_map(
        per_device, mesh=fine, in_specs=in_specs, out_specs=P(CTX, GROUP), check_vma=False
    )
```

```python
import functools
import math

import jax
import jax.numpy as jnp
from jax import lax
from jax.experimental import pallas as pl
from jax.experimental.pallas import tpu as pltpu
from jax.sharding import Mesh
from jax.sharding import PartitionSpec as P

HD = 128
SPAN = 64
epsilon = 1e-05
far_below = -1e30
NZ = 8

VMEM = pl.BlockSpec(memory_space=pltpu.VMEM)
SMEM = pl.BlockSpec(memory_space=pltpu.SMEM)
ANY = pl.BlockSpec(memory_space=pl.ANY)
f32 = jnp.float32
bf16 = jnp.bfloat16

CTX = ("xh", "z", "core")
GROUP = ("y", "xl")
ALL = CTX + GROUP


def dot(a, b):
    return jnp.dot(a, b, preferred_element_type=f32)


def dot_t(a, b):
    return lax.dot_general(a, b, (((1,), (1,)), ((), ())), preferred_element_type=f32)


def call(kernel, out_shape, in_specs, scratch, flops, nbytes):
    return pl.pallas_call(
        kernel,
        out_shape=out_shape,
        in_specs=in_specs,
        out_specs=jax.tree.map(lambda _: VMEM, out_shape),
        scratch_shapes=scratch,
        compiler_params=pltpu.CompilerParams(vmem_limit_bytes=56 * 1024 * 1024),
        cost_estimate=pl.CostEstimate(flops=flops, bytes_accessed=nbytes, transcendentals=0),
    )


def ring(x, first=None, last=None):
    if first is not None:
        x = after(x, first)
    up = [(i, (i + 1) % NZ) for i in range(NZ)]
    down = [(i, (i - 1) % NZ) for i in range(NZ)]
    r1 = lax.ppermute(x, "z", up)
    l1 = lax.ppermute(x, "z", down)
    r2 = lax.ppermute(r1, "z", up)
    l2 = lax.ppermute(l1, "z", down)
    r3 = lax.ppermute(r2, "z", up)
    l3 = lax.ppermute(l2, "z", down)
    if last is not None:
        r3 = after(r3, last)
        l3 = after(l3, last)
    r4 = lax.ppermute(r3[:1], "z", up)
    l4 = lax.ppermute(l3[1:], "z", down)
    return [x, l1, l2, l3, r4, l4, r3, r2, r1]


def fetch_pieces(pieces, other, target, sems):
    copies = []
    for i, piece in enumerate(pieces):
        if i == 4 or i == 5:
            place = target.at[4, pl.ds(i - 4, 1)]
        else:
            place = target.at[i if i < 4 else i - 1]
        copies.append(pltpu.make_async_copy(piece, place, sems.at[9 * other + i]))
    return copies


def wait_distance(copies, distance):
    for i in (4, 5) if distance == 4 else (distance if distance < 4 else distance + 1,):
        copies[i].wait()


def after(x, *earlier):
    return lax.optimization_barrier((x,) + earlier)[0]


def swap_cores(x):
    return lax.ppermute(x, "core", [(0, 1), (1, 0)])


def swap_xh(x):
    return lax.ppermute(x, "xh", [(0, 1), (1, 0)])


def cross_kernel(where, source, count, gain, hidden_in, nbr_in, *rest):
    pieces = (rest[:9], rest[9:18])
    out, normed, hidden, nbr, weights, sems = rest[18:]
    xh, z, core = where[0], where[1], where[2]
    hidden_copy = pltpu.make_async_copy(hidden_in, hidden, sems.at[18])
    nbr_copy = pltpu.make_async_copy(nbr_in, nbr, sems.at[19])
    hidden_copy.start()
    copies = [fetch_pieces(pieces[other], other, weights.at[other], sems) for other in range(2)]
    for i in range(9):
        copies[0][i].start()
        copies[1][i].start()
    nbr_copy.start()
    hidden_copy.wait()
    values = hidden[...].astype(f32)
    row_scale = lax.rsqrt(jnp.mean(values * values, axis=1, keepdims=True) + epsilon)
    for b in range(32):
        cols = slice(b * 128, (b + 1) * 128)
        block = hidden[:, cols].astype(f32)
        normed[:, cols] = (block * row_scale * gain[b : b + 1, :]).astype(bf16)
    acc = jnp.zeros(out.shape, f32)
    for distance in range(NZ):
        zz = lax.rem(z + distance, NZ)
        for other in range(2):
            wait_distance(copies[other], distance)
            left, right = [], []
            for side in range(2):
                owner = (xh ^ side) * 16 + zz * 2 + (core ^ other)
                left.append(normed[:, pl.ds(pl.multiple_of(owner * 128, 128), 128)])
                right.append(weights[other, distance, side])
            acc += dot(jnp.concatenate(left, axis=1), jnp.concatenate(right, axis=0))
    query = acc.astype(bf16)
    nbr_copy.wait()
    scale = 1.0 / math.sqrt(HD)
    lanes = lax.broadcasted_iota(jnp.int32, (SPAN, 128), 1)
    chosen = [source[i] for i in range(8)]
    for s in range(4):
        slots = []
        for j in range(2):
            i = s * 2 + j
            rank = jnp.int32(0)
            for k in range(s * 2):
                rank = rank + (chosen[k] == chosen[i]).astype(jnp.int32)
            slots.append(chosen[i] * 3 + rank)
        alive = lanes < count[s] * 64
        for h in range(2):
            kcols = slice(2 * h * HD, (2 * h + 1) * HD)
            vcols = slice((2 * h + 1) * HD, (2 * h + 2) * HD)
            keys = jnp.concatenate([nbr[slots[0], :, kcols], nbr[slots[1], :, kcols]], axis=0)
            vals = jnp.concatenate([nbr[slots[0], :, vcols], nbr[slots[1], :, vcols]], axis=0)
            part = query[s * SPAN : (s + 1) * SPAN, h * HD : (h + 1) * HD]
            scores = jnp.where(alive, dot_t(part, keys) * scale, far_below)
            top = jnp.max(scores, axis=1, keepdims=True)
            weights = jnp.exp(scores - top)
            total = jnp.sum(weights, axis=1, keepdims=True)
            mixed = dot(weights.astype(bf16), vals) / total
            out[s * SPAN : (s + 1) * SPAN, h * HD : (h + 1) * HD] = mixed.astype(bf16)


def cross_out_kernel(where, share, att_in, *rest):
    pieces = (rest[:9], rest[9:18])
    out, att, weights, sems = rest[18:]
    xh, z, core = where[0], where[1], where[2]
    copies = [pltpu.make_async_copy(att_in, att, sems.at[0])]
    for distance in range(NZ):
        zz = lax.rem(z + distance, NZ)
        for other in range(2):
            for side in range(2):
                first = (core ^ other) * 1024 + (zz * 2 + (xh ^ side)) * 64
                if distance == 4:
                    block = pieces[other][4 + side].at[0]
                else:
                    block = pieces[other][distance if distance < 4 else distance + 1].at[side]
                place = weights.at[pl.ds(pl.multiple_of(first, 64), 64)]
                copies.append(pltpu.make_async_copy(block, place, sems.at[len(copies)]))
    for copy in copies:
        copy.start()
    for copy in copies:
        copy.wait()
    acc = share[...].astype(f32)
    for g in range(8):
        acc += dot(att[g], weights[g * 256 : (g + 1) * 256, :])
    out[...] = acc.astype(bf16)


def qkv_kernel(where, gain, mids_in, own, par, keep, send, normed, proj, mids, weights, sems):
    xh, core = where[0], where[2]
    mids_copy = pltpu.make_async_copy(mids_in, mids, sems.at[16])
    mids_copy.start()
    copies = []
    for z in range(NZ):
        for other in range(2):
            block = (own, par)[other].at[z]
            copies.append(pltpu.make_async_copy(block, weights.at[other, z], sems.at[z * 2 + other]))
    for copy in copies:
        copy.start()
    mids_copy.wait()
    total = jnp.zeros((mids.shape[1], 1), f32)
    for g in range(8):
        values = mids[g].astype(f32)
        total += jnp.sum(values * values, axis=1, keepdims=True)
    row_scale = lax.rsqrt(total * (1.0 / 4096) + epsilon)
    for b in range(32):
        block = mids[b // 4, :, (b % 4) * 128 : (b % 4 + 1) * 128].astype(f32)
        normed[:, b * 128 : (b + 1) * 128] = (block * row_scale * gain[b : b + 1, :]).astype(bf16)
    for copy in copies:
        copy.wait()
    for t in range(3):
        acc = jnp.zeros((mids.shape[1], 256), f32)
        for z in range(NZ):
            for other in range(2):
                left, right = [], []
                for side in range(2):
                    owner = (xh ^ side) * 16 + z * 2 + (core ^ other)
                    left.append(normed[:, pl.ds(pl.multiple_of(owner * 128, 128), 128)])
                    right.append(weights[other, z, side * 3 + t])
                acc += dot(jnp.concatenate(left, axis=1), jnp.concatenate(right, axis=0))
        if t == 0:
            acc = acc * (math.log2(math.e) / math.sqrt(HD))
        proj[...] = acc.astype(bf16)
        keep[t] = proj[:, pl.ds(pl.multiple_of(xh * 128, 128), 128)]
        send[t] = proj[:, pl.ds(pl.multiple_of((1 - xh) * 128, 128), 128)]


def attention_kernel(where, order, query, *rest):
    pieces = (rest[:9], rest[9:18])
    out, kv, sems = rest[18:]
    xh, z, core = where[0], where[1], where[2]
    copies = [fetch_pieces(pieces[other], other, kv.at[other], sems) for other in range(2)]
    for i in range(9):
        copies[0][i].start()
        copies[1][i].start()
    rows = lax.broadcasted_iota(jnp.int32, (SPAN, 1), 0)
    lanes = lax.broadcasted_iota(jnp.int32, (1, 256), 1)
    span_of, within = lanes // SPAN, lanes % SPAN
    q_places = []
    for side in range(2):
        c = (xh ^ side) * 16 + z * 2 + core
        for s in range(4):
            q_places.append(order[c * 4 + s] * SPAN + rows)
    q_places = jnp.concatenate(q_places, axis=0)
    top = jnp.full((512, 1), far_below, f32)
    total = jnp.zeros((512, 1), f32)
    mixed = jnp.zeros((512, HD), f32)
    for distance in range(NZ):
        zz = lax.rem(z + distance, NZ)
        for other in range(2):
            places = []
            for side in range(2):
                c = (xh ^ side) * 16 + zz * 2 + (core ^ other)
                place = jnp.zeros((1, 256), jnp.int32)
                for s in range(4):
                    place = jnp.where(span_of == s, order[c * 4 + s], place)
                places.append(place * SPAN + within)
            k_places = jnp.concatenate(places, axis=1)
            wait_distance(copies[other], distance)
            scores = dot_t(query[...], kv[other, distance, 0])
            visible = k_places <= q_places
            scores = jnp.where(visible, scores, far_below)
            new_top = jnp.maximum(top, jnp.max(scores, axis=1, keepdims=True))
            weights = jnp.where(visible, jnp.exp2(scores - new_top), 0.0)
            fade = jnp.exp2(top - new_top)
            total = total * fade + jnp.sum(weights, axis=1, keepdims=True)
            mixed = mixed * fade + dot(weights.astype(bf16), kv[other, distance, 1])
            top = new_top
    result = (mixed / total).astype(bf16)
    out[xh] = result[:256]
    out[1 - xh] = result[256:]


def self_out_kernel(where, share, att_in, own, par, out, att, weights, sems):
    xh, core = where[0], where[2]
    copies = [pltpu.make_async_copy(att_in, att, sems.at[0])]
    for z in range(NZ):
        for other in range(2):
            for side in range(2):
                first = (core ^ other) * 1024 + (z * 2 + (xh ^ side)) * 64
                place = weights.at[pl.ds(pl.multiple_of(first, 64), 64)]
                copies.append(pltpu.make_async_copy((own, par)[other].at[z, side], place, sems.at[len(copies)]))
    for copy in copies:
        copy.start()
    for copy in copies:
        copy.wait()
    acc = share[...].astype(f32)
    for g in range(8):
        both = jnp.concatenate([att[0, g], att[1, g]], axis=1)
        acc += dot(both, weights[g * 256 : (g + 1) * 256, :])
    out[...] = acc.astype(bf16)


def deal_out_weights(blocks, c):
    n = blocks.shape[0]
    quarters = blocks.reshape(n, 4, 64, 128)
    turn = c % 4
    arrived = []
    for i in range(4):
        pairs = []
        for source_c in range(32):
            for source_g in range(8):
                r = source_g * 4 + (i + source_c) % 4
                target_c = (r % 2) * 16 + ((r % 16) // 2) * 2 + r // 16
                pairs.append((source_c * 8 + source_g, target_c * 8 + source_c // 4))
        piece = lax.dynamic_index_in_dim(quarters, (i + turn) % 4, 1, keepdims=False)
        arrived.append(lax.ppermute(piece, ALL, pairs))
    r = (c % 2) * 16 + ((c // 2) % 8) * 2 + c // 16
    stacked = jnp.stack(arrived)
    columns = [lax.dynamic_index_in_dim(stacked, (r - q) % 4, 0, keepdims=False) for q in range(4)]
    return jnp.concatenate(columns, axis=2)


def per_device(
    hidden_in,
    norm_gains,
    w_cross_query,
    w_cross_out,
    w_self_qkv,
    w_self_out,
    nbr_kv,
    nbr_count,
    nbr_source,
    span_order,
):
    rows, width = hidden_in.shape
    xh, z, core = (lax.axis_index(a) for a in CTX)
    c = lax.axis_index(CTX)
    g = lax.axis_index(GROUP)
    where = jnp.stack([xh, z, core]).astype(jnp.int32)
    gains = norm_gains.reshape(2, 32, 128)

    wq = jnp.stack([w_cross_query, swap_xh(w_cross_query)])
    nbr = after(nbr_kv[0, 0], wq)
    arrived = lax.all_to_all(nbr, "y", split_axis=0, concat_axis=0, tiled=True)
    wq_ring = ring(wq, last=arrived)
    wq_other = [swap_cores(p) for p in wq_ring]

    blocks = after(jnp.stack([w_cross_out, w_self_out]), wq_ring[1], wq_ring[8])
    dealt = deal_out_weights(blocks, c)
    dealt_other = swap_xh(dealt)

    qkv_own = w_self_qkv.transpose(1, 0, 2)
    qkv_other = swap_xh(qkv_own)

    late = jnp.concatenate([qkv_own, qkv_other], axis=0)
    late_own = lax.all_gather(late, "z", axis=0, tiled=False)

    cross_att = call(
        cross_kernel,
        jax.ShapeDtypeStruct((rows, 256), bf16),
        [SMEM] * 3 + [VMEM] + [ANY] * 20,
        [
            pltpu.VMEM((rows, width), bf16),
            pltpu.VMEM((rows, width), bf16),
            pltpu.VMEM((12, 64, 512), bf16),
            pltpu.VMEM((2, NZ, 2, 128, 256), bf16),
            pltpu.SemaphoreType.DMA((20,)),
        ],
        600_000_000,
        5_000_000,
    )(where, nbr_source.reshape(-1), nbr_count, gains[0], hidden_in, arrived.reshape(12, 64, 512), *wq_ring, *wq_other)

    wo_ring = ring(jnp.stack([dealt[0], dealt_other[0]]), last=cross_att)
    wo_other = [swap_cores(p) for p in wo_ring]
    att_all = lax.all_to_all(
        jnp.broadcast_to(cross_att[None], (8, rows, 256)), GROUP, 0, 0, tiled=True
    )
    hidden_share = lax.dynamic_slice_in_dim(hidden_in, g * 512, 512, 1)
    mid_share = call(
        cross_out_kernel,
        jax.ShapeDtypeStruct((rows, 512), bf16),
        [SMEM] + [VMEM] + [ANY] * 19,
        [pltpu.VMEM((8, rows, 256), bf16), pltpu.VMEM((2048, 512), bf16), pltpu.SemaphoreType.DMA((33,))],
        600_000_000,
        4_000_000,
    )(where, hidden_share, att_all, *wo_ring, *wo_other)

    late_own, mid_share = lax.optimization_barrier((late_own, mid_share))
    late_par = swap_cores(late_own)
    wso_own = lax.all_gather(after(jnp.stack([dealt[1], dealt_other[1]]), late_own), "z", axis=0, tiled=False)
    mids = lax.all_to_all(
        jnp.broadcast_to(mid_share[None], (8, rows, 512)), GROUP, 0, 0, tiled=True
    )
    keep, send = call(
        qkv_kernel,
        [jax.ShapeDtypeStruct((3, rows, HD), bf16)] * 2,
        [SMEM] + [VMEM] + [ANY] * 3,
        [
            pltpu.VMEM((rows, width), bf16),
            pltpu.VMEM((rows, 256), bf16),
            pltpu.VMEM((8, rows, 512), bf16),
            pltpu.VMEM((2, NZ, 6, 128, 256), bf16),
            pltpu.SemaphoreType.DMA((17,)),
        ],
        1_600_000_000,
        11_000_000,
    )(where, gains[1], mids, late_own, late_par)

    got = swap_xh(send)
    both = jnp.concatenate([keep, got], axis=1)
    kv_ring = ring(both[1:])
    kv_other = [swap_cores(p) for p in kv_ring]
    wso_own = after(wso_own, kv_ring[3])
    wso_par = swap_cores(wso_own)
    heads = call(
        attention_kernel,
        jax.ShapeDtypeStruct((2, rows, HD), bf16),
        [SMEM] * 2 + [VMEM] + [ANY] * 18,
        [pltpu.VMEM((2, NZ, 2, 2 * rows, HD), bf16), pltpu.SemaphoreType.DMA((18,))],
        2_200_000_000,
        5_000_000,
    )(where, span_order, both[0], *kv_ring, *kv_other)

    self_all = lax.all_to_all(
        jnp.broadcast_to(heads[:, None], (2, 8, rows, HD)).reshape(16, rows, HD),
        ("xh",) + GROUP,
        0,
        0,
        tiled=True,
    ).reshape(2, 8, rows, HD)
    return call(
        self_out_kernel,
        jax.ShapeDtypeStruct((rows, 512), bf16),
        [SMEM] + [VMEM] + [ANY] * 3,
        [
            pltpu.VMEM((2, 8, rows, HD), bf16),
            pltpu.VMEM((2048, 512), bf16),
            pltpu.SemaphoreType.DMA((33,)),
        ],
        600_000_000,
        4_000_000,
    )(where, mid_share, self_all, wso_own, wso_par)


def solution(mesh):
    fine = Mesh(mesh.devices.reshape(2, 8, 2, 4, 2), ALL)
    in_specs = (
        P(CTX, None),
        P(),
        P(CTX, GROUP),
        P(GROUP, CTX),
        P(CTX, None, GROUP),
        P(GROUP, CTX),
        P(CTX, "y", None, None, None, "xl"),
        P(CTX),
        P(CTX, None),
        P(),
    )
    return jax.shard_map(
        per_device, mesh=fine, in_specs=in_specs, out_specs=P(CTX, GROUP), check_vma=False
    )
```

```python
import functools
import math

import jax
import jax.numpy as jnp
from jax import lax
from jax.experimental import pallas as pl
from jax.experimental.pallas import tpu as pltpu
from jax.sharding import Mesh
from jax.sharding import PartitionSpec as P

HD = 128
SPAN = 64
epsilon = 1e-05
far_below = -1e30
NZ = 8

VMEM = pl.BlockSpec(memory_space=pltpu.VMEM)
SMEM = pl.BlockSpec(memory_space=pltpu.SMEM)
f32 = jnp.float32
bf16 = jnp.bfloat16

CTX = ("xh", "z", "core")
GROUP = ("y", "xl")
ALL = CTX + GROUP


def dot(a, b):
    return jnp.dot(a, b, preferred_element_type=f32)


def dot_t(a, b):
    return lax.dot_general(a, b, (((1,), (1,)), ((), ())), preferred_element_type=f32)


def call(kernel, out_shape, in_specs, scratch, flops, nbytes):
    return pl.pallas_call(
        kernel,
        out_shape=out_shape,
        in_specs=in_specs,
        out_specs=jax.tree.map(lambda _: VMEM, out_shape),
        scratch_shapes=scratch,
        compiler_params=pltpu.CompilerParams(vmem_limit_bytes=20 * 1024 * 1024),
        cost_estimate=pl.CostEstimate(flops=flops, bytes_accessed=nbytes, transcendentals=0),
    )


def shift_z(x, by):
    return lax.ppermute(x, "z", [(i, (i + by) % NZ) for i in range(NZ)])


def gather_z(x, between=None):
    r1, l1, r2, l2 = shift_z(x, 1), shift_z(x, -1), shift_z(x, 2), shift_z(x, -2)
    if between is not None:
        r1, l1, r2, l2, _ = lax.optimization_barrier((r1, l1, r2, l2, between))
    r3, l3 = shift_z(r1, 2), shift_z(l1, -2)
    r4, l4 = shift_z(r2[:1], 2), shift_z(l2[1:], -2)
    return [x, l1, l2, l3, r4, l4, r3, r2, r1]


def half(pieces, distance, side):
    if distance < 4:
        return pieces[distance], side
    if distance == 4:
        return pieces[4 + side], 0
    return pieces[distance + 1], side


def shift_group(x, dy, dx):
    pairs = [(y * 2 + xl, (y + dy) % 4 * 2 + (xl ^ dx)) for y in range(4) for xl in range(2)]
    return lax.ppermute(x, GROUP, pairs)


PEERS = ((0, 0), (1, 0), (3, 0), (0, 1), (1, 1), (3, 1), (2, 0), (2, 1))


def gather_group(x):
    return [x] + [shift_group(x, dy, dx) for dy, dx in PEERS[1:]]


def gather_group_small(x):
    w = shift_group(x, 0, 1)
    near = {(dy, 0): shift_group(x, dy, 0) for dy in (1, 3, 2)}
    far = {(dy, 1): shift_group(w, dy, 0) for dy in (1, 3, 2)}
    pieces = {(0, 0): x, (0, 1): w, **near, **far}
    return [pieces[p] for p in PEERS]


def peer_group(where, i):
    dy, dx = PEERS[i]
    return lax.rem(where[3] + 4 - dy, 4) * 2 + (where[4] ^ dx)


def after(x, *earlier):
    return lax.optimization_barrier((x,) + earlier)[0]


def swap_cores(x):
    return lax.ppermute(x, "core", [(0, 1), (1, 0)])


def swap_xh(x):
    return lax.ppermute(x, "xh", [(0, 1), (1, 0)])


def block_of(where, zz, other, side):
    return (where[0] ^ side) * 16 + zz * 2 + (where[2] ^ other)


def cross_kernel(where, source, count, gain, hidden, nbr, *rest):
    pieces = (rest[:9], rest[9:18])
    out, normed = rest[18:]
    values = hidden[...].astype(f32)
    row_scale = lax.rsqrt(jnp.mean(values * values, axis=1, keepdims=True) + epsilon)
    for b in range(32):
        cols = slice(b * 128, (b + 1) * 128)
        block = hidden[:, cols].astype(f32)
        normed[:, cols] = (block * row_scale * gain[b : b + 1, :]).astype(bf16)
    acc = jnp.zeros(out.shape, f32)
    for distance in range(NZ):
        zz = lax.rem(where[1] + distance, NZ)
        for other in range(2):
            left, right = [], []
            for side in range(2):
                owner = block_of(where, zz, other, side)
                left.append(normed[:, pl.ds(pl.multiple_of(owner * 128, 128), 128)])
                ref, index = half(pieces[other], distance, side)
                right.append(ref[index])
            acc += dot(jnp.concatenate(left, axis=1), jnp.concatenate(right, axis=0))
    query = acc.astype(bf16)
    scale = 1.0 / math.sqrt(HD)
    lanes = lax.broadcasted_iota(jnp.int32, (SPAN, 128), 1)
    chosen = [source[i] for i in range(8)]
    for s in range(4):
        slots = []
        for j in range(2):
            i = s * 2 + j
            rank = jnp.int32(0)
            for k in range(s * 2):
                rank = rank + (chosen[k] == chosen[i]).astype(jnp.int32)
            slots.append(chosen[i] * 3 + rank)
        alive = lanes < count[s] * 64
        for h in range(2):
            kcols = slice(2 * h * HD, (2 * h + 1) * HD)
            vcols = slice((2 * h + 1) * HD, (2 * h + 2) * HD)
            keys = jnp.concatenate([nbr[slots[0], :, kcols], nbr[slots[1], :, kcols]], axis=0)
            vals = jnp.concatenate([nbr[slots[0], :, vcols], nbr[slots[1], :, vcols]], axis=0)
            part = query[s * SPAN : (s + 1) * SPAN, h * HD : (h + 1) * HD]
            scores = jnp.where(alive, dot_t(part, keys) * scale, far_below)
            top = jnp.max(scores, axis=1, keepdims=True)
            weights = jnp.exp(scores - top)
            total = jnp.sum(weights, axis=1, keepdims=True)
            mixed = dot(weights.astype(bf16), vals) / total
            out[s * SPAN : (s + 1) * SPAN, h * HD : (h + 1) * HD] = mixed.astype(bf16)


def weight_rows(where, zz, other, side):
    first = (where[2] ^ other) * 1024 + (zz * 2 + (where[0] ^ side)) * 64
    return pl.ds(pl.multiple_of(first, 64), 64)


def cross_out_kernel(where, share, *rest):
    att, pieces = rest[:8], (rest[8:17], rest[17:26])
    out, weights = rest[26:]
    for distance in range(NZ):
        zz = lax.rem(where[1] + distance, NZ)
        for other in range(2):
            for side in range(2):
                ref, index = half(pieces[other], distance, side)
                weights[weight_rows(where, zz, other, side), :] = ref[index]
    acc = share[...].astype(f32)
    for i in range(8):
        first = pl.multiple_of(peer_group(where, i) * 256, 256)
        acc += dot(att[i][...], weights[pl.ds(first, 256), :])
    out[...] = acc.astype(bf16)


def qkv_kernel(where, gain, own, par, *rest):
    mids = rest[:8]
    keep, send, normed, proj = rest[8:]
    xh = where[0]
    rows = mids[0].shape[0]
    squares = jnp.zeros((rows, 512), f32)
    for i in range(8):
        values = mids[i][...].astype(f32)
        squares += values * values
    row_scale = lax.rsqrt(jnp.sum(squares, axis=1, keepdims=True) * (1.0 / 4096) + epsilon)
    for i in range(8):
        first = peer_group(where, i) * 4
        for j in range(4):
            block = mids[i][:, j * 128 : (j + 1) * 128].astype(f32)
            scaled = (block * row_scale * gain[pl.ds(first + j, 1), :]).astype(bf16)
            normed[:, pl.ds(pl.multiple_of((first + j) * 128, 128), 128)] = scaled
    for t in range(3):
        acc = jnp.zeros((rows, 256), f32)
        for z in range(NZ):
            for other in range(2):
                left, right = [], []
                for side in range(2):
                    owner = block_of(where, z, other, side)
                    left.append(normed[:, pl.ds(pl.multiple_of(owner * 128, 128), 128)])
                    right.append((own, par)[other][z, side * 3 + t])
                acc += dot(jnp.concatenate(left, axis=1), jnp.concatenate(right, axis=0))
        if t == 0:
            acc = acc * (math.log2(math.e) / math.sqrt(HD))
        proj[...] = acc.astype(bf16)
        keep[t] = proj[:, pl.ds(pl.multiple_of(xh * 128, 128), 128)]
        send[t] = proj[:, pl.ds(pl.multiple_of((1 - xh) * 128, 128), 128)]


def attention_kernel(distances, last, where, order, query, *rest):
    first = distances[0] == 0
    if not first:
        mixed_in, top_in, total_in = rest[:3]
        rest = rest[3:]
    count = len(rest) - (2 if last else 3)
    refs, outs = rest[:count], rest[count:]
    where_of = {}
    for distance in distances:
        where_of[distance] = [len(where_of) + sum(d == 4 for d in where_of)] * 2
        if distance == 4:
            where_of[distance][1] += 1
    each = count // 2
    rows = lax.broadcasted_iota(jnp.int32, (SPAN, 1), 0)
    lanes = lax.broadcasted_iota(jnp.int32, (1, 256), 1)
    span_of, within = lanes // SPAN, lanes % SPAN
    q_places = []
    for side in range(2):
        c = block_of(where, where[1], 0, side)
        for s in range(4):
            q_places.append(order[c * 4 + s] * SPAN + rows)
    q_places = jnp.concatenate(q_places, axis=0)
    if first:
        top = jnp.full((512, 1), far_below, f32)
        total = jnp.zeros((512, 1), f32)
        mixed = jnp.zeros((512, HD), f32)
    else:
        top, total, mixed = top_in[...], total_in[...], mixed_in[...]
    for distance in distances:
        zz = lax.rem(where[1] + distance, NZ)
        for other in range(2):
            places = []
            for side in range(2):
                c = block_of(where, zz, other, side)
                place = jnp.zeros((1, 256), jnp.int32)
                for s in range(4):
                    place = jnp.where(span_of == s, order[c * 4 + s], place)
                places.append(place * SPAN + within)
            k_places = jnp.concatenate(places, axis=1)
            k_ref, v_ref = (refs[other * each + i] for i in where_of[distance])
            keys, vals = k_ref[0], v_ref[0 if distance == 4 else 1]
            scores = dot_t(query[...], keys)
            visible = k_places <= q_places
            scores = jnp.where(visible, scores, far_below)
            new_top = jnp.maximum(top, jnp.max(scores, axis=1, keepdims=True))
            weights = jnp.where(visible, jnp.exp2(scores - new_top), 0.0)
            fade = jnp.exp2(top - new_top)
            total = total * fade + jnp.sum(weights, axis=1, keepdims=True)
            mixed = mixed * fade + dot(weights.astype(bf16), vals)
            top = new_top
    if last:
        result = (mixed / total).astype(bf16)
        outs[0][...] = result[:256]
        outs[1][...] = result[256:]
    else:
        outs[0][...], outs[1][...], outs[2][...] = mixed, top, total


def attention_part(distances, last, state, where, order, query, own, par):
    n = query.shape[0]
    if last:
        shape = [jax.ShapeDtypeStruct((n // 2, HD), bf16)] * 2
    else:
        shape = [jax.ShapeDtypeStruct((n, w), f32) for w in (HD, 1, 1)]
    return call(
        functools.partial(attention_kernel, distances, last),
        shape,
        [SMEM] * 2 + [VMEM] * (1 + len(state) + len(own) + len(par)),
        [],
        280_000_000 * len(distances),
        500_000 * len(distances),
    )(where, order, query, *state, *own, *par)


def self_out_kernel(where, share, own, par, *rest):
    near, far = rest[:8], rest[8:16]
    out, weights = rest[16:]
    for z in range(NZ):
        for other in range(2):
            for side in range(2):
                weights[weight_rows(where, z, other, side), :] = (own, par)[other][z, side]
    acc = share[...].astype(f32)
    for i in range(8):
        first = peer_group(where, i) * 256
        both = jnp.concatenate([near[i][...], far[i][...]], axis=1)
        right = [
            weights[pl.ds(pl.multiple_of(first + head * 128, 128), 128), :]
            for head in (where[0], 1 - where[0])
        ]
        acc += dot(both, jnp.concatenate(right, axis=0))
    out[...] = acc.astype(bf16)


def deal_out_weights(blocks, c):
    n = blocks.shape[0]
    quarters = blocks.reshape(n, 4, 64, 128)
    turn = c % 4
    arrived = []
    for i in range(4):
        pairs = []
        for source_c in range(32):
            for source_g in range(8):
                r = source_g * 4 + (i + source_c) % 4
                target_c = (r % 2) * 16 + ((r % 16) // 2) * 2 + r // 16
                pairs.append((source_c * 8 + source_g, target_c * 8 + source_c // 4))
        piece = lax.dynamic_index_in_dim(quarters, (i + turn) % 4, 1, keepdims=False)
        arrived.append(lax.ppermute(piece, ALL, pairs))
    r = (c % 2) * 16 + ((c // 2) % 8) * 2 + c // 16
    stacked = jnp.stack(arrived)
    columns = [lax.dynamic_index_in_dim(stacked, (r - q) % 4, 0, keepdims=False) for q in range(4)]
    return jnp.concatenate(columns, axis=2)


def per_device(
    hidden_in,
    norm_gains,
    w_cross_query,
    w_cross_out,
    w_self_qkv,
    w_self_out,
    nbr_kv,
    nbr_count,
    nbr_source,
    span_order,
):
    rows, width = hidden_in.shape
    c = lax.axis_index(CTX)
    g = lax.axis_index(GROUP)
    where = jnp.stack([lax.axis_index(a) for a in ALL]).astype(jnp.int32)
    gains = norm_gains.reshape(2, 32, 128)
    vmem = pltpu.VMEM

    wq = jnp.stack([w_cross_query, swap_xh(w_cross_query)])
    qkv_own, nbr, _ = lax.optimization_barrier((w_self_qkv.transpose(1, 0, 2), nbr_kv[0, 0], wq))
    arrived = lax.all_to_all(nbr, "y", split_axis=0, concat_axis=0, tiled=True)
    wq_own = gather_z(wq)
    wq_par = [swap_cores(p) for p in wq_own]

    late_own = lax.all_gather(jnp.concatenate([qkv_own, swap_xh(qkv_own)], axis=0), "z", axis=0, tiled=False)

    blocks = after(jnp.stack([w_cross_out, w_self_out]), wq_own[1], wq_own[2], wq_own[7], wq_own[8])
    dealt = deal_out_weights(blocks, c)
    dealt_other = swap_xh(dealt)

    cross_att = call(
        cross_kernel,
        jax.ShapeDtypeStruct((rows, 256), bf16),
        [SMEM] * 3 + [VMEM] * 21,
        [vmem((rows, width), bf16)],
        600_000_000,
        5_000_000,
    )(where, nbr_source.reshape(-1), nbr_count, gains[0], hidden_in, arrived.reshape(12, 64, 512), *wq_own, *wq_par)

    wo_own = gather_z(jnp.stack([dealt[0], dealt_other[0]]), cross_att)
    wo_par = [swap_cores(p) for p in wo_own]
    hidden_share = lax.dynamic_slice_in_dim(hidden_in, g * 512, 512, 1)
    mid_share = call(
        cross_out_kernel,
        jax.ShapeDtypeStruct((rows, 512), bf16),
        [SMEM] + [VMEM] * 27,
        [vmem((2048, 512), bf16)],
        600_000_000,
        4_000_000,
    )(where, hidden_share, *gather_group_small(cross_att), *wo_own, *wo_par)

    late_own, mid_share = lax.optimization_barrier((late_own, mid_share))
    late_par = swap_cores(late_own)
    wso_own = lax.all_gather(after(jnp.stack([dealt[1], dealt_other[1]]), late_own), "z", axis=0, tiled=False)
    keep, send = call(
        qkv_kernel,
        [jax.ShapeDtypeStruct((3, rows, HD), bf16)] * 2,
        [SMEM] + [VMEM] * 11,
        [vmem((rows, width), bf16), vmem((rows, 256), bf16)],
        1_600_000_000,
        11_000_000,
    )(where, gains[1], late_own, late_par, *gather_group(mid_share))

    both = jnp.concatenate([keep, swap_xh(send)], axis=1)
    query = both[0]
    kv_own = gather_z(both[1:])
    kv_par = [swap_cores(p) for p in kv_own]
    wso_own = after(wso_own, kv_own[2])
    wso_par = swap_cores(wso_own)
    state = attention_part((0,), False, [], where, span_order, query, kv_own[:1], kv_par[:1])
    near = (1, 2, 7, 8)
    state = attention_part(
        (1, 2, 6, 7), False, state, where, span_order, query, [kv_own[i] for i in near], [kv_par[i] for i in near]
    )
    att_own, att_send = attention_part(
        (3, 4, 5), True, state, where, span_order, query, kv_own[3:7], kv_par[3:7]
    )
    att_far = swap_xh(att_send)
    return call(
        self_out_kernel,
        jax.ShapeDtypeStruct((rows, 512), bf16),
        [SMEM] + [VMEM] * 19,
        [vmem((2048, 512), bf16)],
        600_000_000,
        4_000_000,
    )(where, mid_share, wso_own, wso_par, *gather_group_small(att_own), *gather_group_small(att_far))


def solution(mesh):
    fine = Mesh(mesh.devices.reshape(2, 8, 2, 4, 2), ALL)
    in_specs = (
        P(CTX, None),
        P(),
        P(CTX, GROUP),
        P(GROUP, CTX),
        P(CTX, None, GROUP),
        P(GROUP, CTX),
        P(CTX, "y", None, None, None, "xl"),
        P(CTX),
        P(CTX, None),
        P(),
    )
    return jax.shard_map(
        per_device, mesh=fine, in_specs=in_specs, out_specs=P(CTX, GROUP), check_vma=False
    )
```

```python
import functools
import math

import jax
import jax.numpy as jnp
from jax import lax
from jax.experimental import pallas as pl
from jax.experimental.pallas import tpu as pltpu
from jax.sharding import Mesh
from jax.sharding import PartitionSpec as P

HD = 128
SPAN = 64
epsilon = 1e-05
far_below = -1e30
NZ = 8

VMEM = pl.BlockSpec(memory_space=pltpu.VMEM)
SMEM = pl.BlockSpec(memory_space=pltpu.SMEM)
ANY = pl.BlockSpec(memory_space=pl.ANY)
f32 = jnp.float32
bf16 = jnp.bfloat16

CTX = ("xh", "z", "core")
GROUP = ("y", "xl")
ALL = CTX + GROUP


def dot(a, b):
    return jnp.dot(a, b, preferred_element_type=f32)


def dot_t(a, b):
    return lax.dot_general(a, b, (((1,), (1,)), ((), ())), preferred_element_type=f32)


def call(kernel, out_shape, in_specs, out_specs, scratch, flops, nbytes):
    return pl.pallas_call(
        kernel,
        out_shape=out_shape,
        in_specs=in_specs,
        out_specs=out_specs,
        scratch_shapes=scratch,
        compiler_params=pltpu.CompilerParams(vmem_limit_bytes=24 * 1024 * 1024),
        cost_estimate=pl.CostEstimate(flops=flops, bytes_accessed=nbytes, transcendentals=0),
    )


def sds(shape, dtype=bf16):
    return jax.ShapeDtypeStruct(shape, dtype)


def after(x, *earlier):
    return lax.optimization_barrier((x,) + earlier)[0]


def shift(x, axis, by, size):
    return lax.ppermute(x, axis, [(i, (i + by) % size) for i in range(size)])


def swap_cores(x):
    return shift(x, "core", 1, 2)


def swap_xh(x):
    return shift(x, "xh", 1, 2)


def ring(x, between):
    cut = x.shape[0] // 2
    r1, l1 = shift(x, "z", 1, NZ), shift(x, "z", -1, NZ)
    r2, l2 = shift(r1, "z", 1, NZ), shift(l1, "z", -1, NZ)
    r2, l2, _ = lax.optimization_barrier((r2, l2, between))
    r3, l3 = shift(r2, "z", 1, NZ), shift(l2, "z", -1, NZ)
    r4, l4 = shift(r3[:cut], "z", 1, NZ), shift(l3[cut:], "z", -1, NZ)
    return jnp.concatenate([x, l1, l2, l3, r4, l4, r3, r2, r1], axis=0)


def block_of(where, zz, other, side):
    return (where[0] ^ side) * 16 + zz * 2 + (where[2] ^ other)


class Copies:
    def __init__(self, sems):
        self.sems = sems
        self.used = 0

    def start(self, source, target):
        copy = pltpu.make_async_copy(source, target, self.sems.at[self.used])
        self.used += 1
        copy.start()
        return copy


def cross_kernel(
    where, source, count, gain, hidden_in, own_in, par_in, nbr0, nbr1, nbr2, nbr3, out,
    normed, hidden, weights, nbr, mixed_all, sems,
):
    copies = Copies(sems)
    hidden_copy = copies.start(hidden_in, hidden)
    weight_copies = [copies.start(own_in, weights.at[0]), copies.start(par_in, weights.at[1])]
    y = where[3]
    nbr_copies = [copies.start(nbr0.at[y], nbr.at[y])]
    for k, ref in ((1, nbr1), (2, nbr2), (3, nbr3)):
        nbr_copies.append(copies.start(ref, nbr.at[lax.rem(y + 4 - k, 4)]))
    hidden_copy.wait()
    values = hidden[...].astype(f32)
    row_scale = lax.rsqrt(jnp.mean(values * values, axis=1, keepdims=True) + epsilon)
    for b in range(32):
        cols = slice(b * 128, (b + 1) * 128)
        block = hidden[:, cols].astype(f32)
        normed[:, cols] = (block * row_scale * gain[b : b + 1, :]).astype(bf16)
    for copy in weight_copies + nbr_copies:
        copy.wait()
    acc = jnp.zeros((hidden.shape[0], 256), f32)
    for first in range(0, 16, 2):
        for other in range(2):
            left, right = [], []
            for i in (first, first + 1):
                owner = i * 2 + (where[2] ^ other)
                left.append(normed[:, pl.ds(pl.multiple_of(owner * 128, 128), 128)])
                right.append(weights[other, i])
            acc += dot(jnp.concatenate(left, axis=1), jnp.concatenate(right, axis=0))
    query = acc.astype(bf16)
    scale = 1.0 / math.sqrt(HD)
    lanes = lax.broadcasted_iota(jnp.int32, (SPAN, 128), 1)
    chosen = [source[i] for i in range(8)]
    for s in range(4):
        slots = []
        for j in range(2):
            i = s * 2 + j
            rank = jnp.int32(0)
            for k in range(s * 2):
                rank = rank + (chosen[k] == chosen[i]).astype(jnp.int32)
            slots.append((chosen[i], rank))
        alive = lanes < count[s] * 64
        for h in range(2):
            kcols = slice(2 * h * HD, (2 * h + 1) * HD)
            vcols = slice((2 * h + 1) * HD, (2 * h + 2) * HD)
            keys = jnp.concatenate([nbr[e, r, :, kcols] for e, r in slots], axis=0)
            vals = jnp.concatenate([nbr[e, r, :, vcols] for e, r in slots], axis=0)
            part = query[s * SPAN : (s + 1) * SPAN, h * HD : (h + 1) * HD]
            scores = jnp.where(alive, dot_t(part, keys) * scale, far_below)
            top = jnp.max(scores, axis=1, keepdims=True)
            exps = jnp.exp(scores - top)
            total = jnp.sum(exps, axis=1, keepdims=True)
            mixed = dot(exps.astype(bf16), vals) / total
            mixed_all[s * SPAN : (s + 1) * SPAN, h * HD : (h + 1) * HD] = mixed.astype(bf16)
    out_copies = [copies.start(mixed_all, out.at[i]) for i in range(8)]
    for copy in out_copies:
        copy.wait()


def fetch_out_weights(copies, where, own, par, which, weights):
    started = []
    for distance in range(NZ):
        zz = lax.rem(where[1] + distance, NZ)
        for other in range(2):
            for side in range(2):
                first = (where[2] ^ other) * 1024 + (zz * 2 + (where[0] ^ side)) * 64
                place = weights.at[pl.ds(pl.multiple_of(first, 64), 64)]
                started.append(copies.start((own, par)[other].at[distance * 4 + side * 2 + which], place))
    return started


def cross_out_kernel(where, share, att_in, own, par, mid, spread, weights, att, total, sems):
    copies = Copies(sems)
    started = fetch_out_weights(copies, where, own, par, 0, weights)
    started.append(copies.start(att_in, att))
    for copy in started:
        copy.wait()
    acc = share[...].astype(f32)
    for g in range(8):
        acc += dot(att[g], weights[g * 256 : (g + 1) * 256, :])
    total[...] = acc.astype(bf16)
    out_copies = [copies.start(total, spread.at[i]) for i in range(8)]
    mid[...] = total[...]
    for copy in out_copies:
        copy.wait()


def qkv_kernel(where, gain, mids_in, own_in, par_in, keep, send, normed, proj, mids, weights, sems):
    copies = Copies(sems)
    mids_copy = copies.start(mids_in, mids)
    weight_copies = [copies.start(own_in, weights.at[0]), copies.start(par_in, weights.at[1])]
    xh = where[0]
    rows = mids.shape[1]
    mids_copy.wait()
    squares = jnp.zeros((rows, 512), f32)
    for g in range(8):
        values = mids[g].astype(f32)
        squares += values * values
    row_scale = lax.rsqrt(jnp.sum(squares, axis=1, keepdims=True) * (1.0 / 4096) + epsilon)
    for b in range(32):
        block = mids[b // 4, :, b % 4 * 128 : (b % 4 + 1) * 128].astype(f32)
        normed[:, b * 128 : (b + 1) * 128] = (block * row_scale * gain[b : b + 1, :]).astype(bf16)
    for copy in weight_copies:
        copy.wait()
    for t in range(3):
        acc = jnp.zeros((rows, 256), f32)
        for distance in range(NZ):
            zz = lax.rem(where[1] + distance, NZ)
            for other in range(2):
                left, right = [], []
                for side in range(2):
                    owner = block_of(where, zz, other, side)
                    left.append(normed[:, pl.ds(pl.multiple_of(owner * 128, 128), 128)])
                    right.append(weights[other, distance * 6 + side * 3 + t])
                acc += dot(jnp.concatenate(left, axis=1), jnp.concatenate(right, axis=0))
        if t == 0:
            acc = acc * (math.log2(math.e) / math.sqrt(HD))
        proj[...] = acc.astype(bf16)
        keep[t] = proj[:, pl.ds(pl.multiple_of(xh * 128, 128), 128)]
        send[t] = proj[:, pl.ds(pl.multiple_of((1 - xh) * 128, 128), 128)]


def attention_kernel(distances, where, order, *rest):
    first, last = distances[0] == 0, distances[0] == 4
    queries, rest = rest[:2], rest[2:]
    if not first:
        state_in, rest = rest[:2], rest[2:]
    pieces, state_out, (kv, sems) = rest[:-4], rest[-4:-2], rest[-2:]
    copies = Copies(sems)
    started = []
    if last:
        started = [[copies.start(piece, kv.at[0, pl.ds(i, 1)]) for i, piece in enumerate(pieces)]]
    else:
        started = [[copies.start(piece, kv.at[i])] for i, piece in enumerate(pieces)]
    n = queries[0].shape[0]
    rows = lax.broadcasted_iota(jnp.int32, (SPAN, 1), 0)
    lanes = lax.broadcasted_iota(jnp.int32, (1, 256), 1)
    span_of, within = lanes // SPAN, lanes % SPAN
    k_places = []
    for distance in distances:
        zz = lax.rem(where[1] + distance, NZ)
        places = []
        for side in range(2):
            c = block_of(where, zz, 0, side)
            place = jnp.zeros((1, 256), jnp.int32)
            for s in range(4):
                place = jnp.where(span_of == s, order[c * 4 + s], place)
            places.append(place * SPAN + within)
        k_places.append(jnp.concatenate(places, axis=1))
    for i, group in enumerate(started):
        for copy in group:
            copy.wait()
    for core in range(2):
        q_places = []
        for side in range(2):
            c = block_of(where, where[1], core, side)
            for s in range(4):
                q_places.append(order[c * 4 + s] * SPAN + rows)
        q_places = jnp.concatenate(q_places, axis=0)
        if first:
            top = jnp.full((n, 1), far_below, f32)
            total = jnp.zeros((n, 1), f32)
            mixed = jnp.zeros((n, HD), f32)
        else:
            mixed = state_in[core][:, :HD]
            top = state_in[core][:, HD : HD + 1]
            total = state_in[core][:, 192:193]
        for i in range(len(distances)):
            scores = dot_t(queries[core][...], kv[i, 0])
            scores = jnp.where(k_places[i] <= q_places, scores, far_below)
            new_top = jnp.maximum(top, jnp.max(scores, axis=1, keepdims=True))
            exps = jnp.exp2(scores - new_top)
            fade = jnp.exp2(top - new_top)
            total = total * fade + jnp.sum(exps, axis=1, keepdims=True)
            mixed = mixed * fade + dot(exps.astype(bf16), kv[i, 1])
            top = new_top
        state_out[core][:, :HD] = mixed
        right = lax.broadcasted_iota(jnp.int32, (n, HD), 1)
        state_out[core][:, HD:] = jnp.where(right < 64, top, total)


def attention_part(distances, where, order, queries, state, pieces):
    n = queries[0].shape[0]
    return call(
        functools.partial(attention_kernel, distances),
        [sds((n, 2 * HD), f32)] * 2,
        [SMEM] * 2 + [VMEM] * (2 + len(state)) + [ANY] * len(pieces),
        [VMEM] * 2,
        [pltpu.VMEM((len(distances), 2, n, HD), bf16), pltpu.SemaphoreType.DMA((len(pieces),))],
        280_000_000 * len(distances),
        500_000 * len(distances),
    )(where, order, *queries, *state, *pieces)


def merge_kernel(where, own, par, out, halves, sems):
    top = jnp.maximum(own[:, HD : HD + 1], par[:, HD : HD + 1])
    fade_own, fade_par = (jnp.exp2(x[:, HD : HD + 1] - top) for x in (own, par))
    total = own[:, 192:193] * fade_own + par[:, 192:193] * fade_par
    mixed = (own[:, :HD] * fade_own + par[:, :HD] * fade_par) / total
    copies = Copies(sems)
    started = []
    n = halves.shape[1]
    for side in range(2):
        halves[side] = mixed[side * n : (side + 1) * n].astype(bf16)
        for g in range(8):
            started.append(copies.start(halves.at[side], out.at[(where[0] ^ side) * 8 + g]))
    for copy in started:
        copy.wait()


def self_out_kernel(where, share, att_in, own, par, out, weights, att, sems):
    copies = Copies(sems)
    started = fetch_out_weights(copies, where, own, par, 1, weights)
    started.append(copies.start(att_in, att))
    for copy in started:
        copy.wait()
    acc = share[...].astype(f32)
    for g in range(8):
        both = jnp.concatenate([att[g], att[8 + g]], axis=1)
        acc += dot(both, weights[g * 256 : (g + 1) * 256, :])
    out[...] = acc.astype(bf16)


def deal_out_weights(blocks, c):
    n = blocks.shape[0]
    quarters = blocks.reshape(n, 4, 64, 128)
    turn = c % 4
    arrived = []
    for i in range(4):
        pairs = []
        for source_c in range(32):
            for source_g in range(8):
                r = source_g * 4 + (i + source_c) % 4
                target_c = (r % 2) * 16 + ((r % 16) // 2) * 2 + r // 16
                pairs.append((source_c * 8 + source_g, target_c * 8 + source_c // 4))
        piece = lax.dynamic_index_in_dim(quarters, (i + turn) % 4, 1, keepdims=False)
        arrived.append(lax.ppermute(piece, ALL, pairs))
    r = (c % 2) * 16 + ((c // 2) % 8) * 2 + c // 16
    stacked = jnp.stack(arrived)
    columns = [lax.dynamic_index_in_dim(stacked, (r - q) % 4, 0, keepdims=False) for q in range(4)]
    return jnp.concatenate(columns, axis=2)


def per_device(
    hidden_in,
    norm_gains,
    w_cross_query,
    w_cross_out,
    w_self_qkv,
    w_self_out,
    nbr_kv,
    nbr_count,
    nbr_source,
    span_order,
):
    rows, width = hidden_in.shape
    c = lax.axis_index(CTX)
    g = lax.axis_index(GROUP)
    where = jnp.stack([lax.axis_index(a) for a in ALL]).astype(jnp.int32)
    gains = norm_gains.reshape(2, 32, 128)
    vmem = pltpu.VMEM

    sem = pltpu.SemaphoreType.DMA
    y = lax.axis_index("y")

    wq_own = lax.all_to_all(
        jnp.broadcast_to(w_cross_query[None], (16,) + w_cross_query.shape), ("xh", "z"), 0, 0, tiled=True
    )
    nbr = nbr_kv[0, 0]
    nbr_got = [
        shift(lax.dynamic_index_in_dim(nbr, (y + k) % 4, 0, keepdims=False), "y", k, 4) for k in (1, 2, 3)
    ]
    qkv_own = w_self_qkv.transpose(1, 0, 2)
    late = jnp.concatenate([qkv_own, swap_xh(qkv_own)], axis=0)
    dealt = deal_out_weights(jnp.stack([w_cross_out, w_self_out]), c)
    dealt = jnp.concatenate([dealt, swap_xh(dealt)], axis=0)

    wq_par = swap_cores(wq_own)
    cross_att = call(
        cross_kernel,
        sds((8, rows, 256)),
        [SMEM] * 3 + [VMEM] + [ANY] * 7,
        ANY,
        [
            vmem((rows, width), bf16),
            vmem((rows, width), bf16),
            vmem((2, 16, 128, 256), bf16),
            vmem((4, 3, 64, 512), bf16),
            vmem((rows, 256), bf16),
            sem((15,)),
        ],
        600_000_000,
        5_000_000,
    )(where, nbr_source.reshape(-1), nbr_count, gains[0], hidden_in, wq_own, wq_par, nbr, *nbr_got)

    wo_own = ring(dealt, cross_att)
    late_own = ring(late, cross_att)
    wo_par = swap_cores(wo_own)
    att_all = lax.all_to_all(cross_att, GROUP, 0, 0, tiled=True)
    hidden_share = lax.dynamic_slice_in_dim(hidden_in, g * 512, 512, 1)
    mid_share, spread = call(
        cross_out_kernel,
        [sds((rows, 512)), sds((8, rows, 512))],
        [SMEM, VMEM] + [ANY] * 3,
        [VMEM, ANY],
        [vmem((2048, 512), bf16), vmem((8, rows, 256), bf16), vmem((rows, 512), bf16), sem((41,))],
        600_000_000,
        4_000_000,
    )(where, hidden_share, att_all, wo_own, wo_par)

    late_own = after(late_own, spread)
    late_par = swap_cores(late_own)
    mids = lax.all_to_all(spread, GROUP, 0, 0, tiled=True)
    keep, send = call(
        qkv_kernel,
        [sds((3, rows, HD))] * 2,
        [SMEM, VMEM] + [ANY] * 3,
        [VMEM] * 2,
        [
            vmem((rows, width), bf16),
            vmem((rows, 256), bf16),
            vmem((8, rows, 512), bf16),
            vmem((2, 48, 128, 256), bf16),
            sem((3,)),
        ],
        1_600_000_000,
        11_000_000,
    )(where, gains[1], mids, late_own, late_par)

    both = jnp.concatenate([keep, swap_xh(send)], axis=1)
    kv = both[1:]
    queries = [both[0], swap_cores(both[0])]
    part = functools.partial(attention_part, where=where, order=span_order, queries=queries)
    r1, l1 = shift(kv, "z", 1, NZ), shift(kv, "z", -1, NZ)
    state = part((0,), state=[], pieces=[kv])
    r2, l2 = shift(r1, "z", 1, NZ), shift(l1, "z", -1, NZ)
    r2, l2, state = lax.optimization_barrier((r2, l2, state))
    r3, l3 = shift(r2, "z", 1, NZ), shift(l2, "z", -1, NZ)
    state = part((1, 7), state=state, pieces=[l1, r1])
    r3, l3, state = lax.optimization_barrier((r3, l3, state))
    r4, l4 = shift(r3[:1], "z", 1, NZ), shift(l3[1:], "z", -1, NZ)
    state = part((2, 6, 3, 5), state=state, pieces=[l2, r2, l3, r3])
    r4, l4, state = lax.optimization_barrier((r4, l4, state))
    state = part((4,), state=state, pieces=[r4, l4])
    heads = call(
        merge_kernel,
        sds((16, rows, HD)),
        [SMEM, VMEM, VMEM],
        ANY,
        [vmem((2, rows, HD), bf16), sem((16,))],
        1_000_000,
        2_000_000,
    )(where, state[0], swap_cores(state[1]))
    self_all = lax.all_to_all(heads, ("xh",) + GROUP, 0, 0, tiled=True)
    return call(
        self_out_kernel,
        sds((rows, 512)),
        [SMEM, VMEM] + [ANY] * 3,
        VMEM,
        [vmem((2048, 512), bf16), vmem((16, rows, HD), bf16), sem((33,))],
        600_000_000,
        4_000_000,
    )(where, mid_share, self_all, wo_own, wo_par)


def solution(mesh):
    fine = Mesh(mesh.devices.reshape(2, 8, 2, 4, 2), ALL)
    in_specs = (
        P(CTX, None),
        P(),
        P(CTX, GROUP),
        P(GROUP, CTX),
        P(CTX, None, GROUP),
        P(GROUP, CTX),
        P(CTX, "y", None, None, None, "xl"),
        P(CTX),
        P(CTX, None),
        P(),
    )
    return jax.shard_map(
        per_device, mesh=fine, in_specs=in_specs, out_specs=P(CTX, GROUP), check_vma=False
    )
```

```python
import functools
import math

import jax
import jax.numpy as jnp
from jax import lax
from jax.experimental import pallas as pl
from jax.experimental.pallas import tpu as pltpu
from jax.sharding import Mesh
from jax.sharding import PartitionSpec as P

HD = 128
SPAN = 64
epsilon = 1e-05
far_below = -1e30
NZ = 8

VMEM = pl.BlockSpec(memory_space=pltpu.VMEM)
SMEM = pl.BlockSpec(memory_space=pltpu.SMEM)
ANY = pl.BlockSpec(memory_space=pl.ANY)
f32 = jnp.float32
bf16 = jnp.bfloat16

Z = ("zh", "zl")
CTX = ("xh",) + Z + ("core",)
GROUP = ("y", "xl")
ALL = CTX + GROUP


def dot(a, b):
    return jnp.dot(a, b, preferred_element_type=f32)


def dot_t(a, b):
    return lax.dot_general(a, b, (((1,), (1,)), ((), ())), preferred_element_type=f32)


def call(kernel, out_shape, in_specs, out_specs, scratch, flops, nbytes):
    return pl.pallas_call(
        kernel,
        out_shape=out_shape,
        in_specs=in_specs,
        out_specs=out_specs,
        scratch_shapes=scratch,
        compiler_params=pltpu.CompilerParams(vmem_limit_bytes=16 * 1024 * 1024),
        cost_estimate=pl.CostEstimate(flops=flops, bytes_accessed=nbytes, transcendentals=0),
    )


def sds(shape, dtype=bf16):
    return jax.ShapeDtypeStruct(shape, dtype)


def after(x, *earlier):
    return lax.optimization_barrier((x,) + earlier)[0]


def shift(x, axis, by, size):
    return lax.ppermute(x, axis, [(i, (i + by) % size) for i in range(size)])


def swap_cores(x):
    return shift(x, "core", 1, 2)


def swap_xh(x):
    return shift(x, "xh", 1, 2)


def ring_start(x):
    return x, shift(x, Z, 1, NZ), shift(x, Z, -1, NZ)


def ring(start, third):
    x, r1, l1 = start
    cut = x.shape[0] // 2
    r2, l2 = shift(r1, Z, 1, NZ), shift(l1, Z, -1, NZ)
    r2, l2, _ = lax.optimization_barrier((r2, l2, third))
    r3, l3 = shift(r2, Z, 1, NZ), shift(l2, Z, -1, NZ)
    r4, l4 = shift(r3[:cut], Z, 1, NZ), shift(l3[cut:], Z, -1, NZ)
    return [x, l1, l2, l3, r4, l4, r3, r2, r1]


def block_at(pieces, distance, i):
    if distance == 4:
        cut = pieces[4].shape[0]
        return pieces[4 + i // cut][i % cut]
    return pieces[distance if distance < 4 else distance + 1][i]


def block_of(where, zz, other, side):
    return (where[0] ^ side) * 16 + zz * 2 + (where[2] ^ other)


def spread_out(source, targets, sems):
    copies = [pltpu.make_async_copy(source, target, sems.at[i]) for i, target in enumerate(targets)]
    for copy in copies:
        copy.start()
    for copy in copies:
        copy.wait()


def cross_kernel(
    where, source, count, gain, hidden, own, par, nbr0, nbr1, nbr2, nbr3, out, normed, nbr, mixed_all, sems
):
    y = where[3]
    nbr[y] = nbr0[y]
    for k, ref in ((1, nbr1), (2, nbr2), (3, nbr3)):
        nbr[lax.rem(y + 4 - k, 4)] = ref[...]
    values = hidden[...].astype(f32)
    row_scale = lax.rsqrt(jnp.mean(values * values, axis=1, keepdims=True) + epsilon)
    for b in range(32):
        cols = slice(b * 128, (b + 1) * 128)
        block = hidden[:, cols].astype(f32)
        normed[:, cols] = (block * row_scale * gain[b : b + 1, :]).astype(bf16)
    acc = jnp.zeros((hidden.shape[0], 256), f32)
    for first in range(0, 16, 2):
        for other in range(2):
            left, right = [], []
            for i in (first, first + 1):
                owner = i * 2 + (where[2] ^ other)
                left.append(normed[:, pl.ds(pl.multiple_of(owner * 128, 128), 128)])
                right.append((own, par)[other][i])
            acc += dot(jnp.concatenate(left, axis=1), jnp.concatenate(right, axis=0))
    query = acc.astype(bf16)
    scale = 1.0 / math.sqrt(HD)
    lanes = lax.broadcasted_iota(jnp.int32, (SPAN, 128), 1)
    chosen = [source[i] for i in range(8)]
    for s in range(4):
        slots = []
        for j in range(2):
            i = s * 2 + j
            rank = jnp.int32(0)
            for k in range(s * 2):
                rank = rank + (chosen[k] == chosen[i]).astype(jnp.int32)
            slots.append((chosen[i], rank))
        alive = lanes < count[s] * 64
        for h in range(2):
            kcols = slice(2 * h * HD, (2 * h + 1) * HD)
            vcols = slice((2 * h + 1) * HD, (2 * h + 2) * HD)
            keys = jnp.concatenate([nbr[e, r, :, kcols] for e, r in slots], axis=0)
            vals = jnp.concatenate([nbr[e, r, :, vcols] for e, r in slots], axis=0)
            part = query[s * SPAN : (s + 1) * SPAN, h * HD : (h + 1) * HD]
            scores = jnp.where(alive, dot_t(part, keys) * scale, far_below)
            top = jnp.max(scores, axis=1, keepdims=True)
            exps = jnp.exp(scores - top)
            total = jnp.sum(exps, axis=1, keepdims=True)
            mixed = dot(exps.astype(bf16), vals) / total
            mixed_all[s * SPAN : (s + 1) * SPAN, h * HD : (h + 1) * HD] = mixed.astype(bf16)
    spread_out(mixed_all, [out.at[i] for i in range(8)], sems)


def weight_rows(where, distance, other, side):
    zz = lax.rem(where[1] + distance, NZ)
    return pl.ds(pl.multiple_of(block_of(where, zz, other, side) * 64, 64), 64)


def cross_out_kernel(where, share, att, *rest):
    pieces, (mid, spread, weights, total, sems) = (rest[:9], rest[9:18]), rest[18:]
    for distance in range(NZ):
        for other in range(2):
            for side in range(2):
                rows = weight_rows(where, distance, other, side)
                weights[rows, :] = block_at(pieces[other], distance, side)
    acc = share[...].astype(f32)
    for g in range(8):
        acc += dot(att[g], weights[g * 256 : (g + 1) * 256, :])
    total[...] = acc.astype(bf16)
    mid[...] = total[...]
    spread_out(total, [spread.at[i] for i in range(8)], sems)


def qkv_kernel(where, gain, mids, *rest):
    pieces, (keep, send, normed, proj) = (rest[:9], rest[9:18]), rest[18:]
    xh = where[0]
    rows = mids.shape[1]
    squares = jnp.zeros((rows, 512), f32)
    for g in range(8):
        values = mids[g].astype(f32)
        squares += values * values
    row_scale = lax.rsqrt(jnp.sum(squares, axis=1, keepdims=True) * (1.0 / 4096) + epsilon)
    for b in range(32):
        block = mids[b // 4, :, b % 4 * 128 : (b % 4 + 1) * 128].astype(f32)
        normed[:, b * 128 : (b + 1) * 128] = (block * row_scale * gain[b : b + 1, :]).astype(bf16)
    for t in range(3):
        acc = jnp.zeros((rows, 256), f32)
        for distance in range(NZ):
            zz = lax.rem(where[1] + distance, NZ)
            for other in range(2):
                left, right = [], []
                for side in range(2):
                    owner = block_of(where, zz, other, side)
                    left.append(normed[:, pl.ds(pl.multiple_of(owner * 128, 128), 128)])
                    right.append(block_at(pieces[other], distance, side * 4 + t))
                acc += dot(jnp.concatenate(left, axis=1), jnp.concatenate(right, axis=0))
        if t == 0:
            acc = acc * (math.log2(math.e) / math.sqrt(HD))
        proj[...] = acc.astype(bf16)
        keep[t] = proj[:, pl.ds(pl.multiple_of(xh * 128, 128), 128)]
        send[t] = proj[:, pl.ds(pl.multiple_of((1 - xh) * 128, 128), 128)]


def arrange_kernel(where, *rest):
    pieces, out = (rest[:9], rest[9:18]), rest[18]
    for distance in range(NZ):
        for other in range(2):
            for side in range(2):
                rows = weight_rows(where, distance, other, side)
                block = block_at(pieces[other], distance, side * 4 + 3)
                out[rows, :256] = block[:64]
                out[rows, 256:] = block[64:]


def attention_kernel(distances, where, order, query, *rest):
    first, last = distances[0] == 0, distances[0] == 4
    if not first:
        state_in, rest = rest[0], rest[1:]
    pieces, (state_out, k_places, q_places) = rest[:-3], rest[-3:]
    n = query.shape[1]
    rows = lax.broadcasted_iota(jnp.int32, (SPAN, 1), 0)
    lanes = lax.broadcasted_iota(jnp.int32, (1, 256), 1)
    right = lax.broadcasted_iota(jnp.int32, (n, HD), 1)
    span_of, within = lanes // SPAN, lanes % SPAN
    for i, distance in enumerate(distances):
        for side in range(2):
            c = block_of(where, lax.rem(where[1] + distance, NZ), 0, side)
            place = jnp.zeros((1, 256), jnp.int32)
            for s in range(4):
                place = jnp.where(span_of == s, order[c * 4 + s], place)
            k_places[i : i + 1, side * 256 : (side + 1) * 256] = place * SPAN + within
    for core in range(2):
        for side in range(2):
            c = block_of(where, where[1], core, side)
            for s in range(4):
                begin = (side * 4 + s) * SPAN
                q_places[core, begin : begin + SPAN, :] = order[c * 4 + s] * SPAN + rows

    def one_core(core, carry):
        if first:
            top = jnp.full((n, 1), far_below, f32)
            total = jnp.zeros((n, 1), f32)
            mixed = jnp.zeros((n, HD), f32)
        else:
            mixed = state_in[core, :, :HD]
            top = state_in[core, :, HD : HD + 1]
            total = state_in[core, :, 192:193]
        for i in range(len(distances)):
            keys, vals = (pieces[0][0], pieces[1][0]) if last else (pieces[i][0], pieces[i][1])
            scores = dot_t(query[core], keys)
            scores = jnp.where(k_places[i : i + 1, :] <= q_places[core], scores, far_below)
            new_top = jnp.maximum(top, jnp.max(scores, axis=1, keepdims=True))
            exps = jnp.exp2(scores - new_top)
            fade = jnp.exp2(top - new_top)
            total = total * fade + jnp.sum(exps, axis=1, keepdims=True)
            mixed = mixed * fade + dot(exps.astype(bf16), vals)
            top = new_top
        state_out[core, :, :HD] = mixed
        state_out[core, :, HD:] = jnp.where(right < 64, top, total)
        return carry

    lax.fori_loop(0, 2, one_core, 0)


def attention_part(distances, where, order, query, state, pieces):
    n = query.shape[1]
    return call(
        functools.partial(attention_kernel, distances),
        sds((2, n, 2 * HD), f32),
        [SMEM] * 2 + [VMEM] * (1 + len(state) + len(pieces)),
        VMEM,
        [pltpu.VMEM((8, n), jnp.int32), pltpu.VMEM((2, n, 1), jnp.int32)],
        280_000_000 * len(distances),
        500_000 * len(distances),
    )(where, order, query, *state, *pieces)


def merge_kernel(where, own, par, out, halves, sems):
    top = jnp.maximum(own[:, HD : HD + 1], par[:, HD : HD + 1])
    fade_own, fade_par = (jnp.exp2(x[:, HD : HD + 1] - top) for x in (own, par))
    total = own[:, 192:193] * fade_own + par[:, 192:193] * fade_par
    mixed = (own[:, :HD] * fade_own + par[:, :HD] * fade_par) / total
    n = halves.shape[1]
    for side in range(2):
        halves[side] = mixed[side * n : (side + 1) * n].astype(bf16)
    copies = []
    for side in range(2):
        for g in range(8):
            target = out.at[(where[0] ^ side) * 8 + g]
            copies.append(pltpu.make_async_copy(halves.at[side], target, sems.at[len(copies)]))
            copies[-1].start()
    for copy in copies:
        copy.wait()


def self_out_kernel(where, share, att, weights, out):
    acc = share[...].astype(f32)
    for g in range(8):
        both = jnp.concatenate([att[g], att[8 + g]], axis=1)
        acc += dot(both, weights[g * 256 : (g + 1) * 256, :])
    out[...] = acc.astype(bf16)


def deal_out_weights(blocks):
    n = blocks.shape[0]
    quarters = blocks.reshape(n, 4, 64, 128)
    near = lax.axis_index(("zl", "core"))
    got = [lax.dynamic_index_in_dim(quarters, near, 1, keepdims=False)]
    for m in (1, 2, 3):
        piece = lax.dynamic_index_in_dim(quarters, near ^ m, 1, keepdims=False)
        got.append(lax.ppermute(piece, ("zl", "core"), [(i, i ^ m) for i in range(4)]))
    got = jnp.stack(got)
    columns = [lax.dynamic_index_in_dim(got, near ^ q, 0, keepdims=False) for q in range(4)]
    pairs = [
        ((share * 4 + i) * 8 + group, (group * 4 + i) * 8 + share)
        for share in range(8)
        for i in range(4)
        for group in range(8)
    ]
    return lax.ppermute(jnp.concatenate(columns, axis=2), ALL, pairs)


def per_device(
    hidden_in,
    norm_gains,
    w_cross_query,
    w_cross_out,
    w_self_qkv,
    w_self_out,
    nbr_kv,
    nbr_count,
    nbr_source,
    span_order,
):
    rows, width = hidden_in.shape
    g = lax.axis_index(GROUP)
    y = lax.axis_index("y")
    where = jnp.stack([lax.axis_index(a) for a in ("xh", Z, "core", "y", "xl")]).astype(jnp.int32)
    gains = norm_gains.reshape(2, 32, 128)
    vmem = pltpu.VMEM
    sem = pltpu.SemaphoreType.DMA

    wq_own = lax.all_to_all(
        jnp.broadcast_to(w_cross_query[None], (16,) + w_cross_query.shape), ("xh",) + Z, 0, 0, tiled=True
    )
    dealt = deal_out_weights(jnp.stack([w_cross_out, w_self_out]))
    nbr = nbr_kv[0, 0]
    nbr_got = [
        shift(lax.dynamic_index_in_dim(nbr, (y + k) % 4, 0, keepdims=False), "y", k, 4) for k in (1, 2, 3)
    ]
    qkv_own = after(w_self_qkv.transpose(1, 0, 2), dealt)
    dealt_other, qkv_other = swap_xh(dealt), swap_xh(qkv_own)

    wo_start = ring_start(jnp.stack([dealt[0], dealt_other[0]]))
    wq_par = swap_cores(wq_own)
    wq_own, wq_par, wo_start = lax.optimization_barrier((wq_own, wq_par, wo_start))
    cross_att = call(
        cross_kernel,
        sds((8, rows, 256)),
        [SMEM] * 3 + [VMEM] * 8,
        ANY,
        [vmem((rows, width), bf16), vmem((4, 3, 64, 512), bf16), vmem((rows, 256), bf16), sem((8,))],
        600_000_000,
        5_000_000,
    )(where, nbr_source.reshape(-1), nbr_count, gains[0], hidden_in, wq_own, wq_par, nbr, *nbr_got)

    wo_own = ring(wo_start, cross_att)
    wo_par = [swap_cores(p) for p in wo_own]
    att_all = lax.all_to_all(cross_att, GROUP, 0, 0, tiled=True)

    def halves(x):
        return jnp.concatenate([x[:, :256], x[:, 256:]], axis=0)[None]

    late = jnp.concatenate([qkv_own, halves(dealt[1]), qkv_other, halves(dealt_other[1])], axis=0)
    late_own = ring(ring_start(after(late, cross_att)), att_all)
    hidden_share = lax.dynamic_slice_in_dim(hidden_in, g * 512, 512, 1)
    mid_share, spread = call(
        cross_out_kernel,
        [sds((rows, 512)), sds((8, rows, 512))],
        [SMEM] + [VMEM] * 20,
        [VMEM, ANY],
        [vmem((2048, 512), bf16), vmem((rows, 512), bf16), sem((8,))],
        600_000_000,
        4_000_000,
    )(where, hidden_share, att_all, *wo_own, *wo_par)

    mids = lax.all_to_all(spread, GROUP, 0, 0, tiled=True)
    late_par = [swap_cores(after(p, spread)) for p in late_own]
    keep, send = call(
        qkv_kernel,
        [sds((3, rows, HD))] * 2,
        [SMEM] + [VMEM] * 20,
        [VMEM] * 2,
        [vmem((rows, width), bf16), vmem((rows, 256), bf16)],
        1_600_000_000,
        11_000_000,
    )(where, gains[1], mids, *late_own, *late_par)

    both = jnp.concatenate([keep, swap_xh(send)], axis=1)
    kv = both[1:]
    query = jnp.stack([both[0], swap_cores(both[0])])
    part = functools.partial(attention_part, where=where, order=span_order, query=query)
    r1, l1 = shift(kv, Z, 1, NZ), shift(kv, Z, -1, NZ)
    state = part((0,), state=[], pieces=[kv])
    late_own, late_par, _ = lax.optimization_barrier((late_own, late_par, state))
    weights = call(
        arrange_kernel,
        sds((2048, 512)),
        [SMEM] + [VMEM] * 18,
        VMEM,
        [],
        1_000_000,
        4_000_000,
    )(where, *late_own, *late_par)
    r2, l2 = shift(r1, Z, 1, NZ), shift(l1, Z, -1, NZ)
    r2, l2, state, weights = lax.optimization_barrier((r2, l2, state, weights))
    r3, l3 = shift(r2, Z, 1, NZ), shift(l2, Z, -1, NZ)
    state = part((1, 7), state=[state], pieces=[l1, r1])
    r3, l3, state = lax.optimization_barrier((r3, l3, state))
    r4, l4 = shift(r3[:1], Z, 1, NZ), shift(l3[1:], Z, -1, NZ)
    state = part((2, 6, 3, 5), state=[state], pieces=[l2, r2, l3, r3])
    r4, l4, state = lax.optimization_barrier((r4, l4, state))
    state = part((4,), state=[state], pieces=[r4, l4])
    heads = call(
        merge_kernel,
        sds((16, rows, HD)),
        [SMEM, VMEM, VMEM],
        ANY,
        [vmem((2, rows, HD), bf16), sem((16,))],
        1_000_000,
        2_000_000,
    )(where, state[0], swap_cores(state[1]))
    self_all = lax.all_to_all(heads, ("xh",) + GROUP, 0, 0, tiled=True)
    return call(
        self_out_kernel,
        sds((rows, 512)),
        [SMEM] + [VMEM] * 3,
        VMEM,
        [],
        600_000_000,
        4_000_000,
    )(where, mid_share, self_all, weights)


def solution(mesh):
    fine = Mesh(mesh.devices.reshape(2, 4, 2, 2, 4, 2), ALL)
    in_specs = (
        P(CTX, None),
        P(),
        P(CTX, GROUP),
        P(GROUP, CTX),
        P(CTX, None, GROUP),
        P(GROUP, CTX),
        P(CTX, "y", None, None, None, "xl"),
        P(CTX),
        P(CTX, None),
        P(),
    )
    return jax.shard_map(
        per_device, mesh=fine, in_specs=in_specs, out_specs=P(CTX, GROUP), check_vma=False
    )
```

```python
import functools
import math

import jax
import jax.numpy as jnp
from jax import lax
from jax.experimental import pallas as pl
from jax.experimental.pallas import tpu as pltpu
from jax.sharding import Mesh
from jax.sharding import PartitionSpec as P

HD = 128
SPAN = 64
epsilon = 1e-05
far_below = -1e30
NZ = 8

VMEM = pl.BlockSpec(memory_space=pltpu.VMEM)
SMEM = pl.BlockSpec(memory_space=pltpu.SMEM)
ANY = pl.BlockSpec(memory_space=pl.ANY)
f32 = jnp.float32
bf16 = jnp.bfloat16

Z = ("zh", "zl")
CTX = ("xh",) + Z + ("core",)
GROUP = ("y", "xl")
ALL = CTX + GROUP


def dot(a, b):
    return jnp.dot(a, b, preferred_element_type=f32)


def dot_t(a, b):
    return lax.dot_general(a, b, (((1,), (1,)), ((), ())), preferred_element_type=f32)


def call(kernel, out_shape, in_specs, out_specs, scratch, flops, nbytes):
    return pl.pallas_call(
        kernel,
        out_shape=out_shape,
        in_specs=in_specs,
        out_specs=out_specs,
        scratch_shapes=scratch,
        compiler_params=pltpu.CompilerParams(vmem_limit_bytes=24 * 1024 * 1024),
        cost_estimate=pl.CostEstimate(flops=flops, bytes_accessed=nbytes, transcendentals=0),
    )


def sds(shape, dtype=bf16):
    return jax.ShapeDtypeStruct(shape, dtype)


def after(x, *earlier):
    return lax.optimization_barrier((x,) + earlier)[0]


def shift(x, axis, by, size):
    return lax.ppermute(x, axis, [(i, (i + by) % size) for i in range(size)])


def swap_cores(x):
    return shift(x, "core", 1, 2)


def swap_xh(x):
    return shift(x, "xh", 1, 2)


def gather_z(x):
    r1, l1 = shift(x, Z, 1, NZ), shift(x, Z, -1, NZ)
    r2, l2 = shift(x, Z, 2, NZ), shift(x, Z, -2, NZ)
    r3, l3 = shift(r1, Z, 2, NZ), shift(l1, Z, -2, NZ)
    r4, l4 = shift(r2[:1], Z, 2, NZ), shift(l2[1:], Z, -2, NZ)
    return [x, l1, l2, l3, r4, l4, r3, r2, r1]


def half(pieces, distance, side):
    if distance == 4:
        return pieces[4 + side].at[0]
    return pieces[distance if distance < 4 else distance + 1].at[side]


def block_of(where, zz, other, side):
    return (where[0] ^ side) * 16 + zz * 2 + (where[2] ^ other)


class Copies:
    def __init__(self, sems):
        self.sems = sems
        self.used = 0

    def start(self, source, target):
        copy = pltpu.make_async_copy(source, target, self.sems.at[self.used])
        self.used += 1
        copy.start()
        return copy


def spread_out(copies, source, out):
    started = [copies.start(source, out.at[i]) for i in range(out.shape[0])]
    for copy in started:
        copy.wait()


def cross_kernel(where, source, count, gain, hidden_in, nbr0, nbr1, nbr2, nbr3, *rest):
    pieces = (rest[:9], rest[9:18])
    out, normed, hidden, weights, nbr, mixed_all, sems = rest[18:]
    copies = Copies(sems)
    y = where[3]
    hidden_copy = copies.start(hidden_in, hidden)
    started = []
    for distance in range(NZ):
        for other in range(2):
            for side in range(2):
                piece = half(pieces[other], distance, side)
                started.append(copies.start(piece, weights.at[other, distance, side]))
    started.append(copies.start(nbr0.at[y], nbr.at[y]))
    for k, ref in ((1, nbr1), (2, nbr2), (3, nbr3)):
        started.append(copies.start(ref, nbr.at[lax.rem(y + 4 - k, 4)]))
    hidden_copy.wait()
    values = hidden[...].astype(f32)
    row_scale = lax.rsqrt(jnp.mean(values * values, axis=1, keepdims=True) + epsilon)
    for b in range(32):
        cols = slice(b * 128, (b + 1) * 128)
        block = hidden[:, cols].astype(f32)
        normed[:, cols] = (block * row_scale * gain[b : b + 1, :]).astype(bf16)
    acc = jnp.zeros((hidden.shape[0], 256), f32)
    for copy in started:
        copy.wait()
    for distance in range(NZ):
        zz = lax.rem(where[1] + distance, NZ)
        for other in range(2):
            left, right = [], []
            for side in range(2):
                owner = block_of(where, zz, other, side)
                left.append(normed[:, pl.ds(pl.multiple_of(owner * 128, 128), 128)])
                right.append(weights[other, distance, side])
            acc += dot(jnp.concatenate(left, axis=1), jnp.concatenate(right, axis=0))
    query = acc.astype(bf16)
    scale = 1.0 / math.sqrt(HD)
    lanes = lax.broadcasted_iota(jnp.int32, (SPAN, 128), 1)
    chosen = [source[i] for i in range(8)]
    for s in range(4):
        slots = []
        for j in range(2):
            i = s * 2 + j
            rank = jnp.int32(0)
            for k in range(s * 2):
                rank = rank + (chosen[k] == chosen[i]).astype(jnp.int32)
            slots.append((chosen[i], rank))
        alive = lanes < count[s] * 64
        for h in range(2):
            kcols = slice(2 * h * HD, (2 * h + 1) * HD)
            vcols = slice((2 * h + 1) * HD, (2 * h + 2) * HD)
            keys = jnp.concatenate([nbr[e, r, :, kcols] for e, r in slots], axis=0)
            vals = jnp.concatenate([nbr[e, r, :, vcols] for e, r in slots], axis=0)
            part = query[s * SPAN : (s + 1) * SPAN, h * HD : (h + 1) * HD]
            scores = jnp.where(alive, dot_t(part, keys) * scale, far_below)
            top = jnp.max(scores, axis=1, keepdims=True)
            exps = jnp.exp(scores - top)
            total = jnp.sum(exps, axis=1, keepdims=True)
            mixed = dot(exps.astype(bf16), vals) / total
            mixed_all[s * SPAN : (s + 1) * SPAN, h * HD : (h + 1) * HD] = mixed.astype(bf16)
    spread_out(copies, mixed_all, out)


def weight_rows(where, zz, other, side):
    return pl.ds(pl.multiple_of(block_of(where, zz, other, side) * 64, 64), 64)


def cross_out_kernel(where, share, att_in, *rest):
    pieces, (mid, spread, weights, att, total, sems) = (rest[:9], rest[9:18]), rest[18:]
    copies = Copies(sems)
    started = [copies.start(att_in, att)]
    for distance in range(NZ):
        zz = lax.rem(where[1] + distance, NZ)
        for other in range(2):
            for side in range(2):
                place = weights.at[weight_rows(where, zz, other, side)]
                started.append(copies.start(half(pieces[other], distance, side), place))
    for copy in started:
        copy.wait()
    acc = share[...].astype(f32)
    for g in range(8):
        acc += dot(att[g], weights[g * 256 : (g + 1) * 256, :])
    total[...] = acc.astype(bf16)
    mid[...] = total[...]
    spread_out(copies, total, spread)


def qkv_kernel(where, gain, mids_in, own, par, keep, send, normed, proj, mids, weights, sems):
    copies = Copies(sems)
    mids_copies = [copies.start(mids_in.at[g], mids.at[g]) for g in range(8)]
    started = []
    for z in range(NZ):
        started.append(copies.start(own.at[z], weights.at[0, z]))
        started.append(copies.start(par.at[z], weights.at[1, z]))
    xh = where[0]
    rows = mids.shape[1]
    squares = jnp.zeros((rows, 512), f32)
    for g in range(8):
        mids_copies[g].wait()
        values = mids[g].astype(f32)
        squares += values * values
    row_scale = lax.rsqrt(jnp.sum(squares, axis=1, keepdims=True) * (1.0 / 4096) + epsilon)
    for b in range(32):
        block = mids[b // 4, :, b % 4 * 128 : (b % 4 + 1) * 128].astype(f32)
        normed[:, b * 128 : (b + 1) * 128] = (block * row_scale * gain[b : b + 1, :]).astype(bf16)
    for copy in started:
        copy.wait()
    for t in range(3):
        acc = jnp.zeros((rows, 256), f32)
        for z in range(NZ):
            for other in range(2):
                left, right = [], []
                for side in range(2):
                    owner = block_of(where, z, other, side)
                    left.append(normed[:, pl.ds(pl.multiple_of(owner * 128, 128), 128)])
                    right.append(weights[other, z, side * 3 + t])
                acc += dot(jnp.concatenate(left, axis=1), jnp.concatenate(right, axis=0))
        if t == 0:
            acc = acc * (math.log2(math.e) / math.sqrt(HD))
        proj[...] = acc.astype(bf16)
        keep[t] = proj[:, pl.ds(pl.multiple_of(xh * 128, 128), 128)]
        send[t] = proj[:, pl.ds(pl.multiple_of((1 - xh) * 128, 128), 128)]


def join(left, right):
    top = jnp.maximum(left[1], right[1])
    fade_left, fade_right = jnp.exp2(left[1] - top), jnp.exp2(right[1] - top)
    return (
        left[0] * fade_left + right[0] * fade_right,
        top,
        left[2] * fade_left + right[2] * fade_right,
    )


def attention_kernel(distances, where, order, query, *rest):
    first, last = distances[0] == 0, distances[0] == 4
    if not first:
        state_in, rest = rest[0], rest[1:]
    pieces, (state_out, k_places, q_places) = rest[:-3], rest[-3:]
    n = query.shape[1]
    rows = lax.broadcasted_iota(jnp.int32, (SPAN, 1), 0)
    lanes = lax.broadcasted_iota(jnp.int32, (1, 256), 1)
    right = lax.broadcasted_iota(jnp.int32, (n, HD), 1)
    span_of, within = lanes // SPAN, lanes % SPAN
    for i, distance in enumerate(distances):
        for side in range(2):
            c = block_of(where, lax.rem(where[1] + distance, NZ), 0, side)
            place = jnp.zeros((1, 256), jnp.int32)
            for s in range(4):
                place = jnp.where(span_of == s, order[c * 4 + s], place)
            k_places[i : i + 1, side * 256 : (side + 1) * 256] = place * SPAN + within
    for core in range(2):
        for side in range(2):
            c = block_of(where, where[1], core, side)
            for s in range(4):
                begin = (side * 4 + s) * SPAN
                q_places[core, begin : begin + SPAN, :] = order[c * 4 + s] * SPAN + rows

    def one_core(core, carry):
        top = jnp.full((n, 1), far_below, f32)
        total = jnp.zeros((n, 1), f32)
        mixed = jnp.zeros((n, HD), f32)
        places = q_places[core]
        rows_here = query[core]
        for i in range(len(distances)):
            keys, vals = (pieces[0][0], pieces[1][0]) if last else (pieces[i][0], pieces[i][1])
            scores = dot_t(rows_here, keys)
            scores = jnp.where(k_places[i : i + 1, :] <= places, scores, far_below)
            new_top = jnp.maximum(top, jnp.max(scores, axis=1, keepdims=True))
            exps = jnp.exp2(scores - new_top)
            fade = jnp.exp2(top - new_top)
            total = total * fade + jnp.sum(exps, axis=1, keepdims=True)
            mixed = mixed * fade + dot(exps.astype(bf16), vals)
            top = new_top
        state = (mixed, jnp.broadcast_to(top, (n, HD)), jnp.broadcast_to(total, (n, HD)))
        if not first:
            state = join(state, [state_in[core, :, i * HD : (i + 1) * HD] for i in range(3)])
        for i in range(3):
            state_out[core, :, i * HD : (i + 1) * HD] = state[i]
        return carry

    lax.fori_loop(0, 2, one_core, 0)


def attention_part(distances, where, order, query, state, pieces):
    n = query.shape[1]
    return call(
        functools.partial(attention_kernel, distances),
        sds((2, n, 3 * HD), f32),
        [SMEM] * 2 + [VMEM] * (1 + len(state) + len(pieces)),
        VMEM,
        [pltpu.VMEM((8, n), jnp.int32), pltpu.VMEM((2, n, 1), jnp.int32)],
        280_000_000 * len(distances),
        500_000 * len(distances),
    )(where, order, query, *state, *pieces)


def merge_kernel(where, own, par, out, halves, sems):
    mixed, _, total = join(
        [own[:, i * HD : (i + 1) * HD] for i in range(3)], [par[:, i * HD : (i + 1) * HD] for i in range(3)]
    )
    mixed = mixed / total
    copies = Copies(sems)
    started = []
    n = halves.shape[1]
    for side in range(2):
        halves[side] = mixed[side * n : (side + 1) * n].astype(bf16)
        for g in range(8):
            started.append(copies.start(halves.at[side], out.at[(where[0] ^ side) * 8 + g]))
    for copy in started:
        copy.wait()


def self_out_kernel(where, share, att_in, own, par, out, weights, att, sems):
    copies = Copies(sems)
    started = []
    for z in range(NZ):
        for other in range(2):
            for side in range(2):
                place = weights.at[weight_rows(where, z, other, side)]
                started.append(copies.start((own, par)[other].at[z, side], place))
    started.append(copies.start(att_in, att))
    for copy in started:
        copy.wait()
    acc = share[...].astype(f32)
    for g in range(8):
        both = jnp.concatenate([att[g], att[8 + g]], axis=1)
        acc += dot(both, weights[g * 256 : (g + 1) * 256, :])
    out[...] = acc.astype(bf16)


def deal_out_weights(blocks):
    n = blocks.shape[0]
    quarters = blocks.reshape(n, 4, 64, 128)
    near = lax.axis_index(("zl", "core"))
    got = [lax.dynamic_index_in_dim(quarters, near, 1, keepdims=False)]
    for m in (1, 2, 3):
        piece = lax.dynamic_index_in_dim(quarters, near ^ m, 1, keepdims=False)
        got.append(lax.ppermute(piece, ("zl", "core"), [(i, i ^ m) for i in range(4)]))
    got = jnp.stack(got)
    columns = [lax.dynamic_index_in_dim(got, near ^ q, 0, keepdims=False) for q in range(4)]
    pairs = [
        ((share * 4 + i) * 8 + group, (group * 4 + i) * 8 + share)
        for share in range(8)
        for i in range(4)
        for group in range(8)
    ]
    return lax.ppermute(jnp.concatenate(columns, axis=2), ALL, pairs)


def per_device(
    hidden_in,
    norm_gains,
    w_cross_query,
    w_cross_out,
    w_self_qkv,
    w_self_out,
    nbr_kv,
    nbr_count,
    nbr_source,
    span_order,
):
    rows, width = hidden_in.shape
    g = lax.axis_index(GROUP)
    y = lax.axis_index("y")
    where = jnp.stack([lax.axis_index(a) for a in ("xh", Z, "core", "y", "xl")]).astype(jnp.int32)
    gains = norm_gains.reshape(2, 32, 128)
    vmem = pltpu.VMEM
    sem = pltpu.SemaphoreType.DMA

    wq_own = gather_z(jnp.stack([w_cross_query, swap_xh(w_cross_query)]))
    wq_par = [swap_cores(p) for p in wq_own]
    dealt = deal_out_weights(jnp.stack([w_cross_out, w_self_out]))
    dealt_other = swap_xh(dealt)
    wo = jnp.stack([dealt[0], dealt_other[0]])
    wso = jnp.stack([dealt[1], dealt_other[1]])

    nbr, qkv_own, *_ = lax.optimization_barrier(
        (nbr_kv[0, 0], w_self_qkv.transpose(1, 0, 2), wq_own[1], wq_own[2], wq_own[7], wq_own[8])
    )
    nbr_got = [
        shift(lax.dynamic_index_in_dim(nbr, (y + k) % 4, 0, keepdims=False), "y", k, 4) for k in (1, 2, 3)
    ]
    late = jnp.concatenate([qkv_own, swap_xh(qkv_own)], axis=0)
    late_own = lax.all_gather(late, Z, axis=0, tiled=False)

    wq_own, wq_par, wo = lax.optimization_barrier((wq_own, wq_par, wo))
    cross_att = call(
        cross_kernel,
        sds((8, rows, 256)),
        [SMEM] * 3 + [VMEM] + [ANY] * 23,
        ANY,
        [
            vmem((rows, width), bf16),
            vmem((rows, width), bf16),
            vmem((2, NZ, 2, 128, 256), bf16),
            vmem((4, 3, 64, 512), bf16),
            vmem((rows, 256), bf16),
            sem((45,)),
        ],
        600_000_000,
        5_000_000,
    )(where, nbr_source.reshape(-1), nbr_count, gains[0], hidden_in, nbr, *nbr_got, *wq_own, *wq_par)

    wo_own = gather_z(wo)
    wo_par = [swap_cores(p) for p in wo_own]
    att_all = lax.all_to_all(cross_att, GROUP, 0, 0, tiled=True)
    hidden_share = lax.dynamic_slice_in_dim(hidden_in, g * 512, 512, 1)
    mid_share, spread = call(
        cross_out_kernel,
        [sds((rows, 512)), sds((8, rows, 512))],
        [SMEM, VMEM] + [ANY] * 19,
        [VMEM, ANY],
        [vmem((2048, 512), bf16), vmem((8, rows, 256), bf16), vmem((rows, 512), bf16), sem((41,))],
        600_000_000,
        4_000_000,
    )(where, hidden_share, att_all, *wo_own, *wo_par)

    late_own = after(late_own, spread)
    late_par = swap_cores(late_own)
    wso_own = lax.all_gather(after(wso, late_own), Z, axis=0, tiled=False)
    mids = lax.all_to_all(spread, GROUP, 0, 0, tiled=True)
    keep, send = call(
        qkv_kernel,
        [sds((3, rows, HD))] * 2,
        [SMEM, VMEM] + [ANY] * 3,
        [VMEM] * 2,
        [
            vmem((rows, width), bf16),
            vmem((rows, 256), bf16),
            vmem((8, rows, 512), bf16),
            vmem((2, NZ, 6, 128, 256), bf16),
            sem((24,)),
        ],
        1_600_000_000,
        11_000_000,
    )(where, gains[1], mids, late_own, late_par)

    both = jnp.concatenate([keep, swap_xh(send)], axis=1)
    kv = both[1:]
    query = jnp.stack([both[0], swap_cores(both[0])])
    part = functools.partial(attention_part, where=where, order=span_order, query=query)
    r1, l1 = shift(kv, Z, 1, NZ), shift(kv, Z, -1, NZ)
    state = part((0,), state=[], pieces=[kv])
    r2, l2 = shift(r1, Z, 1, NZ), shift(l1, Z, -1, NZ)
    r2, l2, state = lax.optimization_barrier((r2, l2, state))
    r3, l3 = shift(r2, Z, 1, NZ), shift(l2, Z, -1, NZ)
    state = part((1, 7), state=[state], pieces=[l1, r1])
    r3, l3, state, wso_own = lax.optimization_barrier((r3, l3, state, wso_own))
    r4, l4 = shift(r3[:1], Z, 1, NZ), shift(l3[1:], Z, -1, NZ)
    wso_par = swap_cores(wso_own)
    state = part((2, 6, 3, 5), state=[state], pieces=[l2, r2, l3, r3])
    r4, l4, state = lax.optimization_barrier((r4, l4, state))
    state = part((4,), state=[state], pieces=[r4, l4])
    heads = call(
        merge_kernel,
        sds((16, rows, HD)),
        [SMEM, VMEM, VMEM],
        ANY,
        [vmem((2, rows, HD), bf16), sem((16,))],
        1_000_000,
        2_000_000,
    )(where, state[0], swap_cores(state[1]))
    self_all = lax.all_to_all(heads, ("xh",) + GROUP, 0, 0, tiled=True)
    return call(
        self_out_kernel,
        sds((rows, 512)),
        [SMEM, VMEM] + [ANY] * 3,
        VMEM,
        [vmem((2048, 512), bf16), vmem((16, rows, HD), bf16), sem((33,))],
        600_000_000,
        4_000_000,
    )(where, mid_share, self_all, wso_own, wso_par)


def solution(mesh):
    fine = Mesh(mesh.devices.reshape(2, 4, 2, 2, 4, 2), ALL)
    in_specs = (
        P(CTX, None),
        P(),
        P(CTX, GROUP),
        P(GROUP, CTX),
        P(CTX, None, GROUP),
        P(GROUP, CTX),
        P(CTX, "y", None, None, None, "xl"),
        P(CTX),
        P(CTX, None),
        P(),
    )
    return jax.shard_map(
        per_device, mesh=fine, in_specs=in_specs, out_specs=P(CTX, GROUP), check_vma=False
    )
```

```python
import functools
import math

import jax
import jax.numpy as jnp
from jax import lax
from jax.experimental import pallas as pl
from jax.experimental.pallas import tpu as pltpu
from jax.sharding import Mesh
from jax.sharding import PartitionSpec as P

HD = 128
SPAN = 64
epsilon = 1e-05
far_below = -1e30
NZ = 8

VMEM = pl.BlockSpec(memory_space=pltpu.VMEM)
SMEM = pl.BlockSpec(memory_space=pltpu.SMEM)
ANY = pl.BlockSpec(memory_space=pl.ANY)
f32 = jnp.float32
bf16 = jnp.bfloat16

Z = ("zh", "zl")
CTX = ("xh",) + Z + ("core",)
GROUP = ("y", "xl")
ALL = CTX + GROUP


def dot(a, b):
    return jnp.dot(a, b, preferred_element_type=f32)


def dot_t(a, b):
    return lax.dot_general(a, b, (((1,), (1,)), ((), ())), preferred_element_type=f32)


def call(kernel, out_shape, in_specs, out_specs, scratch, flops, nbytes):
    return pl.pallas_call(
        kernel,
        out_shape=out_shape,
        in_specs=in_specs,
        out_specs=out_specs,
        scratch_shapes=scratch,
        compiler_params=pltpu.CompilerParams(vmem_limit_bytes=24 * 1024 * 1024),
        cost_estimate=pl.CostEstimate(flops=flops, bytes_accessed=nbytes, transcendentals=0),
    )


def sds(shape, dtype=bf16):
    return jax.ShapeDtypeStruct(shape, dtype)


def after(x, *earlier):
    return lax.optimization_barrier((x,) + earlier)[0]


def shift(x, axis, by, size):
    return lax.ppermute(x, axis, [(i, (i + by) % size) for i in range(size)])


def swap_cores(x):
    return shift(x, "core", 1, 2)


def swap_xh(x):
    return shift(x, "xh", 1, 2)


def gather_z(x):
    r1, l1 = shift(x, Z, 1, NZ), shift(x, Z, -1, NZ)
    r2, l2 = shift(x, Z, 2, NZ), shift(x, Z, -2, NZ)
    r3, l3 = shift(r1, Z, 2, NZ), shift(l1, Z, -2, NZ)
    cut = x.shape[0] // 2
    r4, l4 = shift(r2[:cut], Z, 2, NZ), shift(l2[cut:], Z, -2, NZ)
    return [x, l1, l2, l3, r4, l4, r3, r2, r1]


def block_of(where, zz, other, side):
    return (where[0] ^ side) * 16 + zz * 2 + (where[2] ^ other)


class Copies:
    def __init__(self, sems):
        self.sems = sems
        self.used = 0

    def start(self, source, target):
        copy = pltpu.make_async_copy(source, target, self.sems.at[self.used])
        self.used += 1
        copy.start()
        return copy


def spread_out(copies, source, out):
    started = [copies.start(source, out.at[i]) for i in range(out.shape[0])]
    for copy in started:
        copy.wait()


def norm_kernel(hidden, gain, out):
    values = hidden[...].astype(f32)
    row_scale = lax.rsqrt(jnp.mean(values * values, axis=1, keepdims=True) + epsilon)
    for b in range(32):
        cols = slice(b * 128, (b + 1) * 128)
        block = hidden[:, cols].astype(f32)
        out[:, cols] = (block * row_scale * gain[b : b + 1, :]).astype(bf16)


def cross_kernel(where, source, count, normed_in, nbr0, nbr1, nbr2, nbr3, *rest):
    pieces = (rest[:9], rest[9:18])
    out, normed, weights, nbr, mixed_all, sems = rest[18:]
    copies = Copies(sems)
    y = where[3]
    started = [copies.start(normed_in, normed)]
    for i in range(9):
        for other in range(2):
            if i == 4 or i == 5:
                place = weights.at[other, 4, pl.ds((i - 4) * 2, 2)]
            else:
                place = weights.at[other, i if i < 4 else i - 1]
            started.append(copies.start(pieces[other][i], place))
    nbr_copies = [copies.start(nbr0.at[y], nbr.at[y])]
    for k, ref in ((1, nbr1), (2, nbr2), (3, nbr3)):
        nbr_copies.append(copies.start(ref, nbr.at[lax.rem(y + 4 - k, 4)]))
    for copy in started:
        copy.wait()
    acc = jnp.zeros((normed.shape[0], 256), f32)
    for distance in range(NZ):
        zz = lax.rem(where[1] + distance, NZ)
        for other in range(2):
            left, right = [], []
            for side in range(2):
                owner = block_of(where, zz, other, side)
                left.append(normed[:, pl.ds(pl.multiple_of(owner * 128, 128), 128)])
                right.append(weights[other, distance, side * 2])
            acc += dot(jnp.concatenate(left, axis=1), jnp.concatenate(right, axis=0))
    for copy in nbr_copies:
        copy.wait()
    query = acc.astype(bf16)
    scale = 1.0 / math.sqrt(HD)
    lanes = lax.broadcasted_iota(jnp.int32, (SPAN, 128), 1)
    chosen = [source[i] for i in range(8)]
    for s in range(4):
        slots = []
        for j in range(2):
            i = s * 2 + j
            rank = jnp.int32(0)
            for k in range(s * 2):
                rank = rank + (chosen[k] == chosen[i]).astype(jnp.int32)
            slots.append((chosen[i], rank))
        alive = lanes < count[s] * 64
        for h in range(2):
            kcols = slice(2 * h * HD, (2 * h + 1) * HD)
            vcols = slice((2 * h + 1) * HD, (2 * h + 2) * HD)
            keys = jnp.concatenate([nbr[e, r, :, kcols] for e, r in slots], axis=0)
            vals = jnp.concatenate([nbr[e, r, :, vcols] for e, r in slots], axis=0)
            part = query[s * SPAN : (s + 1) * SPAN, h * HD : (h + 1) * HD]
            scores = jnp.where(alive, dot_t(part, keys) * scale, far_below)
            top = jnp.max(scores, axis=1, keepdims=True)
            exps = jnp.exp(scores - top)
            total = jnp.sum(exps, axis=1, keepdims=True)
            mixed = dot(exps.astype(bf16), vals) / total
            mixed_all[s * SPAN : (s + 1) * SPAN, h * HD : (h + 1) * HD] = mixed.astype(bf16)
    att = mixed_all[...]
    for distance in range(NZ):
        zz = lax.rem(where[1] + distance, NZ)
        for other in range(2):
            blocks = [weights[other, distance, side * 2 + 1] for side in range(2)]
            upper = jnp.concatenate([block[:, :128] for block in blocks], axis=1)
            lower = jnp.concatenate([block[:, 128:] for block in blocks], axis=1)
            term = dot(att, jnp.concatenate([upper, lower], axis=0)).astype(bf16)
            for side in range(2):
                owner = block_of(where, zz, other, side)
                cols = pl.ds(pl.multiple_of(lax.rem(owner, 4) * 128, 128), 128)
                out[owner // 4, :, cols] = term[:, side * 128 : (side + 1) * 128]


def weight_rows(where, zz, other, side):
    return pl.ds(pl.multiple_of(block_of(where, zz, other, side) * 64, 64), 64)


def sum_kernel(share, terms, mid, spread, total, sems):
    acc = terms[0].astype(f32)
    for g in range(1, 8):
        acc += terms[g].astype(f32)
    total[...] = (share[...].astype(f32) + acc).astype(bf16)
    mid[...] = total[...]
    spread_out(Copies(sems), total, spread)


def qkv_kernel(where, gain, mids_in, own, par, keep, send, normed, proj, mids, weights, sems):
    copies = Copies(sems)
    mids_copies = [copies.start(mids_in.at[g], mids.at[g]) for g in range(8)]
    started = []
    for z in range(NZ):
        started.append(copies.start(own.at[z], weights.at[0, z]))
        started.append(copies.start(par.at[z], weights.at[1, z]))
    xh = where[0]
    rows = mids.shape[1]
    squares = jnp.zeros((rows, 512), f32)
    for g in range(8):
        mids_copies[g].wait()
        values = mids[g].astype(f32)
        squares += values * values
    row_scale = lax.rsqrt(jnp.sum(squares, axis=1, keepdims=True) * (1.0 / 4096) + epsilon)
    for b in range(32):
        block = mids[b // 4, :, b % 4 * 128 : (b % 4 + 1) * 128].astype(f32)
        normed[:, b * 128 : (b + 1) * 128] = (block * row_scale * gain[b : b + 1, :]).astype(bf16)
    for copy in started:
        copy.wait()
    for t in range(3):
        acc = jnp.zeros((rows, 256), f32)
        for z in range(NZ):
            for other in range(2):
                left, right = [], []
                for side in range(2):
                    owner = block_of(where, z, other, side)
                    left.append(normed[:, pl.ds(pl.multiple_of(owner * 128, 128), 128)])
                    right.append(weights[other, z, side * 3 + t])
                acc += dot(jnp.concatenate(left, axis=1), jnp.concatenate(right, axis=0))
        if t == 0:
            acc = acc * (math.log2(math.e) / math.sqrt(HD))
        proj[...] = acc.astype(bf16)
        keep[t] = proj[:, pl.ds(pl.multiple_of(xh * 128, 128), 128)]
        send[t] = proj[:, pl.ds(pl.multiple_of((1 - xh) * 128, 128), 128)]


def join(left, right):
    top = jnp.maximum(left[1], right[1])
    fade_left, fade_right = jnp.exp2(left[1] - top), jnp.exp2(right[1] - top)
    return (
        left[0] * fade_left + right[0] * fade_right,
        top,
        left[2] * fade_left + right[2] * fade_right,
    )


def attention_kernel(distances, where, order, query, *rest):
    first, last = distances[0] == 0, distances[0] == 4
    if not first:
        state_in, rest = rest[0], rest[1:]
    pieces, (state_out, k_places, q_places) = rest[:-3], rest[-3:]
    n = query.shape[1]
    rows = lax.broadcasted_iota(jnp.int32, (SPAN, 1), 0)
    lanes = lax.broadcasted_iota(jnp.int32, (1, 256), 1)
    right = lax.broadcasted_iota(jnp.int32, (n, HD), 1)
    span_of, within = lanes // SPAN, lanes % SPAN
    for i, distance in enumerate(distances):
        for side in range(2):
            c = block_of(where, lax.rem(where[1] + distance, NZ), 0, side)
            place = jnp.zeros((1, 256), jnp.int32)
            for s in range(4):
                place = jnp.where(span_of == s, order[c * 4 + s], place)
            k_places[i : i + 1, side * 256 : (side + 1) * 256] = place * SPAN + within
    for core in range(2):
        for side in range(2):
            c = block_of(where, where[1], core, side)
            for s in range(4):
                begin = (side * 4 + s) * SPAN
                q_places[core, begin : begin + SPAN, :] = order[c * 4 + s] * SPAN + rows

    def one_core(core, carry):
        top = jnp.full((n, 1), far_below, f32)
        total = jnp.zeros((n, 1), f32)
        mixed = jnp.zeros((n, HD), f32)
        places = q_places[core]
        rows_here = query[core]
        for i in range(len(distances)):
            keys, vals = (pieces[0][0], pieces[1][0]) if last else (pieces[i][0], pieces[i][1])
            scores = dot_t(rows_here, keys)
            scores = jnp.where(k_places[i : i + 1, :] <= places, scores, far_below)
            new_top = jnp.maximum(top, jnp.max(scores, axis=1, keepdims=True))
            exps = jnp.exp2(scores - new_top)
            fade = jnp.exp2(top - new_top)
            total = total * fade + jnp.sum(exps, axis=1, keepdims=True)
            mixed = mixed * fade + dot(exps.astype(bf16), vals)
            top = new_top
        state = (mixed, jnp.broadcast_to(top, (n, HD)), jnp.broadcast_to(total, (n, HD)))
        if not first:
            state = join(state, [state_in[core, :, i * HD : (i + 1) * HD] for i in range(3)])
        for i in range(3):
            state_out[core, :, i * HD : (i + 1) * HD] = state[i]
        return carry

    lax.fori_loop(0, 2, one_core, 0)


def attention_part(distances, where, order, query, state, pieces):
    n = query.shape[1]
    return call(
        functools.partial(attention_kernel, distances),
        sds((2, n, 3 * HD), f32),
        [SMEM] * 2 + [VMEM] * (1 + len(state) + len(pieces)),
        VMEM,
        [pltpu.VMEM((8, n), jnp.int32), pltpu.VMEM((2, n, 1), jnp.int32)],
        280_000_000 * len(distances),
        500_000 * len(distances),
    )(where, order, query, *state, *pieces)


def merge_kernel(where, own, par, out, halves, sems):
    mixed, _, total = join(
        [own[:, i * HD : (i + 1) * HD] for i in range(3)], [par[:, i * HD : (i + 1) * HD] for i in range(3)]
    )
    mixed = mixed / total
    copies = Copies(sems)
    started = []
    n = halves.shape[1]
    for side in range(2):
        halves[side] = mixed[side * n : (side + 1) * n].astype(bf16)
        for g in range(8):
            started.append(copies.start(halves.at[side], out.at[(where[0] ^ side) * 8 + g]))
    for copy in started:
        copy.wait()


def self_out_kernel(where, share, att_in, own, par, out, weights, att, sems):
    copies = Copies(sems)
    started = []
    for z in range(NZ):
        for other in range(2):
            for side in range(2):
                place = weights.at[weight_rows(where, z, other, side)]
                started.append(copies.start((own, par)[other].at[z, side], place))
    started.append(copies.start(att_in, att))
    for copy in started:
        copy.wait()
    acc = share[...].astype(f32)
    for g in range(8):
        both = jnp.concatenate([att[g], att[8 + g]], axis=1)
        acc += dot(both, weights[g * 256 : (g + 1) * 256, :])
    out[...] = acc.astype(bf16)


def deal_out_weights(blocks):
    n = blocks.shape[0]
    quarters = blocks.reshape(n, 4, 64, 128)
    near = lax.axis_index(("zl", "core"))
    got = [lax.dynamic_index_in_dim(quarters, near, 1, keepdims=False)]
    for m in (1, 2, 3):
        piece = lax.dynamic_index_in_dim(quarters, near ^ m, 1, keepdims=False)
        got.append(lax.ppermute(piece, ("zl", "core"), [(i, i ^ m) for i in range(4)]))
    got = jnp.stack(got)
    columns = [lax.dynamic_index_in_dim(got, near ^ q, 0, keepdims=False) for q in range(4)]
    pairs = [
        ((share * 4 + i) * 8 + group, (group * 4 + i) * 8 + share)
        for share in range(8)
        for i in range(4)
        for group in range(8)
    ]
    return lax.ppermute(jnp.concatenate(columns, axis=2), ALL, pairs)


def per_device(
    hidden_in,
    norm_gains,
    w_cross_query,
    w_cross_out,
    w_self_qkv,
    w_self_out,
    nbr_kv,
    nbr_count,
    nbr_source,
    span_order,
):
    rows, width = hidden_in.shape
    g = lax.axis_index(GROUP)
    y = lax.axis_index("y")
    where = jnp.stack([lax.axis_index(a) for a in ("xh", Z, "core", "y", "xl")]).astype(jnp.int32)
    gains = norm_gains.reshape(2, 32, 128)
    vmem = pltpu.VMEM
    sem = pltpu.SemaphoreType.DMA

    first = jnp.stack([w_cross_query, jnp.concatenate([w_cross_out[:128], w_cross_out[128:]], axis=1)])
    first = jnp.concatenate([first, swap_xh(first)], axis=0)
    first_own = gather_z(first)
    first_par = [swap_cores(p) for p in first_own]
    nbr, hidden, _ = lax.optimization_barrier((nbr_kv[0, 0], hidden_in, first))
    nbr_got = [
        shift(lax.dynamic_index_in_dim(nbr, (y + k) % 4, 0, keepdims=False), "y", k, 4) for k in (1, 2, 3)
    ]
    normed = call(norm_kernel, sds((rows, width)), [VMEM] * 2, VMEM, [], 10_000_000, 4_000_000)(hidden, gains[0])
    hidden_share = lax.dynamic_slice_in_dim(hidden, g * 512, 512, 1)
    terms = call(
        cross_kernel,
        sds((8, rows, 512)),
        [SMEM] * 3 + [ANY] * 23,
        VMEM,
        [
            vmem((rows, width), bf16),
            vmem((2, NZ, 4, 128, 256), bf16),
            vmem((4, 3, 64, 512), bf16),
            vmem((rows, 256), bf16),
            sem((23,)),
        ],
        1_200_000_000,
        10_000_000,
    )(where, nbr_source.reshape(-1), nbr_count, normed, nbr, *nbr_got, *first_own, *first_par)

    qkv_own, wso_block, terms = lax.optimization_barrier((w_self_qkv.transpose(1, 0, 2), w_self_out, terms))
    late_own = lax.all_gather(jnp.concatenate([qkv_own, swap_xh(qkv_own)], axis=0), Z, axis=0, tiled=False)
    dealt = deal_out_weights(wso_block[None])
    terms = lax.all_to_all(terms, GROUP, 0, 0, tiled=True)
    mid_share, spread = call(
        sum_kernel,
        [sds((rows, 512)), sds((8, rows, 512))],
        [VMEM] * 2,
        [VMEM, ANY],
        [vmem((rows, 512), bf16), sem((8,))],
        2_000_000,
        4_000_000,
    )(hidden_share, terms)

    late_own = after(late_own, spread)
    late_par = swap_cores(late_own)
    dealt = after(dealt, spread)
    wso = jnp.concatenate([dealt, swap_xh(dealt)], axis=0)
    wso_own = lax.all_gather(after(wso, late_own), Z, axis=0, tiled=False)
    mids = lax.all_to_all(spread, GROUP, 0, 0, tiled=True)
    keep, send = call(
        qkv_kernel,
        [sds((3, rows, HD))] * 2,
        [SMEM, VMEM] + [ANY] * 3,
        [VMEM] * 2,
        [
            vmem((rows, width), bf16),
            vmem((rows, 256), bf16),
            vmem((8, rows, 512), bf16),
            vmem((2, NZ, 6, 128, 256), bf16),
            sem((24,)),
        ],
        1_600_000_000,
        11_000_000,
    )(where, gains[1], mids, late_own, late_par)

    both = jnp.concatenate([keep, swap_xh(send)], axis=1)
    kv = both[1:]
    query = jnp.stack([both[0], swap_cores(both[0])])
    part = functools.partial(attention_part, where=where, order=span_order, query=query)
    r1, l1 = shift(kv, Z, 1, NZ), shift(kv, Z, -1, NZ)
    state = part((0,), state=[], pieces=[kv])
    r2, l2 = shift(r1, Z, 1, NZ), shift(l1, Z, -1, NZ)
    r2, l2, state = lax.optimization_barrier((r2, l2, state))
    r3, l3 = shift(r2, Z, 1, NZ), shift(l2, Z, -1, NZ)
    state = part((1, 7), state=[state], pieces=[l1, r1])
    r3, l3, state, wso_own = lax.optimization_barrier((r3, l3, state, wso_own))
    r4, l4 = shift(r3[:1], Z, 1, NZ), shift(l3[1:], Z, -1, NZ)
    wso_par = swap_cores(wso_own)
    state = part((2, 6, 3, 5), state=[state], pieces=[l2, r2, l3, r3])
    r4, l4, state = lax.optimization_barrier((r4, l4, state))
    state = part((4,), state=[state], pieces=[r4, l4])
    heads = call(
        merge_kernel,
        sds((16, rows, HD)),
        [SMEM, VMEM, VMEM],
        ANY,
        [vmem((2, rows, HD), bf16), sem((16,))],
        1_000_000,
        2_000_000,
    )(where, state[0], swap_cores(state[1]))
    self_all = lax.all_to_all(heads, ("xh",) + GROUP, 0, 0, tiled=True)
    return call(
        self_out_kernel,
        sds((rows, 512)),
        [SMEM, VMEM] + [ANY] * 3,
        VMEM,
        [vmem((2048, 512), bf16), vmem((16, rows, HD), bf16), sem((33,))],
        600_000_000,
        4_000_000,
    )(where, mid_share, self_all, wso_own, wso_par)


def solution(mesh):
    fine = Mesh(mesh.devices.reshape(2, 4, 2, 2, 4, 2), ALL)
    in_specs = (
        P(CTX, None),
        P(),
        P(CTX, GROUP),
        P(GROUP, CTX),
        P(CTX, None, GROUP),
        P(GROUP, CTX),
        P(CTX, "y", None, None, None, "xl"),
        P(CTX),
        P(CTX, None),
        P(),
    )
    return jax.shard_map(
        per_device, mesh=fine, in_specs=in_specs, out_specs=P(CTX, GROUP), check_vma=False
    )
```

```python
import functools
import math

import jax
import jax.numpy as jnp
from jax import lax
from jax.experimental import pallas as pl
from jax.experimental.pallas import tpu as pltpu
from jax.sharding import Mesh
from jax.sharding import PartitionSpec as P

HD = 128
SPAN = 64
epsilon = 1e-05
far_below = -1e30
NZ = 8

VMEM = pl.BlockSpec(memory_space=pltpu.VMEM)
SMEM = pl.BlockSpec(memory_space=pltpu.SMEM)
ANY = pl.BlockSpec(memory_space=pl.ANY)
f32 = jnp.float32
bf16 = jnp.bfloat16

Z = ("zh", "zl")
CTX = ("xh",) + Z + ("core",)
GROUP = ("y", "xl")
ALL = CTX + GROUP


def dot(a, b):
    return jnp.dot(a, b, preferred_element_type=f32)


def dot_t(a, b):
    return lax.dot_general(a, b, (((1,), (1,)), ((), ())), preferred_element_type=f32)


def call(kernel, out_shape, in_specs, out_specs, scratch, flops, nbytes):
    return pl.pallas_call(
        kernel,
        out_shape=out_shape,
        in_specs=in_specs,
        out_specs=out_specs,
        scratch_shapes=scratch,
        compiler_params=pltpu.CompilerParams(vmem_limit_bytes=16 * 1024 * 1024),
        cost_estimate=pl.CostEstimate(flops=flops, bytes_accessed=nbytes, transcendentals=0),
    )


def sds(shape, dtype=bf16):
    return jax.ShapeDtypeStruct(shape, dtype)


def after(x, *earlier):
    return lax.optimization_barrier((x,) + earlier)[0]


def shift(x, axis, by, size):
    return lax.ppermute(x, axis, [(i, (i + by) % size) for i in range(size)])


def swap_cores(x):
    return shift(x, "core", 1, 2)


def swap_xh(x):
    return shift(x, "xh", 1, 2)


def gather_start(x):
    return x, shift(x, Z, 1, NZ), shift(x, Z, -1, NZ), shift(x, Z, 2, NZ), shift(x, Z, -2, NZ)


def gather_end(start):
    x, r1, l1, r2, l2 = start
    r3, l3 = shift(r1, Z, 2, NZ), shift(l1, Z, -2, NZ)
    cut = x.shape[0] // 2
    r4, l4 = shift(r2[:cut], Z, 2, NZ), shift(l2[cut:], Z, -2, NZ)
    return [x, l1, l2, l3, r4, l4, r3, r2, r1]


def shift_group(x, dy, dx):
    pairs = [(y * 2 + xl, (y + dy) % 4 * 2 + (xl ^ dx)) for y in range(4) for xl in range(2)]
    return lax.ppermute(x, GROUP, pairs)


PEERS = ((1, 0), (3, 0), (0, 1), (1, 1), (3, 1), (2, 0), (2, 1))


def here():
    return tuple(lax.axis_index(a) for a in ("xh", Z, "core", "y", "xl"))


def peer_group(where, dy, dx):
    return lax.rem(where[3] + dy, 4) * 2 + (where[4] ^ dx)


def block_of(where, zz, other, side):
    return (where[0] ^ side) * 16 + zz * 2 + (where[2] ^ other)


class Copies:
    def __init__(self, sems):
        self.sems = sems
        self.used = 0

    def start(self, source, target):
        copy = pltpu.make_async_copy(source, target, self.sems.at[self.used])
        self.used += 1
        copy.start()
        return copy


def norm_kernel(hidden, gain, out):
    values = hidden[...].astype(f32)
    row_scale = lax.rsqrt(jnp.mean(values * values, axis=1, keepdims=True) + epsilon)
    for b in range(32):
        cols = slice(b * 128, (b + 1) * 128)
        block = hidden[:, cols].astype(f32)
        out[:, cols] = (block * row_scale * gain[:1, cols]).astype(bf16)


def cross_kernel(source, count, normed, nbr0, nbr1, nbr2, nbr3, *rest):
    pieces = (rest[:9], rest[9:18])
    outs, (weights, nbr, mixed_all, sems) = rest[18:26], rest[26:]
    copies = Copies(sems)
    where = here()
    y = where[3]
    started = []
    for distance in range(NZ):
        zz = lax.rem(where[1] + distance, NZ)
        for other in range(2):
            for side in range(2):
                if distance == 4:
                    piece = pieces[other][4 + side]
                else:
                    piece = pieces[other][distance if distance < 4 else distance + 1].at[pl.ds(side * 2, 2)]
                started.append(copies.start(piece, weights.at[block_of(where, zz, other, side)]))
    nbr_copies = [copies.start(nbr0.at[y], nbr.at[y])]
    for k, ref in ((1, nbr1), (2, nbr2), (3, nbr3)):
        nbr_copies.append(copies.start(ref, nbr.at[lax.rem(y + 4 - k, 4)]))
    for copy in started:
        copy.wait()
    acc = jnp.zeros((normed.shape[0], 256), f32)
    for c in range(0, 32, 2):
        right = jnp.concatenate([weights[c, 0], weights[c + 1, 0]], axis=0)
        acc += dot(normed[:, c * 128 : (c + 2) * 128], right)
    for copy in nbr_copies:
        copy.wait()
    query = acc.astype(bf16)
    scale = 1.0 / math.sqrt(HD)
    lanes = lax.broadcasted_iota(jnp.int32, (SPAN, 128), 1)
    chosen = [source[i // 2, i % 2] for i in range(8)]
    for s in range(4):
        slots = []
        for j in range(2):
            i = s * 2 + j
            rank = jnp.int32(0)
            for k in range(s * 2):
                rank = rank + (chosen[k] == chosen[i]).astype(jnp.int32)
            slots.append((chosen[i], rank))
        alive = lanes < count[s] * 64
        for h in range(2):
            kcols = slice(2 * h * HD, (2 * h + 1) * HD)
            vcols = slice((2 * h + 1) * HD, (2 * h + 2) * HD)
            keys = jnp.concatenate([nbr[e, r, :, kcols] for e, r in slots], axis=0)
            vals = jnp.concatenate([nbr[e, r, :, vcols] for e, r in slots], axis=0)
            part = query[s * SPAN : (s + 1) * SPAN, h * HD : (h + 1) * HD]
            scores = jnp.where(alive, dot_t(part, keys) * scale, far_below)
            top = jnp.max(scores, axis=1, keepdims=True)
            exps = jnp.exp(scores - top)
            total = jnp.sum(exps, axis=1, keepdims=True)
            mixed = dot(exps.astype(bf16), vals) / total
            mixed_all[s * SPAN : (s + 1) * SPAN, h * HD : (h + 1) * HD] = mixed.astype(bf16)
    att = mixed_all[...]
    for out, (dy, dx) in zip(outs, ((0, 0),) + PEERS):
        first = peer_group(where, dy, dx) * 4
        for pair in range(2):
            blocks = [weights[first + pair * 2 + i, 1] for i in range(2)]
            upper = jnp.concatenate([block[:, :128] for block in blocks], axis=1)
            lower = jnp.concatenate([block[:, 128:] for block in blocks], axis=1)
            term = dot(att, jnp.concatenate([upper, lower], axis=0))
            out[:, pair * 256 : (pair + 1) * 256] = term.astype(bf16)


def weight_rows(where, zz, other, side):
    return pl.ds(pl.multiple_of(block_of(where, zz, other, side) * 64, 64), 64)


def sum_kernel(share, *rest):
    terms, mid = rest[:8], rest[8]
    acc = terms[0][...].astype(f32)
    for term in terms[1:]:
        acc += term[...].astype(f32)
    mid[...] = (share[...].astype(f32) + acc).astype(bf16)


def qkv_kernel(gain, own, par, *rest):
    mids, (keep, send, normed, proj) = rest[:8], rest[8:]
    where = here()
    xh = where[0]
    rows = mids[0].shape[0]
    squares = jnp.zeros((rows, 512), f32)
    for mid in mids:
        values = mid[...].astype(f32)
        squares += values * values
    row_scale = lax.rsqrt(jnp.sum(squares, axis=1, keepdims=True) * (1.0 / 4096) + epsilon)
    for mid, (dy, dx) in zip(mids, ((0, 0),) + PEERS):
        first = peer_group(where, 4 - dy, dx) * 512
        for j in range(4):
            cols = pl.ds(pl.multiple_of(first + j * 128, 128), 128)
            block = mid[:, j * 128 : (j + 1) * 128].astype(f32)
            normed[:, cols] = (block * row_scale * gain[1:2, cols]).astype(bf16)
    for t in range(3):
        acc = jnp.zeros((rows, 256), f32)
        for z in range(NZ):
            for other in range(2):
                left, right = [], []
                for side in range(2):
                    owner = block_of(where, z, other, side)
                    left.append(normed[:, pl.ds(pl.multiple_of(owner * 128, 128), 128)])
                    right.append((own, par)[other][z, side * 3 + t])
                acc += dot(jnp.concatenate(left, axis=1), jnp.concatenate(right, axis=0))
        if t == 0:
            acc = acc * (math.log2(math.e) / math.sqrt(HD))
        proj[...] = acc.astype(bf16)
        keep[t] = proj[:, pl.ds(pl.multiple_of(xh * 128, 128), 128)]
        send[t] = proj[:, pl.ds(pl.multiple_of((1 - xh) * 128, 128), 128)]


def join(left, right):
    top = jnp.maximum(left[1], right[1])
    fade_left, fade_right = jnp.exp2(left[1] - top), jnp.exp2(right[1] - top)
    return (
        left[0] * fade_left + right[0] * fade_right,
        top,
        left[2] * fade_left + right[2] * fade_right,
    )


def attention_kernel(distances, order, query, *rest):
    first = distances[0] == 0
    where = here()
    if not first:
        state_in, rest = rest[0], rest[1:]
    pieces, (state_out, k_places, q_places) = rest[:-3], rest[-3:]
    n = query.shape[1]
    rows = lax.broadcasted_iota(jnp.int32, (SPAN, 1), 0)
    lanes = lax.broadcasted_iota(jnp.int32, (1, 256), 1)
    right = lax.broadcasted_iota(jnp.int32, (n, HD), 1)
    span_of, within = lanes // SPAN, lanes % SPAN
    for i, distance in enumerate(distances):
        for side in range(2):
            c = block_of(where, lax.rem(where[1] + distance, NZ), 0, side)
            place = jnp.zeros((1, 256), jnp.int32)
            for s in range(4):
                place = jnp.where(span_of == s, order[c * 4 + s], place)
            k_places[i : i + 1, side * 256 : (side + 1) * 256] = place * SPAN + within
    for core in range(2):
        for side in range(2):
            c = block_of(where, where[1], core, side)
            for s in range(4):
                begin = (side * 4 + s) * SPAN
                q_places[core, begin : begin + SPAN, :] = order[c * 4 + s] * SPAN + rows

    def one_core(core, carry):
        top = jnp.full((n, 1), far_below, f32)
        total = jnp.zeros((n, 1), f32)
        mixed = jnp.zeros((n, HD), f32)
        places = q_places[core]
        rows_here = query[core]
        for i in range(len(distances)):
            if distances[i] == 4:
                keys, vals = pieces[i][0], pieces[i + 1][0]
            else:
                keys, vals = pieces[i][0], pieces[i][1]
            scores = dot_t(rows_here, keys)
            scores = jnp.where(k_places[i : i + 1, :] <= places, scores, far_below)
            new_top = jnp.maximum(top, jnp.max(scores, axis=1, keepdims=True))
            exps = jnp.exp2(scores - new_top)
            fade = jnp.exp2(top - new_top)
            total = total * fade + jnp.sum(exps, axis=1, keepdims=True)
            mixed = mixed * fade + dot(exps.astype(bf16), vals)
            top = new_top
        state = (mixed, jnp.broadcast_to(top, (n, HD)), jnp.broadcast_to(total, (n, HD)))
        if not first:
            state = join(state, [state_in[core, :, i * HD : (i + 1) * HD] for i in range(3)])
        for i in range(3):
            state_out[core, :, i * HD : (i + 1) * HD] = state[i]
        return carry

    lax.fori_loop(0, 2, one_core, 0)


def attention_part(distances, order, query, state, pieces):
    n = query.shape[1]
    return call(
        functools.partial(attention_kernel, distances),
        sds((2, n, 3 * HD), f32),
        [SMEM] + [VMEM] * (1 + len(state) + len(pieces)),
        VMEM,
        [pltpu.VMEM((8, n), jnp.int32), pltpu.VMEM((2, n, 1), jnp.int32)],
        280_000_000 * len(distances),
        500_000 * len(distances),
    )(order, query, *state, *pieces)


def merge_kernel(own, par, out, halves, sems):
    mixed, _, total = join(
        [own[:, i * HD : (i + 1) * HD] for i in range(3)], [par[:, i * HD : (i + 1) * HD] for i in range(3)]
    )
    mixed = mixed / total
    copies = Copies(sems)
    started = []
    n = halves.shape[1]
    for side in range(2):
        halves[side] = mixed[side * n : (side + 1) * n].astype(bf16)
        for g in range(8):
            started.append(copies.start(halves.at[side], out.at[(lax.axis_index("xh") ^ side) * 8 + g]))
    for copy in started:
        copy.wait()


def arrange_kernel(own, par, out):
    where = here()
    for z in range(NZ):
        for other in range(2):
            for side in range(2):
                out[weight_rows(where, z, other, side), :] = (own, par)[other][z, side]


def self_out_kernel(share, att, weights, out):
    acc = share[...].astype(f32)
    for g in range(8):
        both = jnp.concatenate([att[g], att[8 + g]], axis=1)
        acc += dot(both, weights[g * 256 : (g + 1) * 256, :])
    out[...] = acc.astype(bf16)


def deal_near(block):
    quarters = block.reshape(4, 64, 128)
    near = lax.axis_index(("zl", "core"))
    got = [lax.dynamic_index_in_dim(quarters, near, 0, keepdims=False)]
    for m in (1, 2, 3):
        piece = lax.dynamic_index_in_dim(quarters, near ^ m, 0, keepdims=False)
        got.append(lax.ppermute(piece, ("zl", "core"), [(i, i ^ m) for i in range(4)]))
    got = jnp.stack(got)
    return jnp.concatenate([lax.dynamic_index_in_dim(got, near ^ q, 0, keepdims=False) for q in range(4)], axis=1)


def deal_far(block):
    pairs = [
        ((share * 4 + i) * 8 + group, (group * 4 + i) * 8 + share)
        for share in range(8)
        for i in range(4)
        for group in range(8)
    ]
    return lax.ppermute(block, ALL, pairs)


def per_device(
    hidden_in,
    norm_gains,
    w_cross_query,
    w_cross_out,
    w_self_qkv,
    w_self_out,
    nbr_kv,
    nbr_count,
    nbr_source,
    span_order,
):
    rows, width = hidden_in.shape
    g = lax.axis_index(GROUP)
    y = lax.axis_index("y")
    vmem = pltpu.VMEM
    sem = pltpu.SemaphoreType.DMA

    nbr = nbr_kv[0, 0]
    nbr_got = [
        shift(lax.dynamic_index_in_dim(nbr, (y + k) % 4, 0, keepdims=False), "y", k, 4) for k in (1, 2, 3)
    ]
    first = jnp.stack([w_cross_query, jnp.concatenate([w_cross_out[:128], w_cross_out[128:]], axis=1)])
    first = jnp.concatenate([first, swap_xh(first)], axis=0)
    qkv_own = w_self_qkv.transpose(1, 0, 2)
    qkv_other = swap_xh(qkv_own)
    near = deal_near(w_self_out)
    first, nbr_got, near = lax.optimization_barrier((first, nbr_got, near))
    start = gather_start(first)
    hidden = after(hidden_in, start[1])
    normed = call(norm_kernel, sds((rows, width)), [VMEM] * 2, VMEM, [], 10_000_000, 4_000_000)(hidden, norm_gains)
    hidden_share = lax.dynamic_slice_in_dim(hidden, g * 512, 512, 1)
    dealt = deal_far(near)
    qkv_other = after(qkv_other, normed)
    late_own = lax.all_gather(jnp.concatenate([qkv_own, qkv_other], axis=0), Z, axis=0, tiled=False)
    start, normed, hidden_share, dealt = lax.optimization_barrier((start, normed, hidden_share, dealt))
    first_own = gather_end(start)
    wso = jnp.concatenate([dealt[None], swap_xh(dealt)[None]], axis=0)
    first_par = [swap_cores(p) for p in first_own]
    first_par, wso = lax.optimization_barrier((first_par, wso))
    wso_own = lax.all_gather(wso, Z, axis=0, tiled=False)
    terms = call(
        cross_kernel,
        [sds((rows, 512))] * 8,
        [SMEM] * 2 + [VMEM] + [ANY] * 22,
        [VMEM] * 8,
        [
            vmem((32, 2, 128, 256), bf16),
            vmem((4, 3, 64, 512), bf16),
            vmem((rows, 256), bf16),
            sem((36,)),
        ],
        1_200_000_000,
        10_000_000,
    )(nbr_source, nbr_count, normed, nbr, *nbr_got, *first_own, *first_par)

    got = [shift_group(term, dy, dx) for term, (dy, dx) in zip(terms[1:], PEERS)]
    mid_share = call(sum_kernel, sds((rows, 512)), [VMEM] * 9, VMEM, [], 2_000_000, 4_000_000)(
        hidden_share, terms[0], *got
    )
    late_own, mid_share = lax.optimization_barrier((late_own, mid_share))
    late_par = swap_cores(late_own)
    mids = [mid_share] + [shift_group(mid_share, dy, dx) for dy, dx in PEERS]
    keep, send = call(
        qkv_kernel,
        [sds((3, rows, HD))] * 2,
        [VMEM] * 11,
        [VMEM] * 2,
        [vmem((rows, width), bf16), vmem((rows, 256), bf16)],
        1_600_000_000,
        11_000_000,
    )(norm_gains, late_own, late_par, *mids)

    keep, send, wso_own = lax.optimization_barrier((keep, send, wso_own))
    both = jnp.concatenate([keep, swap_xh(send)], axis=1)
    kv = both[1:]
    query = jnp.stack([both[0], swap_cores(both[0])])
    part = functools.partial(attention_part, order=span_order, query=query)
    start = gather_start(kv)
    state = part((0,), state=[], pieces=[kv])
    wso_par = swap_cores(wso_own)
    weights = call(arrange_kernel, sds((2048, 512)), [VMEM] * 2, VMEM, [], 1_000_000, 4_000_000)(wso_own, wso_par)
    start, state, weights = lax.optimization_barrier((start, state, weights))
    kv, l1, l2, l3, r4, l4, r3, r2, r1 = gather_end(start)
    state = part((1, 7, 2, 6), state=[state], pieces=[l1, r1, l2, r2])
    l3, r3, l4, r4, state = lax.optimization_barrier((l3, r3, l4, r4, state))
    state = part((3, 5, 4), state=[state], pieces=[l3, r3, r4, l4])
    heads = call(
        merge_kernel,
        sds((16, rows, HD)),
        [VMEM, VMEM],
        ANY,
        [vmem((2, rows, HD), bf16), sem((16,))],
        1_000_000,
        2_000_000,
    )(state[0], swap_cores(state[1]))
    self_all = lax.all_to_all(heads, ("xh",) + GROUP, 0, 0, tiled=True)
    return call(self_out_kernel, sds((rows, 512)), [VMEM] * 3, VMEM, [], 600_000_000, 4_000_000)(
        mid_share, self_all, weights
    )


def solution(mesh):
    fine = Mesh(mesh.devices.reshape(2, 4, 2, 2, 4, 2), ALL)
    in_specs = (
        P(CTX, None),
        P(),
        P(CTX, GROUP),
        P(GROUP, CTX),
        P(CTX, None, GROUP),
        P(GROUP, CTX),
        P(CTX, "y", None, None, None, "xl"),
        P(CTX),
        P(CTX, None),
        P(),
    )
    return jax.shard_map(
        per_device, mesh=fine, in_specs=in_specs, out_specs=P(CTX, GROUP), check_vma=False
    )
```

```python
import functools
import math

import jax
import jax.numpy as jnp
from jax import lax
from jax.experimental import pallas as pl
from jax.experimental.pallas import tpu as pltpu
from jax.sharding import Mesh
from jax.sharding import PartitionSpec as P

HD = 128
SPAN = 64
epsilon = 1e-05
far_below = -1e30
NZ = 8

VMEM = pl.BlockSpec(memory_space=pltpu.VMEM)
SMEM = pl.BlockSpec(memory_space=pltpu.SMEM)
ANY = pl.BlockSpec(memory_space=pl.ANY)
f32 = jnp.float32
bf16 = jnp.bfloat16

Z = ("zh", "zl")
CTX = ("xh",) + Z + ("core",)
GROUP = ("y", "xl")
ALL = CTX + GROUP


def dot(a, b):
    return jnp.dot(a, b, preferred_element_type=f32)


def dot_t(a, b):
    return lax.dot_general(a, b, (((1,), (1,)), ((), ())), preferred_element_type=f32)


def call(kernel, out_shape, in_specs, out_specs, scratch, flops, nbytes):
    return pl.pallas_call(
        kernel,
        out_shape=out_shape,
        in_specs=in_specs,
        out_specs=out_specs,
        scratch_shapes=scratch,
        compiler_params=pltpu.CompilerParams(vmem_limit_bytes=16 * 1024 * 1024),
        cost_estimate=pl.CostEstimate(flops=flops, bytes_accessed=nbytes, transcendentals=0),
    )


def sds(shape, dtype=bf16):
    return jax.ShapeDtypeStruct(shape, dtype)


def after(x, *earlier):
    return lax.optimization_barrier((x,) + earlier)[0]


def shift(x, axis, by, size):
    return lax.ppermute(x, axis, [(i, (i + by) % size) for i in range(size)])


def swap_cores(x):
    return shift(x, "core", 1, 2)


def swap_xh(x):
    return shift(x, "xh", 1, 2)


def gather_start(x):
    return x, shift(x, Z, 1, NZ), shift(x, Z, -1, NZ), shift(x, Z, 2, NZ), shift(x, Z, -2, NZ)


def gather_end(start):
    x, r1, l1, r2, l2 = start
    r3, l3 = shift(r1, Z, 2, NZ), shift(l1, Z, -2, NZ)
    cut = x.shape[0] // 2
    r4, l4 = shift(r2[:cut], Z, 2, NZ), shift(l2[cut:], Z, -2, NZ)
    return [x, l1, l2, l3, r4, l4, r3, r2, r1]


def shift_group(x, dy, dx):
    pairs = [(y * 2 + xl, (y + dy) % 4 * 2 + (xl ^ dx)) for y in range(4) for xl in range(2)]
    return lax.ppermute(x, GROUP, pairs)


PEERS = ((1, 0), (3, 0), (0, 1), (1, 1), (3, 1), (2, 0), (2, 1))


def here():
    return tuple(lax.axis_index(a) for a in ("xh", Z, "core", "y", "xl"))


def peer_group(where, dy, dx):
    return lax.rem(where[3] + dy, 4) * 2 + (where[4] ^ dx)


def block_of(where, zz, other, side):
    return (where[0] ^ side) * 16 + zz * 2 + (where[2] ^ other)


class Copies:
    def __init__(self, sems):
        self.sems = sems
        self.used = 0

    def start(self, source, target):
        copy = pltpu.make_async_copy(source, target, self.sems.at[self.used])
        self.used += 1
        copy.start()
        return copy


def norm_kernel(hidden, gain, out):
    values = hidden[...].astype(f32)
    row_scale = lax.rsqrt(jnp.mean(values * values, axis=1, keepdims=True) + epsilon)
    for b in range(32):
        cols = slice(b * 128, (b + 1) * 128)
        block = hidden[:, cols].astype(f32)
        out[:, cols] = (block * row_scale * gain[:1, cols]).astype(bf16)


def cross_kernel(source, count, normed, nbr0, nbr1, nbr2, nbr3, *rest):
    pieces = (rest[:9], rest[9:18])
    outs, (weights, nbr, mixed_all, sems) = rest[18:26], rest[26:]
    copies = Copies(sems)
    where = here()
    y = where[3]
    started = []
    for distance in range(NZ):
        zz = lax.rem(where[1] + distance, NZ)
        for other in range(2):
            for side in range(2):
                if distance == 4:
                    piece = pieces[other][4 + side]
                else:
                    piece = pieces[other][distance if distance < 4 else distance + 1].at[pl.ds(side * 2, 2)]
                started.append(copies.start(piece, weights.at[block_of(where, zz, other, side)]))
    nbr_copies = [copies.start(nbr0.at[y], nbr.at[y])]
    for k, ref in ((1, nbr1), (2, nbr2), (3, nbr3)):
        nbr_copies.append(copies.start(ref, nbr.at[lax.rem(y + 4 - k, 4)]))
    for copy in started:
        copy.wait()
    acc = jnp.zeros((normed.shape[0], 256), f32)
    for c in range(0, 32, 2):
        right = jnp.concatenate([weights[c, 0], weights[c + 1, 0]], axis=0)
        acc += dot(normed[:, c * 128 : (c + 2) * 128], right)
    for copy in nbr_copies:
        copy.wait()
    query = acc.astype(bf16)
    scale = 1.0 / math.sqrt(HD)
    lanes = lax.broadcasted_iota(jnp.int32, (SPAN, 128), 1)
    chosen = [source[i // 2, i % 2] for i in range(8)]
    for s in range(4):
        slots = []
        for j in range(2):
            i = s * 2 + j
            rank = jnp.int32(0)
            for k in range(s * 2):
                rank = rank + (chosen[k] == chosen[i]).astype(jnp.int32)
            slots.append((chosen[i], rank))
        alive = lanes < count[s] * 64
        for h in range(2):
            kcols = slice(2 * h * HD, (2 * h + 1) * HD)
            vcols = slice((2 * h + 1) * HD, (2 * h + 2) * HD)
            keys = jnp.concatenate([nbr[e, r, :, kcols] for e, r in slots], axis=0)
            vals = jnp.concatenate([nbr[e, r, :, vcols] for e, r in slots], axis=0)
            part = query[s * SPAN : (s + 1) * SPAN, h * HD : (h + 1) * HD]
            scores = jnp.where(alive, dot_t(part, keys) * scale, far_below)
            top = jnp.max(scores, axis=1, keepdims=True)
            exps = jnp.exp(scores - top)
            total = jnp.sum(exps, axis=1, keepdims=True)
            mixed = dot(exps.astype(bf16), vals) / total
            mixed_all[s * SPAN : (s + 1) * SPAN, h * HD : (h + 1) * HD] = mixed.astype(bf16)
    att = mixed_all[...]
    for out, (dy, dx) in zip(outs, ((0, 0),) + PEERS):
        first = peer_group(where, dy, dx) * 4
        for pair in range(2):
            blocks = [weights[first + pair * 2 + i, 1] for i in range(2)]
            upper = jnp.concatenate([block[:, :128] for block in blocks], axis=1)
            lower = jnp.concatenate([block[:, 128:] for block in blocks], axis=1)
            term = dot(att, jnp.concatenate([upper, lower], axis=0))
            out[:, pair * 256 : (pair + 1) * 256] = term.astype(bf16)


def weight_rows(where, zz, other, side):
    return pl.ds(pl.multiple_of(block_of(where, zz, other, side) * 64, 64), 64)


def sum_kernel(share, *rest):
    terms, mid = rest[:8], rest[8]
    acc = terms[0][...].astype(f32)
    for term in terms[1:]:
        acc += term[...].astype(f32)
    mid[...] = (share[...].astype(f32) + acc).astype(bf16)


def qkv_kernel(gain, own, par, *rest):
    mids, (keep, send, normed, proj) = rest[:8], rest[8:]
    where = here()
    xh = where[0]
    rows = mids[0].shape[0]
    squares = jnp.zeros((rows, 512), f32)
    for mid in mids:
        values = mid[...].astype(f32)
        squares += values * values
    row_scale = lax.rsqrt(jnp.sum(squares, axis=1, keepdims=True) * (1.0 / 4096) + epsilon)
    for mid, (dy, dx) in zip(mids, ((0, 0),) + PEERS):
        first = peer_group(where, 4 - dy, dx) * 512
        for j in range(4):
            cols = pl.ds(pl.multiple_of(first + j * 128, 128), 128)
            block = mid[:, j * 128 : (j + 1) * 128].astype(f32)
            normed[:, cols] = (block * row_scale * gain[1:2, cols]).astype(bf16)
    for t in range(3):
        acc = jnp.zeros((rows, 256), f32)
        for z in range(NZ):
            for other in range(2):
                left, right = [], []
                for side in range(2):
                    owner = block_of(where, z, other, side)
                    left.append(normed[:, pl.ds(pl.multiple_of(owner * 128, 128), 128)])
                    right.append((own, par)[other][z, side * 3 + t])
                acc += dot(jnp.concatenate(left, axis=1), jnp.concatenate(right, axis=0))
        if t == 0:
            acc = acc * (math.log2(math.e) / math.sqrt(HD))
        proj[...] = acc.astype(bf16)
        keep[t] = proj[:, pl.ds(pl.multiple_of(xh * 128, 128), 128)]
        send[t] = proj[:, pl.ds(pl.multiple_of((1 - xh) * 128, 128), 128)]


def join(left, right):
    top = jnp.maximum(left[1], right[1])
    fade_left, fade_right = jnp.exp2(left[1] - top), jnp.exp2(right[1] - top)
    return (
        left[0] * fade_left + right[0] * fade_right,
        top,
        left[2] * fade_left + right[2] * fade_right,
    )


def attention_kernel(distances, order, query, *rest):
    first = distances[0] == 0
    where = here()
    if not first:
        state_in, rest = rest[0], rest[1:]
    pieces, (state_out, k_places, q_places) = rest[:-3], rest[-3:]
    n = query.shape[1]
    rows = lax.broadcasted_iota(jnp.int32, (SPAN, 1), 0)
    lanes = lax.broadcasted_iota(jnp.int32, (1, 256), 1)
    right = lax.broadcasted_iota(jnp.int32, (n, HD), 1)
    span_of, within = lanes // SPAN, lanes % SPAN
    for i, distance in enumerate(distances):
        for side in range(2):
            c = block_of(where, lax.rem(where[1] + distance, NZ), 0, side)
            place = jnp.zeros((1, 256), jnp.int32)
            for s in range(4):
                place = jnp.where(span_of == s, order[c * 4 + s], place)
            k_places[i : i + 1, side * 256 : (side + 1) * 256] = place * SPAN + within
    for core in range(2):
        for side in range(2):
            c = block_of(where, where[1], core, side)
            for s in range(4):
                begin = (side * 4 + s) * SPAN
                q_places[core, begin : begin + SPAN, :] = order[c * 4 + s] * SPAN + rows

    def one_core(core, carry):
        top = jnp.full((n, 1), far_below, f32)
        total = jnp.zeros((n, 1), f32)
        mixed = jnp.zeros((n, HD), f32)
        places = q_places[core]
        rows_here = query[core]
        for i in range(len(distances)):
            if distances[i] == 4:
                keys, vals = pieces[i][0], pieces[i + 1][0]
            else:
                keys, vals = pieces[i][0], pieces[i][1]
            scores = dot_t(rows_here, keys)
            scores = jnp.where(k_places[i : i + 1, :] <= places, scores, far_below)
            new_top = jnp.maximum(top, jnp.max(scores, axis=1, keepdims=True))
            exps = jnp.exp2(scores - new_top)
            fade = jnp.exp2(top - new_top)
            total = total * fade + jnp.sum(exps, axis=1, keepdims=True)
            mixed = mixed * fade + dot(exps.astype(bf16), vals)
            top = new_top
        state = (mixed, jnp.broadcast_to(top, (n, HD)), jnp.broadcast_to(total, (n, HD)))
        if not first:
            state = join(state, [state_in[core, :, i * HD : (i + 1) * HD] for i in range(3)])
        for i in range(3):
            state_out[core, :, i * HD : (i + 1) * HD] = state[i]
        return carry

    lax.fori_loop(0, 2, one_core, 0)


def attention_part(distances, order, query, state, pieces):
    n = query.shape[1]
    return call(
        functools.partial(attention_kernel, distances),
        sds((2, n, 3 * HD), f32),
        [SMEM] + [VMEM] * (1 + len(state) + len(pieces)),
        VMEM,
        [pltpu.VMEM((8, n), jnp.int32), pltpu.VMEM((2, n, 1), jnp.int32)],
        280_000_000 * len(distances),
        500_000 * len(distances),
    )(order, query, *state, *pieces)


def merge_kernel(own, par, out, halves, sems):
    mixed, _, total = join(
        [own[:, i * HD : (i + 1) * HD] for i in range(3)], [par[:, i * HD : (i + 1) * HD] for i in range(3)]
    )
    mixed = mixed / total
    copies = Copies(sems)
    started = []
    n = halves.shape[1]
    for side in range(2):
        halves[side] = mixed[side * n : (side + 1) * n].astype(bf16)
        for g in range(8):
            started.append(copies.start(halves.at[side], out.at[(lax.axis_index("xh") ^ side) * 8 + g]))
    for copy in started:
        copy.wait()


def arrange_kernel(own, par, out):
    where = here()
    for z in range(NZ):
        for other in range(2):
            for side in range(2):
                out[weight_rows(where, z, other, side), :] = (own, par)[other][z, side]


def self_out_kernel(share, att, weights, out):
    acc = share[...].astype(f32)
    for g in range(8):
        both = jnp.concatenate([att[g], att[8 + g]], axis=1)
        acc += dot(both, weights[g * 256 : (g + 1) * 256, :])
    out[...] = acc.astype(bf16)


def deal_near(block):
    quarters = block.reshape(4, 64, 128)
    near = lax.axis_index(("zl", "core"))
    got = [lax.dynamic_index_in_dim(quarters, near, 0, keepdims=False)]
    for m in (1, 2, 3):
        piece = lax.dynamic_index_in_dim(quarters, near ^ m, 0, keepdims=False)
        got.append(lax.ppermute(piece, ("zl", "core"), [(i, i ^ m) for i in range(4)]))
    got = jnp.stack(got)
    return jnp.concatenate([lax.dynamic_index_in_dim(got, near ^ q, 0, keepdims=False) for q in range(4)], axis=1)


def deal_far(block):
    pairs = [
        ((share * 4 + i) * 8 + group, (group * 4 + i) * 8 + share)
        for share in range(8)
        for i in range(4)
        for group in range(8)
    ]
    return lax.ppermute(block, ALL, pairs)


def per_device(
    hidden_in,
    norm_gains,
    w_cross_query,
    w_cross_out,
    w_self_qkv,
    w_self_out,
    nbr_kv,
    nbr_count,
    nbr_source,
    span_order,
):
    rows, width = hidden_in.shape
    g = lax.axis_index(GROUP)
    y = lax.axis_index("y")
    vmem = pltpu.VMEM
    sem = pltpu.SemaphoreType.DMA

    first = jnp.stack([w_cross_query, jnp.concatenate([w_cross_out[:128], w_cross_out[128:]], axis=1)])
    first = jnp.concatenate([first, swap_xh(first)], axis=0)
    near = deal_near(w_self_out)
    first, near = lax.optimization_barrier((first, near))
    start = gather_start(first)
    hidden, near, _ = lax.optimization_barrier((hidden_in, near, start[1]))
    normed = call(norm_kernel, sds((rows, width)), [VMEM] * 2, VMEM, [], 10_000_000, 4_000_000)(hidden, norm_gains)
    hidden_share = lax.dynamic_slice_in_dim(hidden, g * 512, 512, 1)
    dealt = deal_far(near)
    start, normed, hidden_share = lax.optimization_barrier((start, normed, hidden_share))
    first_own = gather_end(start)
    nbr = after(nbr_kv[0, 0], start)
    nbr_got = [
        shift(lax.dynamic_index_in_dim(nbr, (y + k) % 4, 0, keepdims=False), "y", k, 4) for k in (1, 2, 3)
    ]
    qkv_own = w_self_qkv.transpose(1, 0, 2)
    qkv_other = swap_xh(after(qkv_own, normed))
    qkv_other, *_ = lax.optimization_barrier((qkv_other, *first_own[3:7]))
    late_own = lax.all_gather(jnp.concatenate([qkv_own, qkv_other], axis=0), Z, axis=0, tiled=False)
    first_par = [swap_cores(p) for p in first_own]
    first_par, dealt = lax.optimization_barrier((first_par, dealt))
    wso_other = swap_xh(dealt)
    terms = call(
        cross_kernel,
        [sds((rows, 512))] * 8,
        [SMEM] * 2 + [VMEM] + [ANY] * 22,
        [VMEM] * 8,
        [
            vmem((32, 2, 128, 256), bf16),
            vmem((4, 3, 64, 512), bf16),
            vmem((rows, 256), bf16),
            sem((36,)),
        ],
        1_200_000_000,
        10_000_000,
    )(nbr_source, nbr_count, normed, nbr, *nbr_got, *first_own, *first_par)

    terms, wso_other = lax.optimization_barrier((terms, wso_other))
    wso = jnp.concatenate([dealt[None], wso_other[None]], axis=0)
    got = [shift_group(term, dy, dx) for term, (dy, dx) in zip(terms[1:], PEERS)]
    mid_share = call(sum_kernel, sds((rows, 512)), [VMEM] * 9, VMEM, [], 2_000_000, 4_000_000)(
        hidden_share, terms[0], *got
    )
    late_own, mid_share = lax.optimization_barrier((late_own, mid_share))
    mids = [mid_share] + [shift_group(mid_share, dy, dx) for dy, dx in PEERS]
    late_par = swap_cores(late_own)
    wso_own = lax.all_gather(after(wso, late_own), Z, axis=0, tiled=False)
    keep, send = call(
        qkv_kernel,
        [sds((3, rows, HD))] * 2,
        [VMEM] * 11,
        [VMEM] * 2,
        [vmem((rows, width), bf16), vmem((rows, 256), bf16)],
        1_600_000_000,
        11_000_000,
    )(norm_gains, late_own, late_par, *mids)

    keep, send, wso_own = lax.optimization_barrier((keep, send, wso_own))
    both = jnp.concatenate([keep, swap_xh(send)], axis=1)
    kv = both[1:]
    query = jnp.stack([both[0], swap_cores(both[0])])
    part = functools.partial(attention_part, order=span_order, query=query)
    r1, l1 = shift(kv, Z, 1, NZ), shift(kv, Z, -1, NZ)
    state = part((0,), state=[], pieces=[kv])
    wso_par = swap_cores(wso_own)
    weights = call(arrange_kernel, sds((2048, 512)), [VMEM] * 2, VMEM, [], 1_000_000, 4_000_000)(wso_own, wso_par)
    r2, l2 = shift(r1, Z, 1, NZ), shift(l1, Z, -1, NZ)
    r2, l2, state, weights = lax.optimization_barrier((r2, l2, state, weights))
    r3, l3 = shift(r2, Z, 1, NZ), shift(l2, Z, -1, NZ)
    state = part((1, 7), state=[state], pieces=[l1, r1])
    r3, l3, state = lax.optimization_barrier((r3, l3, state))
    r4, l4 = shift(r3[:1], Z, 1, NZ), shift(l3[1:], Z, -1, NZ)
    state = part((2, 6, 3, 5), state=[state], pieces=[l2, r2, l3, r3])
    r4, l4, state = lax.optimization_barrier((r4, l4, state))
    state = part((4,), state=[state], pieces=[r4, l4])
    heads = call(
        merge_kernel,
        sds((16, rows, HD)),
        [VMEM, VMEM],
        ANY,
        [vmem((2, rows, HD), bf16), sem((16,))],
        1_000_000,
        2_000_000,
    )(state[0], swap_cores(state[1]))
    self_all = lax.all_to_all(heads, ("xh",) + GROUP, 0, 0, tiled=True)
    return call(self_out_kernel, sds((rows, 512)), [VMEM] * 3, VMEM, [], 600_000_000, 4_000_000)(
        mid_share, self_all, weights
    )


def solution(mesh):
    fine = Mesh(mesh.devices.reshape(2, 4, 2, 2, 4, 2), ALL)
    in_specs = (
        P(CTX, None),
        P(),
        P(CTX, GROUP),
        P(GROUP, CTX),
        P(CTX, None, GROUP),
        P(GROUP, CTX),
        P(CTX, "y", None, None, None, "xl"),
        P(CTX),
        P(CTX, None),
        P(),
    )
    return jax.shard_map(
        per_device, mesh=fine, in_specs=in_specs, out_specs=P(CTX, GROUP), check_vma=False
    )
```

```python
import functools
import math

import jax
import jax.numpy as jnp
from jax import lax
from jax.experimental import pallas as pl
from jax.experimental.pallas import tpu as pltpu
from jax.sharding import Mesh
from jax.sharding import PartitionSpec as P

HD = 128
SPAN = 64
epsilon = 1e-05
far_below = -1e30
NZ = 8

VMEM = pl.BlockSpec(memory_space=pltpu.VMEM)
SMEM = pl.BlockSpec(memory_space=pltpu.SMEM)
ANY = pl.BlockSpec(memory_space=pl.ANY)
f32 = jnp.float32
bf16 = jnp.bfloat16

Z = ("zh", "zl")
CTX = ("xh",) + Z + ("core",)
GROUP = ("y", "xl")
ALL = CTX + GROUP


def dot(a, b):
    return jnp.dot(a, b, preferred_element_type=f32)


def dot_t(a, b):
    return lax.dot_general(a, b, (((1,), (1,)), ((), ())), preferred_element_type=f32)


def call(kernel, out_shape, in_specs, out_specs, scratch, flops, nbytes):
    return pl.pallas_call(
        kernel,
        out_shape=out_shape,
        in_specs=in_specs,
        out_specs=out_specs,
        scratch_shapes=scratch,
        compiler_params=pltpu.CompilerParams(vmem_limit_bytes=16 * 1024 * 1024),
        cost_estimate=pl.CostEstimate(flops=flops, bytes_accessed=nbytes, transcendentals=0),
    )


def sds(shape, dtype=bf16):
    return jax.ShapeDtypeStruct(shape, dtype)


def after(x, *earlier):
    return lax.optimization_barrier((x,) + earlier)[0]


def shift(x, axis, by, size):
    return lax.ppermute(x, axis, [(i, (i + by) % size) for i in range(size)])


def swap_cores(x):
    return shift(x, "core", 1, 2)


def swap_xh(x):
    return shift(x, "xh", 1, 2)


def gather_start(x):
    return x, shift(x, Z, 1, NZ), shift(x, Z, -1, NZ), shift(x, Z, 2, NZ), shift(x, Z, -2, NZ)


def gather_end(start):
    x, r1, l1, r2, l2 = start
    r3, l3 = shift(r1, Z, 2, NZ), shift(l1, Z, -2, NZ)
    cut = x.shape[0] // 2
    r4, l4 = shift(r2[:cut], Z, 2, NZ), shift(l2[cut:], Z, -2, NZ)
    return [x, l1, l2, l3, r4, l4, r3, r2, r1]


def shift_group(x, dy, dx):
    pairs = [(y * 2 + xl, (y + dy) % 4 * 2 + (xl ^ dx)) for y in range(4) for xl in range(2)]
    return lax.ppermute(x, GROUP, pairs)


PEERS = ((1, 0), (3, 0), (0, 1), (1, 1), (3, 1), (2, 0), (2, 1))


def here():
    return tuple(lax.axis_index(a) for a in ("xh", Z, "core", "y", "xl"))


def peer_group(where, dy, dx):
    return lax.rem(where[3] + dy, 4) * 2 + (where[4] ^ dx)


def block_of(where, zz, other, side):
    return (where[0] ^ side) * 16 + zz * 2 + (where[2] ^ other)


class Copies:
    def __init__(self, sems):
        self.sems = sems
        self.used = 0

    def start(self, source, target):
        copy = pltpu.make_async_copy(source, target, self.sems.at[self.used])
        self.used += 1
        copy.start()
        return copy


def norm_kernel(hidden, gain, out):
    values = hidden[...].astype(f32)
    row_scale = lax.rsqrt(jnp.mean(values * values, axis=1, keepdims=True) + epsilon)
    for b in range(32):
        cols = slice(b * 128, (b + 1) * 128)
        block = hidden[:, cols].astype(f32)
        out[:, cols] = (block * row_scale * gain[:1, cols]).astype(bf16)


def cross_kernel(source, count, normed, nbr0, nbr1, nbr2, nbr3, *rest):
    pieces = (rest[:9], rest[9:18])
    outs, (weights, nbr, mixed_all, sems) = rest[18:26], rest[26:]
    copies = Copies(sems)
    where = here()
    y = where[3]
    started = []
    for distance in range(NZ):
        zz = lax.rem(where[1] + distance, NZ)
        for other in range(2):
            for side in range(2):
                if distance == 4:
                    piece = pieces[other][4 + side]
                else:
                    piece = pieces[other][distance if distance < 4 else distance + 1].at[pl.ds(side * 2, 2)]
                started.append(copies.start(piece, weights.at[block_of(where, zz, other, side)]))
    nbr_copies = [copies.start(nbr0.at[y], nbr.at[y])]
    for k, ref in ((1, nbr1), (2, nbr2), (3, nbr3)):
        nbr_copies.append(copies.start(ref, nbr.at[lax.rem(y + 4 - k, 4)]))
    for copy in started:
        copy.wait()
    acc = jnp.zeros((normed.shape[0], 256), f32)
    for c in range(0, 32, 2):
        right = jnp.concatenate([weights[c, 0], weights[c + 1, 0]], axis=0)
        acc += dot(normed[:, c * 128 : (c + 2) * 128], right)
    for copy in nbr_copies:
        copy.wait()
    query = acc.astype(bf16)
    scale = 1.0 / math.sqrt(HD)
    lanes = lax.broadcasted_iota(jnp.int32, (SPAN, 128), 1)
    chosen = [source[i // 2, i % 2] for i in range(8)]
    for s in range(4):
        slots = []
        for j in range(2):
            i = s * 2 + j
            rank = jnp.int32(0)
            for k in range(s * 2):
                rank = rank + (chosen[k] == chosen[i]).astype(jnp.int32)
            slots.append((chosen[i], rank))
        alive = lanes < count[s] * 64
        for h in range(2):
            kcols = slice(2 * h * HD, (2 * h + 1) * HD)
            vcols = slice((2 * h + 1) * HD, (2 * h + 2) * HD)
            keys = jnp.concatenate([nbr[e, r, :, kcols] for e, r in slots], axis=0)
            vals = jnp.concatenate([nbr[e, r, :, vcols] for e, r in slots], axis=0)
            part = query[s * SPAN : (s + 1) * SPAN, h * HD : (h + 1) * HD]
            scores = jnp.where(alive, dot_t(part, keys) * scale, far_below)
            top = jnp.max(scores, axis=1, keepdims=True)
            exps = jnp.exp(scores - top)
            total = jnp.sum(exps, axis=1, keepdims=True)
            mixed = dot(exps.astype(bf16), vals) / total
            mixed_all[s * SPAN : (s + 1) * SPAN, h * HD : (h + 1) * HD] = mixed.astype(bf16)
    att = mixed_all[...]
    for out, (dy, dx) in zip(outs, ((0, 0),) + PEERS):
        first = peer_group(where, dy, dx) * 4
        for pair in range(2):
            blocks = [weights[first + pair * 2 + i, 1] for i in range(2)]
            upper = jnp.concatenate([block[:, :128] for block in blocks], axis=1)
            lower = jnp.concatenate([block[:, 128:] for block in blocks], axis=1)
            term = dot(att, jnp.concatenate([upper, lower], axis=0))
            out[:, pair * 256 : (pair + 1) * 256] = term.astype(bf16)


def weight_rows(where, zz, other, side):
    return pl.ds(pl.multiple_of(block_of(where, zz, other, side) * 64, 64), 64)


def sum_kernel(share, *rest):
    terms, mid = rest[:8], rest[8]
    acc = terms[0][...].astype(f32)
    for term in terms[1:]:
        acc += term[...].astype(f32)
    mid[...] = (share[...].astype(f32) + acc).astype(bf16)


def qkv_kernel(gain, own, par, *rest):
    mids, (keep, send, normed, proj) = rest[:8], rest[8:]
    where = here()
    xh = where[0]
    rows = mids[0].shape[0]
    squares = jnp.zeros((rows, 512), f32)
    for mid in mids:
        values = mid[...].astype(f32)
        squares += values * values
    row_scale = lax.rsqrt(jnp.sum(squares, axis=1, keepdims=True) * (1.0 / 4096) + epsilon)
    for mid, (dy, dx) in zip(mids, ((0, 0),) + PEERS):
        first = peer_group(where, 4 - dy, dx) * 512
        for j in range(4):
            cols = pl.ds(pl.multiple_of(first + j * 128, 128), 128)
            block = mid[:, j * 128 : (j + 1) * 128].astype(f32)
            normed[:, cols] = (block * row_scale * gain[1:2, cols]).astype(bf16)
    for t in range(3):
        acc = jnp.zeros((rows, 256), f32)
        for z in range(NZ):
            for other in range(2):
                left, right = [], []
                for side in range(2):
                    owner = block_of(where, z, other, side)
                    left.append(normed[:, pl.ds(pl.multiple_of(owner * 128, 128), 128)])
                    right.append((own, par)[other][z, side * 3 + t])
                acc += dot(jnp.concatenate(left, axis=1), jnp.concatenate(right, axis=0))
        if t == 0:
            acc = acc * (math.log2(math.e) / math.sqrt(HD))
        proj[...] = acc.astype(bf16)
        keep[t] = proj[:, pl.ds(pl.multiple_of(xh * 128, 128), 128)]
        send[t] = proj[:, pl.ds(pl.multiple_of((1 - xh) * 128, 128), 128)]


def join(left, right):
    top = jnp.maximum(left[1], right[1])
    fade_left, fade_right = jnp.exp2(left[1] - top), jnp.exp2(right[1] - top)
    return (
        left[0] * fade_left + right[0] * fade_right,
        top,
        left[2] * fade_left + right[2] * fade_right,
    )


def attention_kernel(distances, order, query, *rest):
    first = distances[0] == 0
    where = here()
    if not first:
        state_in, rest = rest[0], rest[1:]
    pieces, (state_out, k_places, q_places) = rest[:-3], rest[-3:]
    n = query.shape[1]
    rows = lax.broadcasted_iota(jnp.int32, (SPAN, 1), 0)
    lanes = lax.broadcasted_iota(jnp.int32, (1, 256), 1)
    right = lax.broadcasted_iota(jnp.int32, (n, HD), 1)
    span_of, within = lanes // SPAN, lanes % SPAN
    for i, distance in enumerate(distances):
        for side in range(2):
            c = block_of(where, lax.rem(where[1] + distance, NZ), 0, side)
            place = jnp.zeros((1, 256), jnp.int32)
            for s in range(4):
                place = jnp.where(span_of == s, order[c * 4 + s], place)
            k_places[i : i + 1, side * 256 : (side + 1) * 256] = place * SPAN + within
    for core in range(2):
        for side in range(2):
            c = block_of(where, where[1], core, side)
            for s in range(4):
                begin = (side * 4 + s) * SPAN
                q_places[core, begin : begin + SPAN, :] = order[c * 4 + s] * SPAN + rows

    def one_core(core, carry):
        top = jnp.full((n, 1), far_below, f32)
        total = jnp.zeros((n, 1), f32)
        mixed = jnp.zeros((n, HD), f32)
        places = q_places[core]
        rows_here = query[core]
        for i in range(len(distances)):
            if distances[i] == 4:
                keys, vals = pieces[i][0], pieces[i + 1][0]
            else:
                keys, vals = pieces[i][0], pieces[i][1]
            scores = dot_t(rows_here, keys)
            scores = jnp.where(k_places[i : i + 1, :] <= places, scores, far_below)
            new_top = jnp.maximum(top, jnp.max(scores, axis=1, keepdims=True))
            exps = jnp.exp2(scores - new_top)
            fade = jnp.exp2(top - new_top)
            total = total * fade + jnp.sum(exps, axis=1, keepdims=True)
            mixed = mixed * fade + dot(exps.astype(bf16), vals)
            top = new_top
        state = (mixed, jnp.broadcast_to(top, (n, HD)), jnp.broadcast_to(total, (n, HD)))
        if not first:
            state = join(state, [state_in[core, :, i * HD : (i + 1) * HD] for i in range(3)])
        for i in range(3):
            state_out[core, :, i * HD : (i + 1) * HD] = state[i]
        return carry

    lax.fori_loop(0, 2, one_core, 0)


def attention_part(distances, order, query, state, pieces):
    n = query.shape[1]
    return call(
        functools.partial(attention_kernel, distances),
        sds((2, n, 3 * HD), f32),
        [SMEM] + [VMEM] * (1 + len(state) + len(pieces)),
        VMEM,
        [pltpu.VMEM((8, n), jnp.int32), pltpu.VMEM((2, n, 1), jnp.int32)],
        280_000_000 * len(distances),
        500_000 * len(distances),
    )(order, query, *state, *pieces)


def merge_kernel(own, par, out, halves, sems):
    mixed, _, total = join(
        [own[:, i * HD : (i + 1) * HD] for i in range(3)], [par[:, i * HD : (i + 1) * HD] for i in range(3)]
    )
    mixed = mixed / total
    copies = Copies(sems)
    started = []
    n = halves.shape[1]
    for side in range(2):
        halves[side] = mixed[side * n : (side + 1) * n].astype(bf16)
        for g in range(8):
            started.append(copies.start(halves.at[side], out.at[(lax.axis_index("xh") ^ side) * 8 + g]))
    for copy in started:
        copy.wait()


def arrange_kernel(own, par, out):
    where = here()
    for z in range(NZ):
        for other in range(2):
            for side in range(2):
                out[weight_rows(where, z, other, side), :] = (own, par)[other][z, side]


def self_out_kernel(share, att, weights, out):
    acc = share[...].astype(f32)
    for g in range(8):
        both = jnp.concatenate([att[g], att[8 + g]], axis=1)
        acc += dot(both, weights[g * 256 : (g + 1) * 256, :])
    out[...] = acc.astype(bf16)


def deal_near(block):
    quarters = block.reshape(4, 64, 128)
    near = lax.axis_index(("zl", "core"))
    got = [lax.dynamic_index_in_dim(quarters, near, 0, keepdims=False)]
    for m in (1, 2, 3):
        piece = lax.dynamic_index_in_dim(quarters, near ^ m, 0, keepdims=False)
        got.append(lax.ppermute(piece, ("zl", "core"), [(i, i ^ m) for i in range(4)]))
    got = jnp.stack(got)
    return jnp.concatenate([lax.dynamic_index_in_dim(got, near ^ q, 0, keepdims=False) for q in range(4)], axis=1)


def deal_far(block):
    pairs = [
        ((share * 4 + i) * 8 + group, (group * 4 + i) * 8 + share)
        for share in range(8)
        for i in range(4)
        for group in range(8)
    ]
    return lax.ppermute(block, ALL, pairs)


def per_device(
    hidden_in,
    norm_gains,
    w_cross_query,
    w_cross_out,
    w_self_qkv,
    w_self_out,
    nbr_kv,
    nbr_count,
    nbr_source,
    span_order,
):
    rows, width = hidden_in.shape
    g = lax.axis_index(GROUP)
    y = lax.axis_index("y")
    vmem = pltpu.VMEM
    sem = pltpu.SemaphoreType.DMA

    first = jnp.stack([w_cross_query, jnp.concatenate([w_cross_out[:128], w_cross_out[128:]], axis=1)])
    first = jnp.concatenate([first, swap_xh(first)], axis=0)
    near = deal_near(w_self_out)
    first, near = lax.optimization_barrier((first, near))
    start = gather_start(first)
    hidden, near, _ = lax.optimization_barrier((hidden_in, near, start[1]))
    normed = call(norm_kernel, sds((rows, width)), [VMEM] * 2, VMEM, [], 10_000_000, 4_000_000)(hidden, norm_gains)
    hidden_share = lax.dynamic_slice_in_dim(hidden, g * 512, 512, 1)
    dealt = deal_far(near)
    nbr = after(nbr_kv[0, 0], first)
    nbr_got = [
        shift(lax.dynamic_index_in_dim(nbr, (y + k) % 4, 0, keepdims=False), "y", k, 4) for k in (1, 2, 3)
    ]
    qkv_own = after(w_self_qkv.transpose(1, 0, 2), first)
    qkv_other = swap_xh(qkv_own)
    start, normed, hidden_share, dealt, qkv_other, nbr_got = lax.optimization_barrier(
        (start, normed, hidden_share, dealt, qkv_other, nbr_got)
    )
    first_own = gather_end(start)
    qkv_other, *_ = lax.optimization_barrier((qkv_other, *first_own[3:7]))
    late_own = lax.all_gather(jnp.concatenate([qkv_own, qkv_other], axis=0), Z, axis=0, tiled=False)
    first_par = [swap_cores(p) for p in first_own]
    first_par, dealt = lax.optimization_barrier((first_par, dealt))
    wso_other = swap_xh(dealt)
    terms = call(
        cross_kernel,
        [sds((rows, 512))] * 8,
        [SMEM] * 2 + [VMEM] + [ANY] * 22,
        [VMEM] * 8,
        [
            vmem((32, 2, 128, 256), bf16),
            vmem((4, 3, 64, 512), bf16),
            vmem((rows, 256), bf16),
            sem((36,)),
        ],
        1_200_000_000,
        10_000_000,
    )(nbr_source, nbr_count, normed, nbr, *nbr_got, *first_own, *first_par)

    terms, wso_other = lax.optimization_barrier((terms, wso_other))
    wso = jnp.concatenate([dealt[None], wso_other[None]], axis=0)
    got = [shift_group(term, dy, dx) for term, (dy, dx) in zip(terms[1:], PEERS)]
    mid_share = call(sum_kernel, sds((rows, 512)), [VMEM] * 9, VMEM, [], 2_000_000, 4_000_000)(
        hidden_share, terms[0], *got
    )
    late_own, mid_share = lax.optimization_barrier((late_own, mid_share))
    mids = [mid_share] + [shift_group(mid_share, dy, dx) for dy, dx in PEERS]
    late_par = swap_cores(late_own)
    wso_own = lax.all_gather(after(wso, late_own), Z, axis=0, tiled=False)
    keep, send = call(
        qkv_kernel,
        [sds((3, rows, HD))] * 2,
        [VMEM] * 11,
        [VMEM] * 2,
        [vmem((rows, width), bf16), vmem((rows, 256), bf16)],
        1_600_000_000,
        11_000_000,
    )(norm_gains, late_own, late_par, *mids)

    keep, send, wso_own = lax.optimization_barrier((keep, send, wso_own))
    both = jnp.concatenate([keep, swap_xh(send)], axis=1)
    kv = both[1:]
    query = jnp.stack([both[0], swap_cores(both[0])])
    part = functools.partial(attention_part, order=span_order, query=query)
    r1, l1 = shift(kv, Z, 1, NZ), shift(kv, Z, -1, NZ)
    state = part((0,), state=[], pieces=[kv])
    wso_par = swap_cores(wso_own)
    weights = call(arrange_kernel, sds((2048, 512)), [VMEM] * 2, VMEM, [], 1_000_000, 4_000_000)(wso_own, wso_par)
    r2, l2 = shift(r1, Z, 1, NZ), shift(l1, Z, -1, NZ)
    r2, l2, state, weights = lax.optimization_barrier((r2, l2, state, weights))
    r3, l3 = shift(r2, Z, 1, NZ), shift(l2, Z, -1, NZ)
    state = part((1, 7), state=[state], pieces=[l1, r1])
    r3, l3, state = lax.optimization_barrier((r3, l3, state))
    r4, l4 = shift(r3[:1], Z, 1, NZ), shift(l3[1:], Z, -1, NZ)
    state = part((2, 6, 3, 5), state=[state], pieces=[l2, r2, l3, r3])
    r4, l4, state = lax.optimization_barrier((r4, l4, state))
    state = part((4,), state=[state], pieces=[r4, l4])
    heads = call(
        merge_kernel,
        sds((16, rows, HD)),
        [VMEM, VMEM],
        ANY,
        [vmem((2, rows, HD), bf16), sem((16,))],
        1_000_000,
        2_000_000,
    )(state[0], swap_cores(state[1]))
    self_all = lax.all_to_all(heads, ("xh",) + GROUP, 0, 0, tiled=True)
    return call(self_out_kernel, sds((rows, 512)), [VMEM] * 3, VMEM, [], 600_000_000, 4_000_000)(
        mid_share, self_all, weights
    )


def solution(mesh):
    fine = Mesh(mesh.devices.reshape(2, 4, 2, 2, 4, 2), ALL)
    in_specs = (
        P(CTX, None),
        P(),
        P(CTX, GROUP),
        P(GROUP, CTX),
        P(CTX, None, GROUP),
        P(GROUP, CTX),
        P(CTX, "y", None, None, None, "xl"),
        P(CTX),
        P(CTX, None),
        P(),
    )
    return jax.shard_map(
        per_device, mesh=fine, in_specs=in_specs, out_specs=P(CTX, GROUP), check_vma=False
    )
```

```python
import functools
import math

import jax
import jax.numpy as jnp
from jax import lax
from jax.experimental import pallas as pl
from jax.experimental.pallas import tpu as pltpu
from jax.sharding import Mesh
from jax.sharding import PartitionSpec as P

HD = 128
SPAN = 64
epsilon = 1e-05
far_below = -1e30
NZ = 8

VMEM = pl.BlockSpec(memory_space=pltpu.VMEM)
SMEM = pl.BlockSpec(memory_space=pltpu.SMEM)
ANY = pl.BlockSpec(memory_space=pl.ANY)
f32 = jnp.float32
bf16 = jnp.bfloat16

Z = ("zh", "zl")
CTX = ("xh",) + Z + ("core",)
GROUP = ("y", "xl")
ALL = CTX + GROUP


def dot(a, b):
    return jnp.dot(a, b, preferred_element_type=f32)


def dot_t(a, b):
    return lax.dot_general(a, b, (((1,), (1,)), ((), ())), preferred_element_type=f32)


def call(kernel, out_shape, in_specs, out_specs, scratch, flops, nbytes, grant=16):
    return pl.pallas_call(
        kernel,
        out_shape=out_shape,
        in_specs=in_specs,
        out_specs=out_specs,
        scratch_shapes=scratch,
        compiler_params=pltpu.CompilerParams(vmem_limit_bytes=grant * 1024 * 1024),
        cost_estimate=pl.CostEstimate(flops=flops, bytes_accessed=nbytes, transcendentals=0),
    )


def sds(shape, dtype=bf16):
    return jax.ShapeDtypeStruct(shape, dtype)


def after(x, *earlier):
    return lax.optimization_barrier((x,) + earlier)[0]


def shift(x, axis, by, size):
    return lax.ppermute(x, axis, [(i, (i + by) % size) for i in range(size)])


def swap_cores(x):
    return shift(x, "core", 1, 2)


def swap_xh(x):
    return shift(x, "xh", 1, 2)


def gather_start(x):
    return x, shift(x, Z, 1, NZ), shift(x, Z, -1, NZ), shift(x, Z, 2, NZ), shift(x, Z, -2, NZ)


def gather_end(start):
    x, r1, l1, r2, l2 = start
    r3, l3 = shift(r1, Z, 2, NZ), shift(l1, Z, -2, NZ)
    cut = x.shape[0] // 2
    r4, l4 = shift(r2[:cut], Z, 2, NZ), shift(l2[cut:], Z, -2, NZ)
    return [x, l1, l2, l3, r4, l4, r3, r2, r1]


def shift_group(x, dy, dx):
    pairs = [(y * 2 + xl, (y + dy) % 4 * 2 + (xl ^ dx)) for y in range(4) for xl in range(2)]
    return lax.ppermute(x, GROUP, pairs)


PEERS = ((1, 0), (3, 0), (0, 1), (1, 1), (3, 1), (2, 0), (2, 1))


def here():
    return tuple(lax.axis_index(a) for a in ("xh", Z, "core", "y", "xl"))


def peer_group(where, dy, dx):
    return lax.rem(where[3] + dy, 4) * 2 + (where[4] ^ dx)


def block_of(where, zz, other, side):
    return (where[0] ^ side) * 16 + zz * 2 + (where[2] ^ other)


class Copies:
    def __init__(self, sems):
        self.sems = sems
        self.used = 0

    def start(self, source, target):
        copy = pltpu.make_async_copy(source, target, self.sems.at[self.used])
        self.used += 1
        copy.start()
        return copy


def norm_kernel(hidden, gain, out):
    values = hidden[...].astype(f32)
    row_scale = lax.rsqrt(jnp.mean(values * values, axis=1, keepdims=True) + epsilon)
    for b in range(32):
        cols = slice(b * 128, (b + 1) * 128)
        block = hidden[:, cols].astype(f32)
        out[:, cols] = (block * row_scale * gain[:1, cols]).astype(bf16)


def cross_kernel(source, count, normed, nbr0, nbr1, nbr2, nbr3, *rest):
    pieces = (rest[:9], rest[9:18])
    outs, (weights, nbr, mixed_all, sems) = rest[18:26], rest[26:]
    copies = Copies(sems)
    where = here()
    y = where[3]
    started = []
    for distance in range(NZ):
        zz = lax.rem(where[1] + distance, NZ)
        for other in range(2):
            for side in range(2):
                if distance == 4:
                    piece = pieces[other][4 + side]
                else:
                    piece = pieces[other][distance if distance < 4 else distance + 1].at[pl.ds(side * 2, 2)]
                started.append(copies.start(piece, weights.at[block_of(where, zz, other, side)]))
    nbr_copies = [copies.start(nbr0.at[y], nbr.at[y])]
    for k, ref in ((1, nbr1), (2, nbr2), (3, nbr3)):
        nbr_copies.append(copies.start(ref, nbr.at[lax.rem(y + 4 - k, 4)]))
    for copy in started:
        copy.wait()
    acc = jnp.zeros((normed.shape[0], 256), f32)
    for c in range(0, 32, 2):
        right = jnp.concatenate([weights[c, 0], weights[c + 1, 0]], axis=0)
        acc += dot(normed[:, c * 128 : (c + 2) * 128], right)
    for copy in nbr_copies:
        copy.wait()
    query = acc.astype(bf16)
    scale = 1.0 / math.sqrt(HD)
    lanes = lax.broadcasted_iota(jnp.int32, (SPAN, 128), 1)
    chosen = [source[i // 2, i % 2] for i in range(8)]
    for s in range(4):
        slots = []
        for j in range(2):
            i = s * 2 + j
            rank = jnp.int32(0)
            for k in range(s * 2):
                rank = rank + (chosen[k] == chosen[i]).astype(jnp.int32)
            slots.append((chosen[i], rank))
        alive = lanes < count[s] * 64
        for h in range(2):
            kcols = slice(2 * h * HD, (2 * h + 1) * HD)
            vcols = slice((2 * h + 1) * HD, (2 * h + 2) * HD)
            keys = jnp.concatenate([nbr[e, r, :, kcols] for e, r in slots], axis=0)
            vals = jnp.concatenate([nbr[e, r, :, vcols] for e, r in slots], axis=0)
            part = query[s * SPAN : (s + 1) * SPAN, h * HD : (h + 1) * HD]
            scores = jnp.where(alive, dot_t(part, keys) * scale, far_below)
            top = jnp.max(scores, axis=1, keepdims=True)
            exps = jnp.exp(scores - top)
            total = jnp.sum(exps, axis=1, keepdims=True)
            mixed = dot(exps.astype(bf16), vals) / total
            mixed_all[s * SPAN : (s + 1) * SPAN, h * HD : (h + 1) * HD] = mixed.astype(bf16)
    att = mixed_all[...]
    for out, (dy, dx) in zip(outs, ((0, 0),) + PEERS):
        first = peer_group(where, dy, dx) * 4
        for pair in range(2):
            blocks = [weights[first + pair * 2 + i, 1] for i in range(2)]
            upper = jnp.concatenate([block[:, :128] for block in blocks], axis=1)
            lower = jnp.concatenate([block[:, 128:] for block in blocks], axis=1)
            term = dot(att, jnp.concatenate([upper, lower], axis=0))
            out[:, pair * 256 : (pair + 1) * 256] = term.astype(bf16)


def weight_rows(where, zz, other, side):
    return pl.ds(pl.multiple_of(block_of(where, zz, other, side) * 64, 64), 64)


def sum_kernel(share, *rest):
    terms, mid = rest[:8], rest[8]
    acc = terms[0][...].astype(f32)
    for term in terms[1:]:
        acc += term[...].astype(f32)
    mid[...] = (share[...].astype(f32) + acc).astype(bf16)


def qkv_kernel(gain, own, par, *rest):
    mids, (keep, send, normed, proj) = rest[:8], rest[8:]
    where = here()
    xh = where[0]
    rows = mids[0].shape[0]
    squares = jnp.zeros((rows, 512), f32)
    for mid in mids:
        values = mid[...].astype(f32)
        squares += values * values
    row_scale = lax.rsqrt(jnp.sum(squares, axis=1, keepdims=True) * (1.0 / 4096) + epsilon)
    for mid, (dy, dx) in zip(mids, ((0, 0),) + PEERS):
        first = peer_group(where, 4 - dy, dx) * 512
        for j in range(4):
            cols = pl.ds(pl.multiple_of(first + j * 128, 128), 128)
            block = mid[:, j * 128 : (j + 1) * 128].astype(f32)
            normed[:, cols] = (block * row_scale * gain[1:2, cols]).astype(bf16)
    for t in range(3):
        acc = jnp.zeros((rows, 256), f32)
        for z in range(NZ):
            for other in range(2):
                left, right = [], []
                for side in range(2):
                    owner = block_of(where, z, other, side)
                    left.append(normed[:, pl.ds(pl.multiple_of(owner * 128, 128), 128)])
                    right.append((own, par)[other][z, side * 3 + t])
                acc += dot(jnp.concatenate(left, axis=1), jnp.concatenate(right, axis=0))
        if t == 0:
            acc = acc * (math.log2(math.e) / math.sqrt(HD))
        proj[...] = acc.astype(bf16)
        keep[t] = proj[:, pl.ds(pl.multiple_of(xh * 128, 128), 128)]
        send[t] = proj[:, pl.ds(pl.multiple_of((1 - xh) * 128, 128), 128)]


def join(left, right):
    top = jnp.maximum(left[1], right[1])
    fade_left, fade_right = jnp.exp2(left[1] - top), jnp.exp2(right[1] - top)
    return (
        left[0] * fade_left + right[0] * fade_right,
        top,
        left[2] * fade_left + right[2] * fade_right,
    )


def attention_kernel(distances, order, query, *rest):
    first = distances[0] == 0
    where = here()
    if not first:
        state_in, rest = rest[0], rest[1:]
    pieces, (state_out, k_places, q_places) = rest[:-3], rest[-3:]
    n = query.shape[1]
    rows = lax.broadcasted_iota(jnp.int32, (SPAN, 1), 0)
    lanes = lax.broadcasted_iota(jnp.int32, (1, 256), 1)
    right = lax.broadcasted_iota(jnp.int32, (n, HD), 1)
    span_of, within = lanes // SPAN, lanes % SPAN
    for i, distance in enumerate(distances):
        for side in range(2):
            c = block_of(where, lax.rem(where[1] + distance, NZ), 0, side)
            place = jnp.zeros((1, 256), jnp.int32)
            for s in range(4):
                place = jnp.where(span_of == s, order[c * 4 + s], place)
            k_places[i : i + 1, side * 256 : (side + 1) * 256] = place * SPAN + within
    for core in range(2):
        for side in range(2):
            c = block_of(where, where[1], core, side)
            for s in range(4):
                begin = (side * 4 + s) * SPAN
                q_places[core, begin : begin + SPAN, :] = order[c * 4 + s] * SPAN + rows

    def one_core(core, carry):
        top = jnp.full((n, 1), far_below, f32)
        total = jnp.zeros((n, 1), f32)
        mixed = jnp.zeros((n, HD), f32)
        places = q_places[core]
        rows_here = query[core]
        for i in range(len(distances)):
            if distances[i] == 4:
                keys, vals = pieces[i][0], pieces[i + 1][0]
            else:
                keys, vals = pieces[i][0], pieces[i][1]
            scores = dot_t(rows_here, keys)
            scores = jnp.where(k_places[i : i + 1, :] <= places, scores, far_below)
            new_top = jnp.maximum(top, jnp.max(scores, axis=1, keepdims=True))
            exps = jnp.exp2(scores - new_top)
            fade = jnp.exp2(top - new_top)
            total = total * fade + jnp.sum(exps, axis=1, keepdims=True)
            mixed = mixed * fade + dot(exps.astype(bf16), vals)
            top = new_top
        state = (mixed, jnp.broadcast_to(top, (n, HD)), jnp.broadcast_to(total, (n, HD)))
        if not first:
            state = join(state, [state_in[core, :, i * HD : (i + 1) * HD] for i in range(3)])
        for i in range(3):
            state_out[core, :, i * HD : (i + 1) * HD] = state[i]
        return carry

    lax.fori_loop(0, 2, one_core, 0)


def attention_part(distances, order, query, state, pieces):
    n = query.shape[1]
    return call(
        functools.partial(attention_kernel, distances),
        sds((2, n, 3 * HD), f32),
        [SMEM] + [VMEM] * (1 + len(state) + len(pieces)),
        VMEM,
        [pltpu.VMEM((8, n), jnp.int32), pltpu.VMEM((2, n, 1), jnp.int32)],
        280_000_000 * len(distances),
        500_000 * len(distances),
    )(order, query, *state, *pieces)


def merge_kernel(own, par, out, halves, sems):
    mixed, _, total = join(
        [own[:, i * HD : (i + 1) * HD] for i in range(3)], [par[:, i * HD : (i + 1) * HD] for i in range(3)]
    )
    mixed = mixed / total
    copies = Copies(sems)
    started = []
    n = halves.shape[1]
    for side in range(2):
        halves[side] = mixed[side * n : (side + 1) * n].astype(bf16)
        for g in range(8):
            started.append(copies.start(halves.at[side], out.at[(lax.axis_index("xh") ^ side) * 8 + g]))
    for copy in started:
        copy.wait()


def arrange_kernel(own, par, out):
    where = here()
    for z in range(NZ):
        for other in range(2):
            for side in range(2):
                out[weight_rows(where, z, other, side), :] = (own, par)[other][z, side]


def self_out_kernel(share, att, weights, out):
    acc = share[...].astype(f32)
    for g in range(8):
        both = jnp.concatenate([att[g], att[8 + g]], axis=1)
        acc += dot(both, weights[g * 256 : (g + 1) * 256, :])
    out[...] = acc.astype(bf16)


def deal_near(block):
    quarters = block.reshape(4, 64, 128)
    near = lax.axis_index(("zl", "core"))
    got = [lax.dynamic_index_in_dim(quarters, near, 0, keepdims=False)]
    for m in (1, 2, 3):
        piece = lax.dynamic_index_in_dim(quarters, near ^ m, 0, keepdims=False)
        got.append(lax.ppermute(piece, ("zl", "core"), [(i, i ^ m) for i in range(4)]))
    got = jnp.stack(got)
    return jnp.concatenate([lax.dynamic_index_in_dim(got, near ^ q, 0, keepdims=False) for q in range(4)], axis=1)


def deal_far(block):
    pairs = [
        ((share * 4 + i) * 8 + group, (group * 4 + i) * 8 + share)
        for share in range(8)
        for i in range(4)
        for group in range(8)
    ]
    return lax.ppermute(block, ALL, pairs)


def per_device(
    hidden_in,
    norm_gains,
    w_cross_query,
    w_cross_out,
    w_self_qkv,
    w_self_out,
    nbr_kv,
    nbr_count,
    nbr_source,
    span_order,
):
    rows, width = hidden_in.shape
    g = lax.axis_index(GROUP)
    y = lax.axis_index("y")
    vmem = pltpu.VMEM
    sem = pltpu.SemaphoreType.DMA

    first = jnp.stack([w_cross_query, jnp.concatenate([w_cross_out[:128], w_cross_out[128:]], axis=1)])
    first = jnp.concatenate([first, swap_xh(first)], axis=0)
    near = deal_near(w_self_out)
    first, near = lax.optimization_barrier((first, near))
    start = gather_start(first)
    hidden, near, _ = lax.optimization_barrier((hidden_in, near, start[1]))
    normed = call(norm_kernel, sds((rows, width)), [VMEM] * 2, VMEM, [], 10_000_000, 4_000_000)(hidden, norm_gains)
    hidden_share = lax.dynamic_slice_in_dim(hidden, g * 512, 512, 1)
    dealt = deal_far(near)
    start, normed, hidden_share = lax.optimization_barrier((start, normed, hidden_share))
    nbr = after(nbr_kv[0, 0], start)
    nbr_got = [
        shift(lax.dynamic_index_in_dim(nbr, (y + k) % 4, 0, keepdims=False), "y", k, 4) for k in (1, 2, 3)
    ]
    qkv_own = after(w_self_qkv.transpose(1, 0, 2), start)
    qkv_other = swap_xh(qkv_own)
    first_own, nbr_got, qkv_other = lax.optimization_barrier((gather_end(start), nbr_got, qkv_other))
    late_own = lax.all_gather(jnp.concatenate([qkv_own, qkv_other], axis=0), Z, axis=0, tiled=False)
    first_par = [swap_cores(p) for p in first_own]
    first_par, dealt = lax.optimization_barrier((first_par, dealt))
    wso_other = swap_xh(dealt)
    terms = call(
        cross_kernel,
        [sds((rows, 512))] * 8,
        [SMEM] * 2 + [VMEM] + [ANY] * 22,
        [VMEM] * 8,
        [
            vmem((32, 2, 128, 256), bf16),
            vmem((4, 3, 64, 512), bf16),
            vmem((rows, 256), bf16),
            sem((36,)),
        ],
        1_200_000_000,
        10_000_000,
        56,
    )(nbr_source, nbr_count, normed, nbr, *nbr_got, *first_own, *first_par)

    terms, wso_other = lax.optimization_barrier((terms, wso_other))
    wso = jnp.concatenate([dealt[None], wso_other[None]], axis=0)
    got = [shift_group(term, dy, dx) for term, (dy, dx) in zip(terms[1:], PEERS)]
    mid_share = call(sum_kernel, sds((rows, 512)), [VMEM] * 9, VMEM, [], 2_000_000, 4_000_000)(
        hidden_share, terms[0], *got
    )
    late_own, mid_share = lax.optimization_barrier((late_own, mid_share))
    mids = [mid_share] + [shift_group(mid_share, dy, dx) for dy, dx in PEERS]
    late_par = swap_cores(late_own)
    wso_own = lax.all_gather(after(wso, late_own), Z, axis=0, tiled=False)
    keep, send = call(
        qkv_kernel,
        [sds((3, rows, HD))] * 2,
        [VMEM] * 11,
        [VMEM] * 2,
        [vmem((rows, width), bf16), vmem((rows, 256), bf16)],
        1_600_000_000,
        11_000_000,
    )(norm_gains, late_own, late_par, *mids)

    keep, send, wso_own = lax.optimization_barrier((keep, send, wso_own))
    both = jnp.concatenate([keep, swap_xh(send)], axis=1)
    kv = both[1:]
    query = jnp.stack([both[0], swap_cores(both[0])])
    part = functools.partial(attention_part, order=span_order, query=query)
    r1, l1 = shift(kv, Z, 1, NZ), shift(kv, Z, -1, NZ)
    state = part((0,), state=[], pieces=[kv])
    wso_par = swap_cores(wso_own)
    weights = call(arrange_kernel, sds((2048, 512)), [VMEM] * 2, VMEM, [], 1_000_000, 4_000_000)(wso_own, wso_par)
    r2, l2 = shift(r1, Z, 1, NZ), shift(l1, Z, -1, NZ)
    r2, l2, state, weights = lax.optimization_barrier((r2, l2, state, weights))
    r3, l3 = shift(r2, Z, 1, NZ), shift(l2, Z, -1, NZ)
    state = part((1, 7), state=[state], pieces=[l1, r1])
    r3, l3, state = lax.optimization_barrier((r3, l3, state))
    r4, l4 = shift(r3[:1], Z, 1, NZ), shift(l3[1:], Z, -1, NZ)
    state = part((2, 6, 3, 5), state=[state], pieces=[l2, r2, l3, r3])
    r4, l4, state = lax.optimization_barrier((r4, l4, state))
    state = part((4,), state=[state], pieces=[r4, l4])
    heads = call(
        merge_kernel,
        sds((16, rows, HD)),
        [VMEM, VMEM],
        ANY,
        [vmem((2, rows, HD), bf16), sem((16,))],
        1_000_000,
        2_000_000,
    )(state[0], swap_cores(state[1]))
    self_all = lax.all_to_all(heads, ("xh",) + GROUP, 0, 0, tiled=True)
    return call(self_out_kernel, sds((rows, 512)), [VMEM] * 3, VMEM, [], 600_000_000, 4_000_000)(
        mid_share, self_all, weights
    )


def solution(mesh):
    fine = Mesh(mesh.devices.reshape(2, 4, 2, 2, 4, 2), ALL)
    in_specs = (
        P(CTX, None),
        P(),
        P(CTX, GROUP),
        P(GROUP, CTX),
        P(CTX, None, GROUP),
        P(GROUP, CTX),
        P(CTX, "y", None, None, None, "xl"),
        P(CTX),
        P(CTX, None),
        P(),
    )
    return jax.shard_map(
        per_device, mesh=fine, in_specs=in_specs, out_specs=P(CTX, GROUP), check_vma=False
    )
```

```python
import functools
import math

import jax
import jax.numpy as jnp
from jax import lax
from jax.experimental import pallas as pl
from jax.experimental.pallas import tpu as pltpu
from jax.sharding import Mesh
from jax.sharding import PartitionSpec as P

HD = 128
SPAN = 64
epsilon = 1e-05
far_below = -1e30
NZ = 8

VMEM = pl.BlockSpec(memory_space=pltpu.VMEM)
SMEM = pl.BlockSpec(memory_space=pltpu.SMEM)
ANY = pl.BlockSpec(memory_space=pl.ANY)
f32 = jnp.float32
bf16 = jnp.bfloat16

Z = ("zh", "zl")
CTX = ("xh",) + Z + ("core",)
GROUP = ("y", "xl")
ALL = CTX + GROUP


def dot(a, b):
    return jnp.dot(a, b, preferred_element_type=f32)


def dot_t(a, b):
    return lax.dot_general(a, b, (((1,), (1,)), ((), ())), preferred_element_type=f32)


def call(kernel, out_shape, in_specs, out_specs, scratch, flops, nbytes, grant=16):
    return pl.pallas_call(
        kernel,
        out_shape=out_shape,
        in_specs=in_specs,
        out_specs=out_specs,
        scratch_shapes=scratch,
        compiler_params=pltpu.CompilerParams(vmem_limit_bytes=grant * 1024 * 1024),
        cost_estimate=pl.CostEstimate(flops=flops, bytes_accessed=nbytes, transcendentals=0),
    )


def sds(shape, dtype=bf16):
    return jax.ShapeDtypeStruct(shape, dtype)


def after(x, *earlier):
    return lax.optimization_barrier((x,) + earlier)[0]


def shift(x, axis, by, size):
    return lax.ppermute(x, axis, [(i, (i + by) % size) for i in range(size)])


def swap_cores(x):
    return shift(x, "core", 1, 2)


def swap_xh(x):
    return shift(x, "xh", 1, 2)


def gather_start(x):
    return x, shift(x, Z, 1, NZ), shift(x, Z, -1, NZ), shift(x, Z, 2, NZ), shift(x, Z, -2, NZ)


def gather_end(start):
    x, r1, l1, r2, l2 = start
    r3, l3 = shift(r1, Z, 2, NZ), shift(l1, Z, -2, NZ)
    cut = x.shape[0] // 2
    r4, l4 = shift(r2[:cut], Z, 2, NZ), shift(l2[cut:], Z, -2, NZ)
    return [x, l1, l2, l3, r4, l4, r3, r2, r1]


def shift_group(x, dy, dx):
    pairs = [(y * 2 + xl, (y + dy) % 4 * 2 + (xl ^ dx)) for y in range(4) for xl in range(2)]
    return lax.ppermute(x, GROUP, pairs)


PEERS = ((1, 0), (3, 0), (0, 1), (1, 1), (3, 1), (2, 0), (2, 1))


def here():
    return tuple(lax.axis_index(a) for a in ("xh", Z, "core", "y", "xl"))


def peer_group(where, dy, dx):
    return lax.rem(where[3] + dy, 4) * 2 + (where[4] ^ dx)


def block_of(where, zz, other, side):
    return (where[0] ^ side) * 16 + zz * 2 + (where[2] ^ other)


class Copies:
    def __init__(self, sems):
        self.sems = sems
        self.used = 0

    def start(self, source, target):
        copy = pltpu.make_async_copy(source, target, self.sems.at[self.used])
        self.used += 1
        copy.start()
        return copy


def norm_kernel(hidden, gain, out):
    values = hidden[...].astype(f32)
    row_scale = lax.rsqrt(jnp.mean(values * values, axis=1, keepdims=True) + epsilon)
    for b in range(32):
        cols = slice(b * 128, (b + 1) * 128)
        block = hidden[:, cols].astype(f32)
        out[:, cols] = (block * row_scale * gain[:1, cols]).astype(bf16)


def cross_kernel(source, count, normed, nbr0, nbr1, nbr2, nbr3, *rest):
    pieces = (rest[:9], rest[9:18])
    outs, (weights, nbr, mixed_all, sems) = rest[18:26], rest[26:]
    copies = Copies(sems)
    where = here()
    y = where[3]
    started = []
    for distance in range(NZ):
        zz = lax.rem(where[1] + distance, NZ)
        for other in range(2):
            for side in range(2):
                if distance == 4:
                    piece = pieces[other][4 + side]
                else:
                    piece = pieces[other][distance if distance < 4 else distance + 1].at[pl.ds(side * 2, 2)]
                started.append(copies.start(piece, weights.at[block_of(where, zz, other, side)]))
    nbr_copies = [copies.start(nbr0.at[y], nbr.at[y])]
    for k, ref in ((1, nbr1), (2, nbr2), (3, nbr3)):
        nbr_copies.append(copies.start(ref, nbr.at[lax.rem(y + 4 - k, 4)]))
    for copy in started:
        copy.wait()
    acc = jnp.zeros((normed.shape[0], 256), f32)
    for c in range(0, 32, 2):
        right = jnp.concatenate([weights[c, 0], weights[c + 1, 0]], axis=0)
        acc += dot(normed[:, c * 128 : (c + 2) * 128], right)
    for copy in nbr_copies:
        copy.wait()
    query = acc.astype(bf16)
    scale = 1.0 / math.sqrt(HD)
    lanes = lax.broadcasted_iota(jnp.int32, (SPAN, 128), 1)
    chosen = [source[i // 2, i % 2] for i in range(8)]
    for s in range(4):
        slots = []
        for j in range(2):
            i = s * 2 + j
            rank = jnp.int32(0)
            for k in range(s * 2):
                rank = rank + (chosen[k] == chosen[i]).astype(jnp.int32)
            slots.append((chosen[i], rank))
        alive = lanes < count[s] * 64
        for h in range(2):
            kcols = slice(2 * h * HD, (2 * h + 1) * HD)
            vcols = slice((2 * h + 1) * HD, (2 * h + 2) * HD)
            keys = jnp.concatenate([nbr[e, r, :, kcols] for e, r in slots], axis=0)
            vals = jnp.concatenate([nbr[e, r, :, vcols] for e, r in slots], axis=0)
            part = query[s * SPAN : (s + 1) * SPAN, h * HD : (h + 1) * HD]
            scores = jnp.where(alive, dot_t(part, keys) * scale, far_below)
            top = jnp.max(scores, axis=1, keepdims=True)
            exps = jnp.exp(scores - top)
            total = jnp.sum(exps, axis=1, keepdims=True)
            mixed = dot(exps.astype(bf16), vals) / total
            mixed_all[s * SPAN : (s + 1) * SPAN, h * HD : (h + 1) * HD] = mixed.astype(bf16)
    att = mixed_all[...]
    for out, (dy, dx) in zip(outs, ((0, 0),) + PEERS):
        first = peer_group(where, dy, dx) * 4
        for pair in range(2):
            blocks = [weights[first + pair * 2 + i, 1] for i in range(2)]
            upper = jnp.concatenate([block[:, :128] for block in blocks], axis=1)
            lower = jnp.concatenate([block[:, 128:] for block in blocks], axis=1)
            term = dot(att, jnp.concatenate([upper, lower], axis=0))
            out[:, pair * 256 : (pair + 1) * 256] = term.astype(bf16)


def weight_rows(where, zz, other, side):
    return pl.ds(pl.multiple_of(block_of(where, zz, other, side) * 64, 64), 64)


def sum_kernel(share, *rest):
    terms, mid = rest[:8], rest[8]
    acc = terms[0][...].astype(f32)
    for term in terms[1:]:
        acc += term[...].astype(f32)
    mid[...] = (share[...].astype(f32) + acc).astype(bf16)


def qkv_kernel(gain, own, par, *rest):
    mids, (keep, send, normed, proj) = rest[:8], rest[8:]
    where = here()
    xh = where[0]
    rows = mids[0].shape[0]
    squares = jnp.zeros((rows, 512), f32)
    for mid in mids:
        values = mid[...].astype(f32)
        squares += values * values
    row_scale = lax.rsqrt(jnp.sum(squares, axis=1, keepdims=True) * (1.0 / 4096) + epsilon)
    for mid, (dy, dx) in zip(mids, ((0, 0),) + PEERS):
        first = peer_group(where, 4 - dy, dx) * 512
        for j in range(4):
            cols = pl.ds(pl.multiple_of(first + j * 128, 128), 128)
            block = mid[:, j * 128 : (j + 1) * 128].astype(f32)
            normed[:, cols] = (block * row_scale * gain[1:2, cols]).astype(bf16)
    for t in range(3):
        acc = jnp.zeros((rows, 256), f32)
        for z in range(NZ):
            for other in range(2):
                left, right = [], []
                for side in range(2):
                    owner = block_of(where, z, other, side)
                    left.append(normed[:, pl.ds(pl.multiple_of(owner * 128, 128), 128)])
                    right.append((own, par)[other][z, side * 4 + t])
                acc += dot(jnp.concatenate(left, axis=1), jnp.concatenate(right, axis=0))
        if t == 0:
            acc = acc * (math.log2(math.e) / math.sqrt(HD))
        proj[...] = acc.astype(bf16)
        keep[t] = proj[:, pl.ds(pl.multiple_of(xh * 128, 128), 128)]
        send[t] = proj[:, pl.ds(pl.multiple_of((1 - xh) * 128, 128), 128)]


def join(left, right):
    top = jnp.maximum(left[1], right[1])
    fade_left, fade_right = jnp.exp2(left[1] - top), jnp.exp2(right[1] - top)
    return (
        left[0] * fade_left + right[0] * fade_right,
        top,
        left[2] * fade_left + right[2] * fade_right,
    )


def attention_kernel(distances, order, query, *rest):
    first = distances[0] == 0
    where = here()
    if not first:
        state_in, rest = rest[0], rest[1:]
    pieces, (state_out, k_places, q_places) = rest[:-3], rest[-3:]
    n = query.shape[1]
    rows = lax.broadcasted_iota(jnp.int32, (SPAN, 1), 0)
    lanes = lax.broadcasted_iota(jnp.int32, (1, 256), 1)
    right = lax.broadcasted_iota(jnp.int32, (n, HD), 1)
    span_of, within = lanes // SPAN, lanes % SPAN
    for i, distance in enumerate(distances):
        for side in range(2):
            c = block_of(where, lax.rem(where[1] + distance, NZ), 0, side)
            place = jnp.zeros((1, 256), jnp.int32)
            for s in range(4):
                place = jnp.where(span_of == s, order[c * 4 + s], place)
            k_places[i : i + 1, side * 256 : (side + 1) * 256] = place * SPAN + within
    for core in range(2):
        for side in range(2):
            c = block_of(where, where[1], core, side)
            for s in range(4):
                begin = (side * 4 + s) * SPAN
                q_places[core, begin : begin + SPAN, :] = order[c * 4 + s] * SPAN + rows

    def one_core(core, carry):
        top = jnp.full((n, 1), far_below, f32)
        total = jnp.zeros((n, 1), f32)
        mixed = jnp.zeros((n, HD), f32)
        places = q_places[core]
        rows_here = query[core]
        for i in range(len(distances)):
            if distances[i] == 4:
                keys, vals = pieces[i][0], pieces[i + 1][0]
            else:
                keys, vals = pieces[i][0], pieces[i][1]
            scores = dot_t(rows_here, keys)
            scores = jnp.where(k_places[i : i + 1, :] <= places, scores, far_below)
            new_top = jnp.maximum(top, jnp.max(scores, axis=1, keepdims=True))
            exps = jnp.exp2(scores - new_top)
            fade = jnp.exp2(top - new_top)
            total = total * fade + jnp.sum(exps, axis=1, keepdims=True)
            mixed = mixed * fade + dot(exps.astype(bf16), vals)
            top = new_top
        state = (mixed, jnp.broadcast_to(top, (n, HD)), jnp.broadcast_to(total, (n, HD)))
        if not first:
            state = join(state, [state_in[core, :, i * HD : (i + 1) * HD] for i in range(3)])
        for i in range(3):
            state_out[core, :, i * HD : (i + 1) * HD] = state[i]
        return carry

    lax.fori_loop(0, 2, one_core, 0)


def attention_part(distances, order, query, state, pieces):
    n = query.shape[1]
    return call(
        functools.partial(attention_kernel, distances),
        sds((2, n, 3 * HD), f32),
        [SMEM] + [VMEM] * (1 + len(state) + len(pieces)),
        VMEM,
        [pltpu.VMEM((8, n), jnp.int32), pltpu.VMEM((2, n, 1), jnp.int32)],
        280_000_000 * len(distances),
        500_000 * len(distances),
    )(order, query, *state, *pieces)


def merge_kernel(own, par, out, halves, sems):
    mixed, _, total = join(
        [own[:, i * HD : (i + 1) * HD] for i in range(3)], [par[:, i * HD : (i + 1) * HD] for i in range(3)]
    )
    mixed = mixed / total
    copies = Copies(sems)
    started = []
    n = halves.shape[1]
    for side in range(2):
        halves[side] = mixed[side * n : (side + 1) * n].astype(bf16)
        for g in range(8):
            started.append(copies.start(halves.at[side], out.at[(lax.axis_index("xh") ^ side) * 8 + g]))
    for copy in started:
        copy.wait()


def arrange_kernel(own, par, out, sems):
    where = here()
    copies = Copies(sems)
    started = []
    for z in range(NZ):
        for other in range(2):
            for side in range(2):
                rows = weight_rows(where, z, other, side)
                for part in range(2):
                    source = (own, par)[other].at[z, side * 4 + 3, pl.ds(part * 64, 64)]
                    started.append(copies.start(source, out.at[rows, pl.ds(part * 256, 256)]))
    for copy in started:
        copy.wait()


def self_out_kernel(share, att, weights, out):
    acc = share[...].astype(f32)
    for g in range(8):
        both = jnp.concatenate([att[g], att[8 + g]], axis=1)
        acc += dot(both, weights[g * 256 : (g + 1) * 256, :])
    out[...] = acc.astype(bf16)


def deal_near(block):
    quarters = block.reshape(4, 64, 128)
    near = lax.axis_index(("zl", "core"))
    got = [lax.dynamic_index_in_dim(quarters, near, 0, keepdims=False)]
    for m in (1, 2, 3):
        piece = lax.dynamic_index_in_dim(quarters, near ^ m, 0, keepdims=False)
        got.append(lax.ppermute(piece, ("zl", "core"), [(i, i ^ m) for i in range(4)]))
    got = jnp.stack(got)
    return jnp.concatenate([lax.dynamic_index_in_dim(got, near ^ q, 0, keepdims=False) for q in range(4)], axis=1)


def deal_far(block):
    pairs = [
        ((share * 4 + i) * 8 + group, (group * 4 + i) * 8 + share)
        for share in range(8)
        for i in range(4)
        for group in range(8)
    ]
    return lax.ppermute(block, ALL, pairs)


def per_device(
    hidden_in,
    norm_gains,
    w_cross_query,
    w_cross_out,
    w_self_qkv,
    w_self_out,
    nbr_kv,
    nbr_count,
    nbr_source,
    span_order,
):
    rows, width = hidden_in.shape
    g = lax.axis_index(GROUP)
    y = lax.axis_index("y")
    vmem = pltpu.VMEM
    sem = pltpu.SemaphoreType.DMA

    first = jnp.stack([w_cross_query, jnp.concatenate([w_cross_out[:128], w_cross_out[128:]], axis=1)])
    first = jnp.concatenate([first, swap_xh(first)], axis=0)
    near = deal_near(w_self_out)
    first, near = lax.optimization_barrier((first, near))
    start = gather_start(first)
    hidden, near, _ = lax.optimization_barrier((hidden_in, near, start[1]))
    normed = call(norm_kernel, sds((rows, width)), [VMEM] * 2, VMEM, [], 10_000_000, 4_000_000)(hidden, norm_gains)
    hidden_share = lax.dynamic_slice_in_dim(hidden, g * 512, 512, 1)
    dealt = deal_far(near)
    start, normed, hidden_share, dealt = lax.optimization_barrier((start, normed, hidden_share, dealt))
    nbr = after(nbr_kv[0, 0], start)
    nbr_got = [
        shift(lax.dynamic_index_in_dim(nbr, (y + k) % 4, 0, keepdims=False), "y", k, 4) for k in (1, 2, 3)
    ]
    late = jnp.concatenate(
        [w_self_qkv.transpose(1, 0, 2), jnp.concatenate([dealt[:, :256], dealt[:, 256:]], axis=0)[None]], axis=0
    )
    late = after(late, start)
    late_other = swap_xh(late)
    first_own, nbr_got, late_other = lax.optimization_barrier((gather_end(start), nbr_got, late_other))
    late_own = lax.all_gather(jnp.concatenate([late, late_other], axis=0), Z, axis=0, tiled=False)
    first_par = [swap_cores(p) for p in first_own]
    terms = call(
        cross_kernel,
        [sds((rows, 512))] * 8,
        [SMEM] * 2 + [VMEM] + [ANY] * 22,
        [VMEM] * 8,
        [
            vmem((32, 2, 128, 256), bf16),
            vmem((4, 3, 64, 512), bf16),
            vmem((rows, 256), bf16),
            sem((36,)),
        ],
        1_200_000_000,
        10_000_000,
        56,
    )(nbr_source, nbr_count, normed, nbr, *nbr_got, *first_own, *first_par)

    got = [shift_group(term, dy, dx) for term, (dy, dx) in zip(terms[1:], PEERS)]
    mid_share = call(sum_kernel, sds((rows, 512)), [VMEM] * 9, VMEM, [], 2_000_000, 4_000_000)(
        hidden_share, terms[0], *got
    )
    late_own, mid_share = lax.optimization_barrier((late_own, mid_share))
    mids = [mid_share] + [shift_group(mid_share, dy, dx) for dy, dx in PEERS]
    late_par = swap_cores(late_own)
    keep, send = call(
        qkv_kernel,
        [sds((3, rows, HD))] * 2,
        [VMEM] * 11,
        [VMEM] * 2,
        [vmem((rows, width), bf16), vmem((rows, 256), bf16)],
        1_600_000_000,
        11_000_000,
    )(norm_gains, late_own, late_par, *mids)

    both = jnp.concatenate([keep, swap_xh(send)], axis=1)
    kv = both[1:]
    query = jnp.stack([both[0], swap_cores(both[0])])
    part = functools.partial(attention_part, order=span_order, query=query)
    r1, l1 = shift(kv, Z, 1, NZ), shift(kv, Z, -1, NZ)
    state = part((0,), state=[], pieces=[kv])
    late_own, late_par, _ = lax.optimization_barrier((late_own, late_par, r1))
    weights = call(arrange_kernel, sds((2048, 512)), [ANY] * 2, VMEM, [sem((64,))], 1_000_000, 4_000_000)(
        late_own, late_par
    )
    r2, l2 = shift(r1, Z, 1, NZ), shift(l1, Z, -1, NZ)
    r2, l2, state, weights = lax.optimization_barrier((r2, l2, state, weights))
    r3, l3 = shift(r2, Z, 1, NZ), shift(l2, Z, -1, NZ)
    state = part((1, 7), state=[state], pieces=[l1, r1])
    r3, l3, state = lax.optimization_barrier((r3, l3, state))
    r4, l4 = shift(r3[:1], Z, 1, NZ), shift(l3[1:], Z, -1, NZ)
    state = part((2, 6, 3, 5), state=[state], pieces=[l2, r2, l3, r3])
    r4, l4, state = lax.optimization_barrier((r4, l4, state))
    state = part((4,), state=[state], pieces=[r4, l4])
    heads = call(
        merge_kernel,
        sds((16, rows, HD)),
        [VMEM, VMEM],
        ANY,
        [vmem((2, rows, HD), bf16), sem((16,))],
        1_000_000,
        2_000_000,
    )(state[0], swap_cores(state[1]))
    self_all = lax.all_to_all(heads, ("xh",) + GROUP, 0, 0, tiled=True)
    return call(self_out_kernel, sds((rows, 512)), [VMEM] * 3, VMEM, [], 600_000_000, 4_000_000)(
        mid_share, self_all, weights
    )


def solution(mesh):
    fine = Mesh(mesh.devices.reshape(2, 4, 2, 2, 4, 2), ALL)
    in_specs = (
        P(CTX, None),
        P(),
        P(CTX, GROUP),
        P(GROUP, CTX),
        P(CTX, None, GROUP),
        P(GROUP, CTX),
        P(CTX, "y", None, None, None, "xl"),
        P(CTX),
        P(CTX, None),
        P(),
    )
    return jax.shard_map(
        per_device, mesh=fine, in_specs=in_specs, out_specs=P(CTX, GROUP), check_vma=False
    )
```

```python
import functools
import math

import jax
import jax.numpy as jnp
from jax import lax
from jax.experimental import pallas as pl
from jax.experimental.pallas import tpu as pltpu
from jax.sharding import Mesh
from jax.sharding import PartitionSpec as P

HD = 128
SPAN = 64
epsilon = 1e-05
far_below = -1e30
NZ = 8

VMEM = pl.BlockSpec(memory_space=pltpu.VMEM)
SMEM = pl.BlockSpec(memory_space=pltpu.SMEM)
ANY = pl.BlockSpec(memory_space=pl.ANY)
f32 = jnp.float32
bf16 = jnp.bfloat16

Z = ("zh", "zl")
CTX = ("xh",) + Z + ("core",)
GROUP = ("y", "xl")
ALL = CTX + GROUP


def dot(a, b):
    return jnp.dot(a, b, preferred_element_type=f32)


def dot_t(a, b):
    return lax.dot_general(a, b, (((1,), (1,)), ((), ())), preferred_element_type=f32)


def call(kernel, out_shape, in_specs, out_specs, scratch, flops, nbytes, grant=16):
    return pl.pallas_call(
        kernel,
        out_shape=out_shape,
        in_specs=in_specs,
        out_specs=out_specs,
        scratch_shapes=scratch,
        compiler_params=pltpu.CompilerParams(vmem_limit_bytes=grant * 1024 * 1024),
        cost_estimate=pl.CostEstimate(flops=flops, bytes_accessed=nbytes, transcendentals=0),
    )


def sds(shape, dtype=bf16):
    return jax.ShapeDtypeStruct(shape, dtype)


def after(x, *earlier):
    return lax.optimization_barrier((x,) + earlier)[0]


def shift(x, axis, by, size):
    return lax.ppermute(x, axis, [(i, (i + by) % size) for i in range(size)])


def swap_cores(x):
    return shift(x, "core", 1, 2)


def swap_xh(x):
    return shift(x, "xh", 1, 2)


def gather_start(x):
    return x, shift(x, Z, 1, NZ), shift(x, Z, -1, NZ), shift(x, Z, 2, NZ), shift(x, Z, -2, NZ)


def gather_end(start):
    x, r1, l1, r2, l2 = start
    r3, l3 = shift(r1, Z, 2, NZ), shift(l1, Z, -2, NZ)
    cut = x.shape[0] // 2
    r4, l4 = shift(r2[:cut], Z, 2, NZ), shift(l2[cut:], Z, -2, NZ)
    return [x, l1, l2, l3, r4, l4, r3, r2, r1]


def shift_group(x, dy, dx):
    pairs = [(y * 2 + xl, (y + dy) % 4 * 2 + (xl ^ dx)) for y in range(4) for xl in range(2)]
    return lax.ppermute(x, GROUP, pairs)


PEERS = ((1, 0), (3, 0), (0, 1), (1, 1), (3, 1), (2, 0), (2, 1))


def here():
    return tuple(lax.axis_index(a) for a in ("xh", Z, "core", "y", "xl"))


def peer_group(where, dy, dx):
    return lax.rem(where[3] + dy, 4) * 2 + (where[4] ^ dx)


def block_of(where, zz, other, side):
    return (where[0] ^ side) * 16 + zz * 2 + (where[2] ^ other)


class Copies:
    def __init__(self, sems):
        self.sems = sems
        self.used = 0

    def start(self, source, target):
        copy = pltpu.make_async_copy(source, target, self.sems.at[self.used])
        self.used += 1
        copy.start()
        return copy


def norm_kernel(hidden, gain, out):
    values = hidden[...].astype(f32)
    row_scale = lax.rsqrt(jnp.mean(values * values, axis=1, keepdims=True) + epsilon)
    for b in range(32):
        cols = slice(b * 128, (b + 1) * 128)
        block = hidden[:, cols].astype(f32)
        out[:, cols] = (block * row_scale * gain[:1, cols]).astype(bf16)


def cross_kernel(source, count, normed, nbr0, nbr1, nbr2, nbr3, *rest):
    pieces = (rest[:9], rest[9:18])
    outs, (weights, nbr, mixed_all, sems) = rest[18:26], rest[26:]
    copies = Copies(sems)
    where = here()
    y = where[3]
    started = []
    for distance in range(NZ):
        zz = lax.rem(where[1] + distance, NZ)
        for other in range(2):
            for side in range(2):
                if distance == 4:
                    piece = pieces[other][4 + side]
                else:
                    piece = pieces[other][distance if distance < 4 else distance + 1].at[pl.ds(side * 2, 2)]
                started.append(copies.start(piece, weights.at[block_of(where, zz, other, side)]))
    nbr_copies = [copies.start(nbr0.at[y], nbr.at[y])]
    for k, ref in ((1, nbr1), (2, nbr2), (3, nbr3)):
        nbr_copies.append(copies.start(ref, nbr.at[lax.rem(y + 4 - k, 4)]))
    for copy in started:
        copy.wait()
    acc = jnp.zeros((normed.shape[0], 256), f32)
    for c in range(0, 32, 2):
        right = jnp.concatenate([weights[c, 0], weights[c + 1, 0]], axis=0)
        acc += dot(normed[:, c * 128 : (c + 2) * 128], right)
    for copy in nbr_copies:
        copy.wait()
    query = acc.astype(bf16)
    scale = 1.0 / math.sqrt(HD)
    lanes = lax.broadcasted_iota(jnp.int32, (SPAN, 128), 1)
    chosen = [source[i // 2, i % 2] for i in range(8)]
    for s in range(4):
        slots = []
        for j in range(2):
            i = s * 2 + j
            rank = jnp.int32(0)
            for k in range(s * 2):
                rank = rank + (chosen[k] == chosen[i]).astype(jnp.int32)
            slots.append((chosen[i], rank))
        alive = lanes < count[s] * 64
        for h in range(2):
            kcols = slice(2 * h * HD, (2 * h + 1) * HD)
            vcols = slice((2 * h + 1) * HD, (2 * h + 2) * HD)
            keys = jnp.concatenate([nbr[e, r, :, kcols] for e, r in slots], axis=0)
            vals = jnp.concatenate([nbr[e, r, :, vcols] for e, r in slots], axis=0)
            part = query[s * SPAN : (s + 1) * SPAN, h * HD : (h + 1) * HD]
            scores = jnp.where(alive, dot_t(part, keys) * scale, far_below)
            top = jnp.max(scores, axis=1, keepdims=True)
            exps = jnp.exp(scores - top)
            total = jnp.sum(exps, axis=1, keepdims=True)
            mixed = dot(exps.astype(bf16), vals) / total
            mixed_all[s * SPAN : (s + 1) * SPAN, h * HD : (h + 1) * HD] = mixed.astype(bf16)
    att = mixed_all[...]
    for out, (dy, dx) in zip(outs, ((0, 0),) + PEERS):
        first = peer_group(where, dy, dx) * 4
        for pair in range(2):
            blocks = [weights[first + pair * 2 + i, 1] for i in range(2)]
            upper = jnp.concatenate([block[:, :128] for block in blocks], axis=1)
            lower = jnp.concatenate([block[:, 128:] for block in blocks], axis=1)
            term = dot(att, jnp.concatenate([upper, lower], axis=0))
            out[:, pair * 256 : (pair + 1) * 256] = term.astype(bf16)


def weight_rows(where, zz, other, side):
    return pl.ds(pl.multiple_of(block_of(where, zz, other, side) * 64, 64), 64)


def sum_kernel(share, *rest):
    terms, mid = rest[:8], rest[8]
    acc = terms[0][...].astype(f32)
    for term in terms[1:]:
        acc += term[...].astype(f32)
    mid[...] = (share[...].astype(f32) + acc).astype(bf16)


def qkv_kernel(gain, own, par, *rest):
    mids, (keep, send, normed, proj) = rest[:8], rest[8:]
    where = here()
    xh = where[0]
    rows = mids[0].shape[0]
    squares = jnp.zeros((rows, 512), f32)
    for mid in mids:
        values = mid[...].astype(f32)
        squares += values * values
    row_scale = lax.rsqrt(jnp.sum(squares, axis=1, keepdims=True) * (1.0 / 4096) + epsilon)
    for mid, (dy, dx) in zip(mids, ((0, 0),) + PEERS):
        first = peer_group(where, 4 - dy, dx) * 512
        for j in range(4):
            cols = pl.ds(pl.multiple_of(first + j * 128, 128), 128)
            block = mid[:, j * 128 : (j + 1) * 128].astype(f32)
            normed[:, cols] = (block * row_scale * gain[1:2, cols]).astype(bf16)
    for t in range(3):
        acc = jnp.zeros((rows, 256), f32)
        for z in range(NZ):
            for other in range(2):
                left, right = [], []
                for side in range(2):
                    owner = block_of(where, z, other, side)
                    left.append(normed[:, pl.ds(pl.multiple_of(owner * 128, 128), 128)])
                    right.append((own, par)[other][z, side * 4 + t])
                acc += dot(jnp.concatenate(left, axis=1), jnp.concatenate(right, axis=0))
        if t == 0:
            acc = acc * (math.log2(math.e) / math.sqrt(HD))
        proj[...] = acc.astype(bf16)
        keep[t] = proj[:, pl.ds(pl.multiple_of(xh * 128, 128), 128)]
        send[t] = proj[:, pl.ds(pl.multiple_of((1 - xh) * 128, 128), 128)]


def join(left, right):
    top = jnp.maximum(left[1], right[1])
    fade_left, fade_right = jnp.exp2(left[1] - top), jnp.exp2(right[1] - top)
    return (
        left[0] * fade_left + right[0] * fade_right,
        top,
        left[2] * fade_left + right[2] * fade_right,
    )


def attention_kernel(distances, order, query, *rest):
    first = distances[0] == 0
    where = here()
    if not first:
        state_in, rest = rest[0], rest[1:]
    pieces, (state_out, k_places, q_places) = rest[:-3], rest[-3:]
    n = query.shape[1]
    rows = lax.broadcasted_iota(jnp.int32, (SPAN, 1), 0)
    lanes = lax.broadcasted_iota(jnp.int32, (1, 256), 1)
    right = lax.broadcasted_iota(jnp.int32, (n, HD), 1)
    span_of, within = lanes // SPAN, lanes % SPAN
    for i, distance in enumerate(distances):
        for side in range(2):
            c = block_of(where, lax.rem(where[1] + distance, NZ), 0, side)
            place = jnp.zeros((1, 256), jnp.int32)
            for s in range(4):
                place = jnp.where(span_of == s, order[c * 4 + s], place)
            k_places[i : i + 1, side * 256 : (side + 1) * 256] = place * SPAN + within
    for core in range(2):
        for side in range(2):
            c = block_of(where, where[1], core, side)
            for s in range(4):
                begin = (side * 4 + s) * SPAN
                q_places[core, begin : begin + SPAN, :] = order[c * 4 + s] * SPAN + rows

    def one_core(core, carry):
        top = jnp.full((n, 1), far_below, f32)
        total = jnp.zeros((n, 1), f32)
        mixed = jnp.zeros((n, HD), f32)
        places = q_places[core]
        rows_here = query[core]
        for i in range(len(distances)):
            if distances[i] == 4:
                keys, vals = pieces[i][0], pieces[i + 1][0]
            else:
                keys, vals = pieces[i][0], pieces[i][1]
            scores = dot_t(rows_here, keys)
            scores = jnp.where(k_places[i : i + 1, :] <= places, scores, far_below)
            new_top = jnp.maximum(top, jnp.max(scores, axis=1, keepdims=True))
            exps = jnp.exp2(scores - new_top)
            fade = jnp.exp2(top - new_top)
            total = total * fade + jnp.sum(exps, axis=1, keepdims=True)
            mixed = mixed * fade + dot(exps.astype(bf16), vals)
            top = new_top
        state = (mixed, jnp.broadcast_to(top, (n, HD)), jnp.broadcast_to(total, (n, HD)))
        if not first:
            state = join(state, [state_in[core, :, i * HD : (i + 1) * HD] for i in range(3)])
        for i in range(3):
            state_out[core, :, i * HD : (i + 1) * HD] = state[i]
        return carry

    lax.fori_loop(0, 2, one_core, 0)


def attention_part(distances, order, query, state, pieces):
    n = query.shape[1]
    return call(
        functools.partial(attention_kernel, distances),
        sds((2, n, 3 * HD), f32),
        [SMEM] + [VMEM] * (1 + len(state) + len(pieces)),
        VMEM,
        [pltpu.VMEM((8, n), jnp.int32), pltpu.VMEM((2, n, 1), jnp.int32)],
        280_000_000 * len(distances),
        500_000 * len(distances),
    )(order, query, *state, *pieces)


def merge_kernel(own, par, out, halves, sems):
    mixed, _, total = join(
        [own[:, i * HD : (i + 1) * HD] for i in range(3)], [par[:, i * HD : (i + 1) * HD] for i in range(3)]
    )
    mixed = mixed / total
    copies = Copies(sems)
    started = []
    n = halves.shape[1]
    for side in range(2):
        halves[side] = mixed[side * n : (side + 1) * n].astype(bf16)
        for g in range(8):
            started.append(copies.start(halves.at[side], out.at[(lax.axis_index("xh") ^ side) * 8 + g]))
    for copy in started:
        copy.wait()


def arrange_kernel(own, par, out, sems):
    where = here()
    copies = Copies(sems)
    started = []
    for z in range(NZ):
        for other in range(2):
            for side in range(2):
                rows = weight_rows(where, z, other, side)
                for part in range(2):
                    source = (own, par)[other].at[z, side * 4 + 3, pl.ds(part * 64, 64)]
                    started.append(copies.start(source, out.at[rows, pl.ds(part * 256, 256)]))
    for copy in started:
        copy.wait()


def self_out_kernel(share, att, weights, out):
    acc = share[...].astype(f32)
    for g in range(8):
        both = jnp.concatenate([att[g], att[8 + g]], axis=1)
        acc += dot(both, weights[g * 256 : (g + 1) * 256, :])
    out[...] = acc.astype(bf16)


def deal_near(block):
    quarters = block.reshape(4, 64, 128)
    near = lax.axis_index(("zl", "core"))
    got = [lax.dynamic_index_in_dim(quarters, near, 0, keepdims=False)]
    for m in (1, 2, 3):
        piece = lax.dynamic_index_in_dim(quarters, near ^ m, 0, keepdims=False)
        got.append(lax.ppermute(piece, ("zl", "core"), [(i, i ^ m) for i in range(4)]))
    got = jnp.stack(got)
    return jnp.concatenate([lax.dynamic_index_in_dim(got, near ^ q, 0, keepdims=False) for q in range(4)], axis=1)


def deal_far(block):
    pairs = [
        ((share * 4 + i) * 8 + group, (group * 4 + i) * 8 + share)
        for share in range(8)
        for i in range(4)
        for group in range(8)
    ]
    return lax.ppermute(block, ALL, pairs)


def per_device(
    hidden_in,
    norm_gains,
    w_cross_query,
    w_cross_out,
    w_self_qkv,
    w_self_out,
    nbr_kv,
    nbr_count,
    nbr_source,
    span_order,
):
    rows, width = hidden_in.shape
    g = lax.axis_index(GROUP)
    y = lax.axis_index("y")
    vmem = pltpu.VMEM
    sem = pltpu.SemaphoreType.DMA

    first = jnp.stack([w_cross_query, jnp.concatenate([w_cross_out[:128], w_cross_out[128:]], axis=1)])
    first = jnp.concatenate([first, swap_xh(first)], axis=0)
    near = deal_near(w_self_out)
    first, near = lax.optimization_barrier((first, near))
    start = gather_start(first)
    hidden, near, _ = lax.optimization_barrier((hidden_in, near, start[1]))
    normed = call(norm_kernel, sds((rows, width)), [VMEM] * 2, VMEM, [], 10_000_000, 4_000_000)(hidden, norm_gains)
    hidden_share = lax.dynamic_slice_in_dim(hidden, g * 512, 512, 1)
    dealt = deal_far(near)
    start, normed, hidden_share, dealt = lax.optimization_barrier((start, normed, hidden_share, dealt))
    nbr = after(nbr_kv[0, 0], start)
    nbr_got = [
        shift(lax.dynamic_index_in_dim(nbr, (y + k) % 4, 0, keepdims=False), "y", k, 4) for k in (1, 2, 3)
    ]
    late = jnp.concatenate(
        [w_self_qkv.transpose(1, 0, 2), jnp.concatenate([dealt[:, :256], dealt[:, 256:]], axis=0)[None]], axis=0
    )
    late = after(late, start)
    late_other = swap_xh(late)
    first_own, nbr_got, late_other = lax.optimization_barrier((gather_end(start), nbr_got, late_other))
    late_own = lax.all_gather(jnp.concatenate([late, late_other], axis=0), Z, axis=0, tiled=False)
    first_par = [swap_cores(p) for p in first_own]
    terms = call(
        cross_kernel,
        [sds((rows, 512))] * 8,
        [SMEM] * 2 + [VMEM] + [ANY] * 22,
        [VMEM] * 8,
        [
            vmem((32, 2, 128, 256), bf16),
            vmem((4, 3, 64, 512), bf16),
            vmem((rows, 256), bf16),
            sem((36,)),
        ],
        1_200_000_000,
        10_000_000,
        56,
    )(nbr_source, nbr_count, normed, nbr, *nbr_got, *first_own, *first_par)

    got = [shift_group(term, dy, dx) for term, (dy, dx) in zip(terms[1:], PEERS)]
    mid_share = call(sum_kernel, sds((rows, 512)), [VMEM] * 9, VMEM, [], 2_000_000, 4_000_000)(
        hidden_share, terms[0], *got
    )
    mids = [mid_share] + [shift_group(mid_share, dy, dx) for dy, dx in PEERS]
    late_own, *_ = lax.optimization_barrier((late_own, mids[1], mids[2], mids[3]))
    late_par = swap_cores(late_own)
    keep, send = call(
        qkv_kernel,
        [sds((3, rows, HD))] * 2,
        [VMEM] * 11,
        [VMEM] * 2,
        [vmem((rows, width), bf16), vmem((rows, 256), bf16)],
        1_600_000_000,
        11_000_000,
    )(norm_gains, late_own, late_par, *mids)

    both = jnp.concatenate([keep, swap_xh(send)], axis=1)
    kv = both[1:]
    query = jnp.stack([both[0], swap_cores(both[0])])
    part = functools.partial(attention_part, order=span_order, query=query)
    r1, l1 = shift(kv, Z, 1, NZ), shift(kv, Z, -1, NZ)
    state = part((0,), state=[], pieces=[kv])
    late_own, late_par, _ = lax.optimization_barrier((late_own, late_par, r1))
    weights = call(arrange_kernel, sds((2048, 512)), [ANY] * 2, VMEM, [sem((64,))], 1_000_000, 4_000_000)(
        late_own, late_par
    )
    r2, l2 = shift(r1, Z, 1, NZ), shift(l1, Z, -1, NZ)
    r2, l2, state, weights = lax.optimization_barrier((r2, l2, state, weights))
    r3, l3 = shift(r2, Z, 1, NZ), shift(l2, Z, -1, NZ)
    state = part((1, 7), state=[state], pieces=[l1, r1])
    r3, l3, state = lax.optimization_barrier((r3, l3, state))
    r4, l4 = shift(r3[:1], Z, 1, NZ), shift(l3[1:], Z, -1, NZ)
    state = part((2, 6, 3, 5), state=[state], pieces=[l2, r2, l3, r3])
    r4, l4, state = lax.optimization_barrier((r4, l4, state))
    state = part((4,), state=[state], pieces=[r4, l4])
    heads = call(
        merge_kernel,
        sds((16, rows, HD)),
        [VMEM, VMEM],
        ANY,
        [vmem((2, rows, HD), bf16), sem((16,))],
        1_000_000,
        2_000_000,
    )(state[0], swap_cores(state[1]))
    self_all = lax.all_to_all(heads, ("xh",) + GROUP, 0, 0, tiled=True)
    return call(self_out_kernel, sds((rows, 512)), [VMEM] * 3, VMEM, [], 600_000_000, 4_000_000)(
        mid_share, self_all, weights
    )


def solution(mesh):
    fine = Mesh(mesh.devices.reshape(2, 4, 2, 2, 4, 2), ALL)
    in_specs = (
        P(CTX, None),
        P(),
        P(CTX, GROUP),
        P(GROUP, CTX),
        P(CTX, None, GROUP),
        P(GROUP, CTX),
        P(CTX, "y", None, None, None, "xl"),
        P(CTX),
        P(CTX, None),
        P(),
    )
    return jax.shard_map(
        per_device, mesh=fine, in_specs=in_specs, out_specs=P(CTX, GROUP), check_vma=False
    )
```
